32 devices in a mesh: expert: 16 (over z, y, x), dp: 2 (over core).
Axes of the slice: x: 2, y: 2, z: 4, core: 2. Of those that a mesh axis runs over, the one named last changes fastest.
Arguments:
- layer_input: bfloat16 [4096, 3584], P(('expert', 'dp')), may hold values from -6 to 6
- out_grad: bfloat16 [4096, 3584], P(('expert', 'dp')), may hold values from -6 to 6
- routes: int32 [4096, 8], P(('expert', 'dp')), may hold values from 0 to 255, as said below
- gate_values: float32 [4096, 8], P(('expert', 'dp')), may hold values from 0.1 to 1
- keep_mask: int32 [4096, 8], P(('expert', 'dp')), may hold values 0 or 1
- gate_weight: bfloat16 [3584, 6144], P('dp', 'expert'), may hold values from -0.09375 to 0.09375
- up_weight: bfloat16 [3584, 6144], P('dp', 'expert'), may hold values from -0.09375 to 0.09375
- down_transposed: bfloat16 [3584, 6144], P('dp', 'expert'), may hold values from -0.15625 to 0.15625
Outputs:
- input_grad: bfloat16 [4096, 3584], P(('expert', 'dp'))
- gate_grad: bfloat16 [3584, 6144], P('dp', 'expert')
- up_grad: bfloat16 [3584, 6144], P('dp', 'expert')
- down_grad: bfloat16 [3584, 6144], P('dp', 'expert')
The draws below stay inside these ranges and needn't reach their ends.
Inputs may be any that keep to these rules, and one draw needn't show every extreme that they name: `routes`: each token names 8 different experts. Among one device's 128 tokens no expert is named more than 5 times; on every device some expert below 4 is named exactly 5 times, and one expert below 4 is named 5 times on every device.
All inputs are finite; a program needn't handle non-finite values. No bound on the sum of `keep_mask` on one device may be relied on, other than what follows from the above.
Results may differ from the reference program's by a relative error of at most 0.0065.
Values may be sent and summed in bfloat16 or wider, within the bound.
No kernel may reach another device: no remote copies, remote signals or barrier semaphores. Data moves between devices by JAX's collectives and lax.ppermute only.
A program may use at most 128 MiB of HBM per device.

```python
import jax
import jax.numpy as jnp
from jax import lax

D = 3584
HID = 1536
EXPERTS = 256
TOP = 8
SPLIT = 4
TOK = 128
MOST = 5
LIVE = 4
F_DEV = 384
TOKENS = 4096
N_EXPERT = 16
N_DP = 2


def route_block(block_key, hot_limit, full_expert):
    count_key, own_key, row_key, column_key = jax.random.split(block_key, 4)
    live_iota = jnp.arange(LIVE, dtype=jnp.int32)
    counts = jnp.minimum(jax.random.randint(count_key, (LIVE,), 0, hot_limit + 1, dtype=jnp.int32), MOST)
    own_full = jax.random.randint(own_key, (), 0, LIVE, dtype=jnp.int32)
    counts = jnp.where((live_iota == own_full) | (live_iota == full_expert), MOST, counts).astype(jnp.int32)
    live_ends = jnp.cumsum(counts).astype(jnp.int32)
    live_total = live_ends[LIVE - 1]
    positions = jnp.arange(TOK * TOP, dtype=jnp.int32)
    live_ids = jnp.sum((positions[:, None] >= live_ends[None, :]).astype(jnp.int32), axis=1)
    dead_ids = LIVE + (positions - live_total) * (EXPERTS - LIVE) // (TOK * TOP - live_total)
    sorted_ids = jnp.where(positions < live_total, live_ids, dead_ids).astype(jnp.int32)
    route_table = sorted_ids.reshape(TOP, TOK).T
    route_table = route_table[jax.random.permutation(row_key, TOK)]
    scores = jax.random.randint(column_key, (TOK, TOP), 0, 1 << 20, dtype=jnp.int32) * TOP + jnp.arange(TOP, dtype=jnp.int32)[None, :]
    column_order = jnp.argsort(scores, axis=1)
    return jnp.take_along_axis(route_table, column_order, axis=1).astype(jnp.int32)


def draw_routes(key, part):
    hot_limit = jax.random.randint(jax.random.fold_in(key, 11), (LIVE,), 1, 2 * MOST + 1, dtype=jnp.int32)
    full_expert = jax.random.randint(jax.random.fold_in(key, 12), (), 0, LIVE, dtype=jnp.int32)
    block_keys = jax.random.split(jax.random.fold_in(key, 13), TOKENS // TOK)
    tables = jax.vmap(lambda block_key: route_block(block_key, hot_limit, full_expert))(block_keys)
    return tables.reshape(TOKENS, TOP)


def place_ends(result, stream_key, least, largest):
    extent = result.shape
    place = [jax.random.randint(jax.random.fold_in(stream_key, axis), (), 0, extent[axis]) for axis in range(len(extent))]
    result = result.at[tuple(place)].set(least)
    longest = extent.index(max(extent))
    place[longest] = (place[longest] + 1) % extent[longest]
    return result.at[tuple(place)].set(largest)


def block_scale(key, shape, shards, low, top_value):
    loudness = 1.0
    for position, shards_of in shards:
        draws = jax.random.uniform(jax.random.fold_in(jax.random.fold_in(key, 6), position), (shards_of,), jnp.float32, low / len(shards), top_value / len(shards))
        loudness = loudness * jnp.repeat(jnp.exp(draws), shape[position] // shards_of).reshape((-1,) + (1,) * (len(shape) - 1 - position))
    return loudness


def scatter_about(rng, extent, scale, limit, cuts=(), held_as=jnp.bfloat16):
    level = block_scale(rng, extent, cuts, -0.22, 0.18) if cuts else 1.0
    drawn = jax.random.normal(rng, extent, jnp.float32) * scale * level
    return jnp.minimum(jnp.maximum(drawn, -limit), limit).astype(held_as)


def setup_inputs(seed: int = 0) -> dict:
    key_of = jax.random.split(jax.random.key(seed), 9)
    return {
        "layer_input": scatter_about(key_of[0], (TOKENS, D), 1.0, 6.0, ((0, 32),)),
        "out_grad": scatter_about(key_of[1], (TOKENS, D), 1.0, 6.0, ((0, 32),)),
        "routes": draw_routes(jax.random.fold_in(key_of[8], 71), 0),
        "gate_values": jnp.clip(0.1 + 0.9 * jax.random.uniform(key_of[3], (TOKENS, TOP), jnp.float32) ** block_scale(key_of[3], (TOKENS, TOP), ((0, 32),), -0.2, 0.2), 0.1, 1.0),
        "keep_mask": place_ends((jax.random.randint(key_of[4], (TOKENS, TOP), 0, 5) < 4).astype(jnp.int32), jax.random.fold_in(key_of[4], 1), 0, 1),
        "gate_weight": scatter_about(key_of[5], (D, LIVE * HID), D ** -0.5, 0.09375, ((0, 2), (1, 16))),
        "up_weight": scatter_about(key_of[6], (D, LIVE * HID), D ** -0.5, 0.09375, ((0, 2), (1, 16))),
        "down_transposed": scatter_about(key_of[7], (D, LIVE * HID), HID ** -0.5, 0.15625, ((0, 2), (1, 16))),
    }


def silu_parts(pre_gate):
    sigma = jax.nn.sigmoid(pre_gate)
    return pre_gate * sigma, sigma * (1.0 + pre_gate * (1.0 - sigma))


def route_tables(routes, keep_mask, live_count, slot_count):
    flat_routes = routes.reshape(-1)
    flat_keep = keep_mask.reshape(-1)
    expert_iota = jnp.arange(live_count, dtype=jnp.int32)
    chosen = ((flat_routes[:, None] == expert_iota[None, :]) & (flat_keep[:, None] == 1)).astype(jnp.int32)
    route_ranks = (jnp.cumsum(chosen, axis=0) - 1).astype(jnp.int32)
    slot_iota = jnp.arange(slot_count, dtype=jnp.int32)
    matched = chosen[:, :, None] * (route_ranks[:, :, None] == slot_iota[None, None, :]).astype(jnp.int32)
    route_iota = jnp.arange(flat_routes.shape[0], dtype=jnp.int32)
    picked = jnp.sum(matched * route_iota[:, None, None], axis=0).astype(jnp.int32)
    filled = jnp.sum(matched, axis=0).astype(jnp.int32)
    return picked.reshape(-1), filled.reshape(-1)


def expert_terms(slot_inputs, slot_grads, gate_part, up_part, down_part):
    pre_gate = jnp.dot(slot_inputs, gate_part, preferred_element_type=jnp.float32)
    pre_up = jnp.dot(slot_inputs, up_part, preferred_element_type=jnp.float32)
    activated, slope = silu_parts(pre_gate)
    hidden = (activated * pre_up).astype(jnp.bfloat16)
    hidden_grad = jnp.dot(slot_grads, down_part, preferred_element_type=jnp.float32)
    gate_side = (hidden_grad * pre_up * slope).astype(jnp.bfloat16)
    up_side = (hidden_grad * activated).astype(jnp.bfloat16)
    rows_first = (((0,), (0,)), ((), ()))
    weight_terms = (
        lax.dot_general(slot_inputs, gate_side, rows_first, preferred_element_type=jnp.float32),
        lax.dot_general(slot_inputs, up_side, rows_first, preferred_element_type=jnp.float32),
        lax.dot_general(slot_grads, hidden, rows_first, preferred_element_type=jnp.float32),
    )
    return gate_side, up_side, weight_terms


def reference(layer_input, out_grad, routes, gate_values, keep_mask, gate_weight, up_weight, down_transposed):
    blocks = N_EXPERT * N_DP
    picked, filled = jax.vmap(lambda block_routes, block_keep: route_tables(block_routes, block_keep, LIVE, MOST))(
        routes.reshape(blocks, TOK, TOP), keep_mask.reshape(blocks, TOK, TOP))
    block_start = (jnp.arange(blocks, dtype=jnp.int32) * TOK)[:, None]
    global_token = (picked // TOP + block_start).astype(jnp.int32)
    route_scale = jnp.take_along_axis(gate_values.reshape(blocks, TOK * TOP), picked, axis=1) * filled.astype(jnp.float32)
    slot_inputs = jnp.take(layer_input, global_token, axis=0) * filled.astype(layer_input.dtype)[:, :, None]
    slot_grads = (jnp.take(out_grad, global_token, axis=0).astype(jnp.float32) * route_scale[:, :, None]).astype(jnp.bfloat16)
    shaped_inputs = slot_inputs.reshape(N_EXPERT, N_DP, LIVE, MOST, D)
    shaped_grads = slot_grads.reshape(N_EXPERT, N_DP, LIVE, MOST, D)
    token_index = global_token.reshape(N_EXPERT, N_DP, LIVE, MOST)
    live_slots = filled.reshape(N_EXPERT, N_DP, LIVE, MOST).astype(jnp.float32)
    input_sum = jnp.zeros((TOKENS, D), jnp.float32)
    grad_totals = None
    for replica in range(N_DP):
        inputs_replica = shaped_inputs[:, replica]
        grads_replica = shaped_grads[:, replica]

        def one_expert(expert):
            start = expert * HID
            gate_part = lax.dynamic_slice_in_dim(gate_weight, start, HID, axis=1)
            up_part = lax.dynamic_slice_in_dim(up_weight, start, HID, axis=1)
            down_part = lax.dynamic_slice_in_dim(down_transposed, start, HID, axis=1)
            inputs_now = lax.dynamic_index_in_dim(inputs_replica, expert, axis=1, keepdims=False).reshape(-1, D)
            grads_now = lax.dynamic_index_in_dim(grads_replica, expert, axis=1, keepdims=False).reshape(-1, D)
            gate_side, up_side, weight_terms = expert_terms(inputs_now, grads_now, gate_part, up_part, down_part)
            slot_total = inputs_now.shape[0]
            pieces = jnp.einsum("smf,dmf->smd", gate_side.astype(jnp.float32).reshape(slot_total, SPLIT, F_DEV),
                                gate_part.astype(jnp.float32).reshape(D, SPLIT, F_DEV))
            pieces = pieces + jnp.einsum("smf,dmf->smd", up_side.astype(jnp.float32).reshape(slot_total, SPLIT, F_DEV),
                                         up_part.astype(jnp.float32).reshape(D, SPLIT, F_DEV))
            summed = jnp.sum(lax.optimization_barrier(pieces.astype(jnp.bfloat16)).astype(jnp.float32), axis=1)
            return summed, weight_terms

        summed, weight_terms = lax.map(one_expert, jnp.arange(LIVE, dtype=jnp.int32))
        values = jnp.transpose(summed.reshape(LIVE, N_EXPERT, MOST, D), (1, 0, 2, 3)) * live_slots[:, replica][:, :, :, None]
        input_sum = input_sum.at[token_index[:, replica].reshape(-1)].add(values.reshape(-1, D))
        rounded = tuple(lax.optimization_barrier(weight_term.astype(jnp.bfloat16)).astype(jnp.float32) for weight_term in weight_terms)
        if replica == 0:
            grad_totals = rounded
        else:
            grad_totals = tuple(first_term + second_term for first_term, second_term in zip(grad_totals, rounded))
    outputs = tuple(jnp.transpose(total_term, (1, 0, 2)).reshape(D, LIVE * HID).astype(jnp.bfloat16) for total_term in grad_totals)
    return input_sum.astype(jnp.bfloat16), outputs[0], outputs[1], outputs[2]
```

```python
import jax
import jax.numpy as jnp
from jax import lax
from jax.experimental import pallas as pl
from jax.experimental.pallas import tpu as pltpu
from jax.sharding import PartitionSpec as P

SPLIT = 4
MOST = 5
PIECE = 16
BACK = 8

F32 = jnp.float32
BF16 = jnp.bfloat16


def params(mib=40):
    return pltpu.CompilerParams(vmem_limit_bytes=mib * 1024 * 1024)


def cost(flops, moved):
    return pl.CostEstimate(flops=int(flops), bytes_accessed=int(moved), transcendentals=0)


def iota(shape, axis):
    return lax.broadcasted_iota(jnp.int32, shape, axis)


def dot(a, b, dims=((1,), (0,))):
    return lax.dot_general(a, b, (dims, ((), ())), preferred_element_type=F32)


def pick_rows(routes, keep, gates, expert, slot, valid):
    rows, tokens = expert.shape[0], routes.shape[1]
    chosen = jnp.zeros((rows, tokens), F32)
    gate = jnp.zeros((rows, tokens), F32)
    for k in range(routes.shape[0]):
        hit = (routes[k : k + 1, :] == expert) & (keep[k : k + 1, :] == 1)
        chosen = jnp.where(hit, 1.0, chosen)
        gate = jnp.where(hit, gates[k : k + 1, :], gate)
    upto = (iota((tokens, tokens), 0) <= iota((tokens, tokens), 1)).astype(BF16)
    rank = dot(chosen.astype(BF16), upto)
    hot = (chosen > 0.5) & (rank == (slot + 1).astype(F32)) & valid
    return hot, gate


def gather_kernel(live, where_ref, routes_ref, keep_ref, gates_ref, x_ref, o_ref, *outs):
    place = where_ref[0] // SPLIT
    me = where_ref[1]
    half = x_ref.shape[1] // 2
    pieces, back_ref = outs[:-1], outs[-1]
    routes, keep, gates = routes_ref[...], keep_ref[...], gates_ref[...]

    row = iota((live * PIECE, 1), 0)
    expert = lax.rem(place + row // PIECE, live)
    side = lax.rem(row, PIECE) // MOST
    slot = lax.rem(lax.rem(row, PIECE), MOST)
    hot, gate = pick_rows(routes, keep, gates, expert, slot, side < 2)
    hot_x = (hot & (side == 0)).astype(F32).astype(BF16)
    hot_s = hot & (side == 1)
    scale = jnp.sum(jnp.where(hot_s, gate, 0.0), axis=1, keepdims=True)
    hot_s = hot_s.astype(F32).astype(BF16)
    for q in range(2):
        start = pl.multiple_of((me ^ q) * half, 128)
        rows = dot(hot_x, x_ref[:, pl.ds(start, half)])
        rows = rows + scale * dot(hot_s, o_ref[:, pl.ds(start, half)])
        rows = rows.astype(BF16)
        for d in range(live):
            pieces[2 * d + q][...] = rows[d * PIECE : (d + 1) * PIECE]

    row = iota((live * BACK, 1), 0)
    expert = lax.rem(place + row // BACK, live)
    slot = lax.rem(row, BACK)
    hot, _ = pick_rows(routes, keep, gates, expert, slot, slot < MOST)
    back_ref[...] = hot.astype(F32)


def merge_kernel(live, where_ref, *refs):
    pieces, (x_ref, s_ref) = refs[:-2], refs[-2:]
    me = where_ref[1]
    rows = live * 2 * MOST
    stacked = jnp.concatenate([piece[...] for piece in pieces], axis=0)
    shape = (2 * rows, 2 * live * PIECE)
    out, source = iota(shape, 0), iota(shape, 1)
    side, at = out // rows, lax.rem(out, rows)
    d, replica, slot = at // (2 * MOST), lax.rem(at, 2 * MOST) // MOST, lax.rem(at, MOST)
    wanted = (2 * d + (replica ^ me)) * PIECE + side * MOST + slot
    merged = dot((source == wanted).astype(F32).astype(BF16), stacked).astype(BF16)
    x_ref[...] = merged[:rows]
    s_ref[...] = merged[rows:]


def partial_kernel(*refs):
    xs, ss = refs[:SPLIT], refs[SPLIT : 2 * SPLIT]
    gate_ref, up_ref, down_ref, out_ref = refs[2 * SPLIT :]
    x = jnp.concatenate([r[...] for r in xs], axis=0)
    s = jnp.concatenate([r[...] for r in ss], axis=0)
    width = gate_ref.shape[1]
    out = jnp.concatenate([dot(x, gate_ref[...]), dot(x, up_ref[...]), dot(s, down_ref[...])], axis=1)

    @pl.when(pl.program_id(0) == 0)
    def _():
        out_ref[...] = out

    @pl.when(pl.program_id(0) > 0)
    def _():
        out_ref[...] += out


def sides_kernel(mine_ref, other_ref, gate_ref, up_ref, *outs):
    parts, sides_ref = outs[:-1], outs[-1]
    width = gate_ref.shape[1]
    rows = mine_ref.shape[0] // SPLIT

    @pl.when(pl.program_id(0) == 0)
    def _():
        total = mine_ref[...] + other_ref[...]
        pre_gate, pre_up = total[:, :width], total[:, width : 2 * width]
        hidden_grad = total[:, 2 * width :]
        sigma = jax.nn.sigmoid(pre_gate)
        activated = pre_gate * sigma
        slope = sigma * (1.0 + pre_gate * (1.0 - sigma))
        sides_ref[:, :width] = (hidden_grad * pre_up * slope).astype(BF16)
        sides_ref[:, width : 2 * width] = (hidden_grad * activated).astype(BF16)
        sides_ref[:, 2 * width :] = (activated * pre_up).astype(BF16)

    across = ((1,), (1,))
    part = dot(sides_ref[:, :width], gate_ref[...], across)
    part = (part + dot(sides_ref[:, width : 2 * width], up_ref[...], across)).astype(BF16)
    for k in range(SPLIT):
        parts[k][...] = part[k * rows : (k + 1) * rows]


def grads_kernel(*refs):
    xs, ss = refs[:SPLIT], refs[SPLIT : 2 * SPLIT]
    sides_ref, gate_out, up_out, down_out = refs[2 * SPLIT :]
    width = gate_out.shape[1]
    x = jnp.concatenate([r[...] for r in xs], axis=0)
    s = jnp.concatenate([r[...] for r in ss], axis=0)
    first = ((0,), (0,))
    gate_out[...] = dot(x, sides_ref[:, :width], first).astype(BF16)
    up_out[...] = dot(x, sides_ref[:, width : 2 * width], first).astype(BF16)
    down_out[...] = dot(s, sides_ref[:, 2 * width :], first).astype(BF16)


def sum_kernel(live, where_ref, *refs):
    parts, outs = refs[:SPLIT], refs[SPLIT:]
    me = where_ref[1]
    total = parts[0][...].astype(F32)
    for part in parts[1:]:
        total = total + part[...].astype(F32)
    total = total.astype(BF16)
    rows = live * 2 * MOST
    shape = (2 * live * BACK, rows)
    out, source = iota(shape, 0), iota(shape, 1)
    d, q, slot = out // (2 * BACK), lax.rem(out, 2 * BACK) // BACK, lax.rem(out, BACK)
    wanted = d * 2 * MOST + (q ^ me) * MOST + slot
    take = (source == wanted) & (slot < MOST)
    moved = dot(take.astype(F32).astype(BF16), total)
    for piece in range(2 * live):
        outs[piece][...] = moved[piece * BACK : (piece + 1) * BACK].astype(BF16)


def place_kernel(live, where_ref, hot_ref, *refs):
    pieces, out_ref = refs[:-1], refs[-1]
    me = where_ref[1]
    half = out_ref.shape[1] // 2
    hot = hot_ref[...].astype(BF16)
    for q in range(2):
        rows = jnp.concatenate([pieces[2 * d + q][...].astype(F32) for d in range(live)], axis=0)
        start = pl.multiple_of((me ^ q) * half, 128)
        out_ref[:, pl.ds(start, half)] = dot(hot, rows.astype(BF16), ((0,), (0,))).astype(BF16)


def like(shape, dtype):
    return jax.ShapeDtypeStruct(shape, dtype)


def body(
    layer_input, out_grad, routes, gate_values, keep_mask, gate_weight, up_weight, down_transposed
):
    devices, cores = lax.axis_size("expert"), lax.axis_size("dp")
    live = devices // SPLIT
    tokens, model = layer_input.shape
    half, width = gate_weight.shape
    where = jnp.stack([lax.axis_index("expert"), lax.axis_index("dp")]).astype(jnp.int32)
    smem, vmem = pl.BlockSpec(memory_space=pltpu.SMEM), pl.BlockSpec(memory_space=pltpu.VMEM)
    rows = 2 * live * MOST
    total = SPLIT * rows

    def to_source(d, q, forth):
        moved = []
        for i in range(devices):
            for r in range(cores):
                g, m = (i // SPLIT + d) % live, i % SPLIT
                there = (g * SPLIT + m) * cores + (r ^ q)
                here = i * cores + r
                moved.append((here, there) if forth else (there, here))
        return moved

    def in_plane(k):
        return [(i, (i // SPLIT) * SPLIT + ((i % SPLIT) ^ k)) for i in range(devices)]

    def travel(pieces, forth):
        out = []
        for d in range(live):
            for q in range(2):
                piece = pieces[2 * d + q]
                if d or q:
                    piece = lax.ppermute(piece, ("expert", "dp"), to_source(d, q, forth))
                out.append(piece)
        return out

    gathered = pl.pallas_call(
        lambda *refs: gather_kernel(live, *refs),
        out_shape=[like((PIECE, half), BF16)] * (2 * live) + [like((live * BACK, tokens), F32)],
        in_specs=[smem] + [vmem] * 5,
        out_specs=[vmem] * (2 * live + 1),
        compiler_params=params(),
        name="gather_rows",
    )(where, routes.T, keep_mask.T, gate_values.T, layer_input, out_grad)
    pieces, hot = gathered[:-1], gathered[-1]
    pieces = travel(pieces, True)
    x_own, s_own = pl.pallas_call(
        lambda *refs: merge_kernel(live, *refs),
        out_shape=[like((rows, half), BF16)] * 2,
        in_specs=[smem] + [vmem] * (2 * live),
        out_specs=[vmem] * 2,
        compiler_params=params(),
        name="merge_rows",
    )(where, *pieces)
    xs = [x_own] + [lax.ppermute(x_own, "expert", in_plane(k)) for k in range(1, SPLIT)]
    ss = [s_own] + [lax.ppermute(s_own, "expert", in_plane(k)) for k in range(1, SPLIT)]

    chunk = 256
    steps = half // chunk
    row_block = pl.BlockSpec((rows, chunk), lambda j: (0, j))
    weight_block = pl.BlockSpec((chunk, width), lambda j: (j, 0))
    whole = pl.BlockSpec((total, 3 * width), lambda j: (0, 0))
    mine = pl.pallas_call(
        partial_kernel,
        out_shape=like((total, 3 * width), F32),
        grid=(steps,),
        in_specs=[row_block] * (2 * SPLIT) + [weight_block] * 3,
        out_specs=whole,
        compiler_params=params(),
        cost_estimate=cost(6 * total * half * width, 6 * half * width + 4 * total * half),
        name="partial_products",
    )(*xs, *ss, gate_weight, up_weight, down_transposed)
    other = lax.ppermute(mine, "dp", [(r, r ^ 1) for r in range(cores)])
    sided = pl.pallas_call(
        sides_kernel,
        out_shape=[like((rows, half), BF16)] * SPLIT + [like((total, 3 * width), BF16)],
        grid=(steps,),
        in_specs=[whole] * 2 + [weight_block] * 2,
        out_specs=[row_block] * SPLIT + [whole],
        compiler_params=params(),
        cost_estimate=cost(4 * total * half * width, 4 * half * width + 2 * total * half),
        name="sides_and_parts",
    )(mine, other, gate_weight, up_weight)
    parts, sides = sided[:-1], sided[-1]
    parts = [parts[0]] + [lax.ppermute(parts[k], "expert", in_plane(k)) for k in range(1, SPLIT)]
    gate_grad, up_grad, down_grad = pl.pallas_call(
        grads_kernel,
        out_shape=[like((half, width), BF16)] * 3,
        grid=(steps,),
        in_specs=[row_block] * (2 * SPLIT) + [whole],
        out_specs=[weight_block] * 3,
        compiler_params=params(),
        cost_estimate=cost(6 * total * half * width, 6 * half * width + 4 * total * half),
        name="weight_grads",
    )(*xs, *ss, sides)
    returned = pl.pallas_call(
        lambda *refs: sum_kernel(live, *refs),
        out_shape=[like((BACK, half), BF16)] * (2 * live),
        in_specs=[smem] + [vmem] * SPLIT,
        out_specs=[vmem] * (2 * live),
        compiler_params=params(),
        name="sum_parts",
    )(where, *parts)
    returned = travel(returned, False)
    input_grad = pl.pallas_call(
        lambda *refs: place_kernel(live, *refs),
        out_shape=like((tokens, model), BF16),
        in_specs=[smem] + [vmem] * (2 * live + 1),
        out_specs=vmem,
        compiler_params=params(),
        name="place_rows",
    )(where, hot, *returned)
    return (input_grad, gate_grad, up_grad, down_grad)


def solution(mesh):
    return jax.shard_map(
        body,
        mesh=mesh,
        in_specs=(
            P(("expert", "dp"), None),
            P(("expert", "dp"), None),
            P(("expert", "dp"), None),
            P(("expert", "dp"), None),
            P(("expert", "dp"), None),
            P("dp", "expert"),
            P("dp", "expert"),
            P("dp", "expert"),
        ),
        out_specs=(
            P(("expert", "dp"), None),
            P("dp", "expert"),
            P("dp", "expert"),
            P("dp", "expert"),
        ),
        check_vma=False,
    )
```

```python
import jax
import jax.numpy as jnp
from jax import lax
from jax.experimental import pallas as pl
from jax.experimental.pallas import tpu as pltpu
from jax.sharding import PartitionSpec as P

SPLIT = 4
MOST = 5
TOP = 8
PIECE = 16
BACK = 8

F32 = jnp.float32
BF16 = jnp.bfloat16


def params(mib=16):
    return pltpu.CompilerParams(vmem_limit_bytes=mib * 1024 * 1024)


def cost(flops, moved):
    return pl.CostEstimate(flops=int(flops), bytes_accessed=int(moved), transcendentals=0)


def iota(shape, axis):
    return lax.broadcasted_iota(jnp.int32, shape, axis)


def dot(a, b, dims=((1,), (0,))):
    return lax.dot_general(a, b, (dims, ((), ())), preferred_element_type=F32)


def pick_rows(routes, keep, gates, expert, slot, valid):
    rows, tokens = expert.shape[0], routes.shape[1]
    chosen = jnp.zeros((rows, tokens), F32)
    gate = jnp.zeros((rows, tokens), F32)
    for k in range(routes.shape[0]):
        hit = (routes[k : k + 1, :] == expert) & (keep[k : k + 1, :] == 1)
        chosen = jnp.where(hit, 1.0, chosen)
        gate = jnp.where(hit, gates[k : k + 1, :], gate)
    upto = (iota((tokens, tokens), 0) <= iota((tokens, tokens), 1)).astype(BF16)
    rank = dot(chosen.astype(BF16), upto)
    hot = (chosen > 0.5) & (rank == (slot + 1).astype(F32)) & valid
    return hot, gate


def gather_kernel(live, *refs):
    sources, (pieces_ref, back_ref), local, sems = refs[:5], refs[5:7], refs[7:12], refs[12]
    copies = [pltpu.make_async_copy(sources[i], local[i], sems.at[i]) for i in range(5)]
    for copy in copies:
        copy.start()
    routes_ref, keep_ref, gates_ref, x_ref, o_ref = local
    for copy in copies[:3]:
        copy.wait()
    half = x_ref.shape[1] // 2
    routes, keep, gates = routes_ref[...], keep_ref[...], gates_ref[...]

    row = iota((live * BACK, 1), 0)
    slot = lax.rem(row, BACK)
    hot, _ = pick_rows(routes, keep, gates, row // BACK, slot, slot < MOST)
    back_ref[...] = hot.astype(F32)

    row = iota((live * PIECE, 1), 0)
    side = lax.rem(row, PIECE) // MOST
    slot = lax.rem(lax.rem(row, PIECE), MOST)
    hot, gate = pick_rows(routes, keep, gates, row // PIECE, slot, side < 2)
    hot_x = (hot & (side == 0)).astype(F32).astype(BF16)
    hot_s = hot & (side == 1)
    scale = jnp.sum(jnp.where(hot_s, gate, 0.0), axis=1, keepdims=True)
    hot_s = hot_s.astype(F32).astype(BF16)
    for copy in copies[3:]:
        copy.wait()
    for core in range(2):
        columns = slice(core * half, (core + 1) * half)
        rows = dot(hot_x, x_ref[:, columns]) + scale * dot(hot_s, o_ref[:, columns])
        rows = rows.astype(BF16)
        for g in range(live):
            pieces_ref[2 * g + core] = rows[g * PIECE : (g + 1) * PIECE]


def merge_kernel(live, pieces_ref, out_ref):
    rows = live * 2 * MOST
    stacked = jnp.concatenate([pieces_ref[p] for p in range(2 * live)], axis=0)
    shape = (2 * rows, 2 * live * PIECE)
    out, source = iota(shape, 0), iota(shape, 1)
    side, at = out // rows, lax.rem(out, rows)
    wanted = (at // MOST) * PIECE + side * MOST + lax.rem(at, MOST)
    merged = dot((source == wanted).astype(F32).astype(BF16), stacked).astype(BF16)
    for k in range(SPLIT):
        out_ref[k] = merged


def rows_of(rows_ref, side):
    rows = rows_ref.shape[1] // 2
    return jnp.concatenate([rows_ref[m, side * rows : (side + 1) * rows] for m in range(SPLIT)], axis=0)


def partial_kernel(rows_ref, gate_ref, up_ref, down_ref, out_ref):
    x, s = rows_of(rows_ref, 0), rows_of(rows_ref, 1)
    out = jnp.concatenate([dot(x, gate_ref[...]), dot(x, up_ref[...]), dot(s, down_ref[...])], axis=1)

    @pl.when(pl.program_id(0) == 0)
    def _():
        out_ref[...] = out

    @pl.when(pl.program_id(0) > 0)
    def _():
        out_ref[...] += out


def sides_kernel(mine_ref, other_ref, gate_ref, up_ref, parts_ref, sides_ref):
    width = gate_ref.shape[1]
    rows = mine_ref.shape[0] // SPLIT

    @pl.when(pl.program_id(0) == 0)
    def _():
        total = mine_ref[...] + other_ref[...]
        pre_gate, pre_up = total[:, :width], total[:, width : 2 * width]
        hidden_grad = total[:, 2 * width :]
        sigma = jax.nn.sigmoid(pre_gate)
        activated = pre_gate * sigma
        slope = sigma * (1.0 + pre_gate * (1.0 - sigma))
        sides_ref[:, :width] = (hidden_grad * pre_up * slope).astype(BF16)
        sides_ref[:, width : 2 * width] = (hidden_grad * activated).astype(BF16)
        sides_ref[:, 2 * width :] = (activated * pre_up).astype(BF16)

    across = ((1,), (1,))
    part = dot(sides_ref[:, :width], gate_ref[...], across)
    part = (part + dot(sides_ref[:, width : 2 * width], up_ref[...], across)).astype(BF16)
    for k in range(SPLIT):
        parts_ref[k] = part[k * rows : (k + 1) * rows]


def grads_kernel(rows_ref, sides_ref, gate_out, up_out, down_out):
    width = gate_out.shape[1]
    x, s = rows_of(rows_ref, 0), rows_of(rows_ref, 1)
    first = ((0,), (0,))
    gate_out[...] = dot(x, sides_ref[:, :width], first).astype(BF16)
    up_out[...] = dot(x, sides_ref[:, width : 2 * width], first).astype(BF16)
    down_out[...] = dot(s, sides_ref[:, 2 * width :], first).astype(BF16)


def sum_kernel(live, parts_ref, out_ref):
    total = parts_ref[0].astype(F32)
    for m in range(1, SPLIT):
        total = total + parts_ref[m].astype(F32)
    total = total.astype(BF16)
    shape = (2 * live * BACK, live * 2 * MOST)
    out, source = iota(shape, 0), iota(shape, 1)
    slot = lax.rem(out, BACK)
    take = (source == (out // BACK) * MOST + slot) & (slot < MOST)
    moved = dot(take.astype(F32).astype(BF16), total)
    for piece in range(2 * live):
        out_ref[piece] = moved[piece * BACK : (piece + 1) * BACK].astype(BF16)


def place_kernel(live, hot_ref, pieces_ref, out_ref):
    half = out_ref.shape[1] // 2
    hot = hot_ref[...].astype(BF16)
    for core in range(2):
        rows = jnp.concatenate([pieces_ref[2 * g + core].astype(F32) for g in range(live)], axis=0)
        columns = slice(core * half, (core + 1) * half)
        out_ref[:, columns] = dot(hot, rows.astype(BF16), ((0,), (0,))).astype(BF16)


def like(shape, dtype):
    return jax.ShapeDtypeStruct(shape, dtype)


def body(
    layer_input, out_grad, routes, gate_values, keep_mask, gate_weight, up_weight, down_transposed
):
    devices, cores = lax.axis_size("expert"), lax.axis_size("dp")
    live = devices // SPLIT
    tokens, model = layer_input.shape
    half, width = gate_weight.shape
    vmem, hbm = pl.BlockSpec(memory_space=pltpu.VMEM), pl.BlockSpec(memory_space=pltpu.HBM)
    rows = 2 * live * MOST
    total = SPLIT * rows

    def through_planes(array):
        groups = [
            [(g * SPLIT + m) * cores + r for g in range(live) for r in range(cores)]
            for m in range(SPLIT)
        ]
        return lax.all_to_all(array, ("expert", "dp"), 0, 0, axis_index_groups=groups, tiled=True)

    def in_plane(array):
        groups = [[g * SPLIT + m for m in range(SPLIT)] for g in range(live)]
        return lax.all_to_all(array, "expert", 0, 0, axis_index_groups=groups, tiled=True)

    pieces, hot = pl.pallas_call(
        lambda *refs: gather_kernel(live, *refs),
        out_shape=[like((2 * live, PIECE, half), BF16), like((live * BACK, tokens), F32)],
        in_specs=[hbm] * 5,
        out_specs=[vmem] * 2,
        scratch_shapes=[
            pltpu.VMEM((TOP, tokens), jnp.int32),
            pltpu.VMEM((TOP, tokens), jnp.int32),
            pltpu.VMEM((TOP, tokens), F32),
            pltpu.VMEM((tokens, model), BF16),
            pltpu.VMEM((tokens, model), BF16),
            pltpu.SemaphoreType.DMA((5,)),
        ],
        compiler_params=params(),
        name="gather_rows",
    )(routes.T, keep_mask.T, gate_values.T, layer_input, out_grad)
    copies = pl.pallas_call(
        lambda *refs: merge_kernel(live, *refs),
        out_shape=like((SPLIT, 2 * rows, half), BF16),
        in_specs=[vmem],
        out_specs=vmem,
        compiler_params=params(),
        name="merge_rows",
    )(through_planes(pieces))
    slots = in_plane(copies)

    chunk = 256
    steps = half // chunk
    row_block = pl.BlockSpec((SPLIT, 2 * rows, chunk), lambda j: (0, 0, j))
    part_block = pl.BlockSpec((SPLIT, rows, chunk), lambda j: (0, 0, j))
    weight_block = pl.BlockSpec((chunk, width), lambda j: (j, 0))
    whole = pl.BlockSpec((total, 3 * width), lambda j: (0, 0))
    mine = pl.pallas_call(
        partial_kernel,
        out_shape=like((total, 3 * width), F32),
        grid=(steps,),
        in_specs=[row_block] + [weight_block] * 3,
        out_specs=whole,
        compiler_params=params(),
        cost_estimate=cost(6 * total * half * width, 6 * half * width + 4 * total * half),
        name="partial_products",
    )(slots, gate_weight, up_weight, down_transposed)
    other = lax.ppermute(mine, "dp", [(r, r ^ 1) for r in range(cores)])
    parts, sides = pl.pallas_call(
        sides_kernel,
        out_shape=[like((SPLIT, rows, half), BF16), like((total, 3 * width), BF16)],
        grid=(steps,),
        in_specs=[whole] * 2 + [weight_block] * 2,
        out_specs=[part_block, whole],
        compiler_params=params(),
        cost_estimate=cost(4 * total * half * width, 4 * half * width + 2 * total * half),
        name="sides_and_parts",
    )(mine, other, gate_weight, up_weight)
    parts = in_plane(parts)
    gate_grad, up_grad, down_grad = pl.pallas_call(
        grads_kernel,
        out_shape=[like((half, width), BF16)] * 3,
        grid=(steps,),
        in_specs=[row_block, whole],
        out_specs=[weight_block] * 3,
        compiler_params=params(),
        cost_estimate=cost(6 * total * half * width, 6 * half * width + 4 * total * half),
        name="weight_grads",
    )(slots, sides)
    returned = pl.pallas_call(
        lambda *refs: sum_kernel(live, *refs),
        out_shape=like((2 * live, BACK, half), BF16),
        in_specs=[vmem],
        out_specs=vmem,
        compiler_params=params(),
        name="sum_parts",
    )(parts)
    input_grad = pl.pallas_call(
        lambda *refs: place_kernel(live, *refs),
        out_shape=like((tokens, model), BF16),
        in_specs=[vmem] * 2,
        out_specs=vmem,
        compiler_params=params(),
        name="place_rows",
    )(hot, through_planes(returned))
    return (input_grad, gate_grad, up_grad, down_grad)


def solution(mesh):
    return jax.shard_map(
        body,
        mesh=mesh,
        in_specs=(
            P(("expert", "dp"), None),
            P(("expert", "dp"), None),
            P(("expert", "dp"), None),
            P(("expert", "dp"), None),
            P(("expert", "dp"), None),
            P("dp", "expert"),
            P("dp", "expert"),
            P("dp", "expert"),
        ),
        out_specs=(
            P(("expert", "dp"), None),
            P("dp", "expert"),
            P("dp", "expert"),
            P("dp", "expert"),
        ),
        check_vma=False,
    )
```

```python
import jax
import jax.numpy as jnp
from jax import lax
from jax.experimental import pallas as pl
from jax.experimental.pallas import tpu as pltpu
from jax.sharding import PartitionSpec as P

SPLIT = 4
MOST = 5
TOP = 8
SIDES = 2
CORES = 2
FOLDS = 2
FIRST_MIB = 60
CHUNKS = 7

F32 = jnp.float32
BF16 = jnp.bfloat16


def params(mib=16):
    return pltpu.CompilerParams(vmem_limit_bytes=int(mib * 1024 * 1024))


def cost(flops, moved):
    return pl.CostEstimate(flops=int(flops), bytes_accessed=int(moved), transcendentals=0)


def iota(shape, axis):
    return lax.broadcasted_iota(jnp.int32, shape, axis)


def dot(a, b, dims=((1,), (0,))):
    return lax.dot_general(a, b, (dims, ((), ())), preferred_element_type=F32)


def one_hot(wanted, columns):
    return (iota((wanted.shape[0], columns), 1) == wanted).astype(F32).astype(BF16)


def pick_rows(routes, keep, gates, expert, slot, valid):
    rows, tokens = expert.shape[0], routes.shape[1]
    chosen = jnp.zeros((rows, tokens), F32)
    gate = jnp.zeros((rows, tokens), F32)
    for k in range(routes.shape[0]):
        hit = (routes[k : k + 1, :] == expert) & (keep[k : k + 1, :] == 1)
        chosen = jnp.where(hit, 1.0, chosen)
        gate = jnp.where(hit, gates[k : k + 1, :], gate)
    upto = (iota((tokens, tokens), 0) <= iota((tokens, tokens), 1)).astype(F32).astype(BF16)
    rank = dot(chosen.astype(BF16), upto)
    hot = (chosen > 0.5) & (rank == (slot + 1).astype(F32)) & valid
    return hot, gate


def gather_kernel(live, *refs):
    sources, outs, local, sems = refs[:5], refs[5:8], refs[8:13], refs[13]
    copies = [pltpu.make_async_copy(sources[i], local[i], sems.at[i]) for i in range(5)]
    for copy in copies:
        copy.start()
    routes_ref, keep_ref, gates_ref, x_ref, o_ref = local
    place, me = lax.axis_index("expert") // SPLIT, lax.axis_index("dp")
    half = x_ref.shape[1] // CORES
    for copy in copies[:3]:
        copy.wait()
    routes, keep, gates = routes_ref[...], keep_ref[...], gates_ref[...]

    row = iota((live * 8, 1), 0)
    expert, slot = lax.rem(place + row // 8, live), lax.rem(row, 8)
    hot, _ = pick_rows(routes, keep, gates, expert, slot, slot < MOST)
    outs[2][...] = hot.astype(F32)

    row = iota((live * SIDES * MOST, 1), 0)
    expert = lax.rem(place + row // (SIDES * MOST), live)
    side, slot = lax.rem(row // MOST, SIDES), lax.rem(row, MOST)
    hot, gate = pick_rows(routes, keep, gates, expert, slot, row >= 0)
    hot_x = (hot & (side == 0)).astype(F32).astype(BF16)
    hot_s = hot & (side == 1)
    scale = jnp.sum(jnp.where(hot_s, gate, 0.0), axis=1, keepdims=True)
    hot_s = hot_s.astype(F32).astype(BF16)
    for copy in copies[3:]:
        copy.wait()
    for q in range(CORES):
        columns = pl.ds(pl.multiple_of((me ^ q) * half, 128), half)
        rows = dot(hot_x, x_ref[:, columns]) + scale * dot(hot_s, o_ref[:, columns])
        outs[q][...] = rows.astype(BF16)


def chunk_kernel(live, mine_ref, other_ref, *outs):
    me = lax.axis_index("dp")
    rows, half = mine_ref.shape
    fold = half // FOLDS
    each = SIDES * MOST
    stacked = jnp.concatenate([mine_ref[...], other_ref[...]], axis=0)
    size = FOLDS * CORES * each
    row = iota((live * size, 1), 0)
    d, part, at = row // size, lax.rem(row // (CORES * each), FOLDS), lax.rem(row, CORES * each)
    wanted = (at // each ^ me) * rows + d * each + lax.rem(at, each)
    total = jnp.zeros((live * size, fold), F32)
    for f in range(FOLDS):
        pick = one_hot(jnp.where(part == f, wanted, -1), CORES * rows)
        total = total + dot(pick, stacked[:, f * fold : (f + 1) * fold])
    total = total.astype(BF16)
    for d in range(live):
        outs[d][...] = total[d * size : (d + 1) * size]


def merge_kernel(live, *refs):
    chunks, outs = refs[:live], refs[live:]
    size, fold = chunks[0].shape
    stacked = jnp.concatenate([chunk[...] for chunk in chunks], axis=0)
    rows = live * CORES * MOST
    out = iota((SIDES * rows, 1), 0)
    side, at = out // rows, lax.rem(out, rows)
    d, replica, slot = at // (CORES * MOST), lax.rem(at // MOST, CORES), lax.rem(at, MOST)
    for f in range(FOLDS):
        wanted = d * size + ((f * CORES + replica) * SIDES + side) * MOST + slot
        picked = dot(one_hot(wanted, live * size), stacked).astype(BF16)
        for s in range(SIDES):
            outs[s][:, f * fold : (f + 1) * fold] = picked[s * rows : (s + 1) * rows]


def rows_of(refs):
    return jnp.concatenate([ref[...] for ref in refs], axis=0)


def partial_kernel(*refs):
    x, s = rows_of(refs[:SPLIT]), rows_of(refs[SPLIT : 2 * SPLIT])
    sources, out_ref, held, sems = refs[2 * SPLIT : -5], refs[-5], refs[-4:-1], refs[-1]
    width = held[0].shape[1]
    copies = [pltpu.make_async_copy(sources[i], held[i], sems.at[i]) for i in range(3)]
    for copy in copies:
        copy.start()
    for i, rows in enumerate((x, x, s)):
        copies[i].wait()
        out_ref[:, i * width : (i + 1) * width] = dot(rows, held[i][...])


def sides_kernel(mine_ref, other_ref, gate_ref, up_ref, *outs):
    parts, sides_ref = outs[:SPLIT], outs[SPLIT]
    width = gate_ref.shape[1]
    rows = mine_ref.shape[0] // SPLIT
    total = mine_ref[...] + other_ref[...]
    pre_gate, pre_up = total[:, :width], total[:, width : 2 * width]
    hidden_grad = total[:, 2 * width :]
    sigma = jax.nn.sigmoid(pre_gate)
    activated = pre_gate * sigma
    slope = sigma * (1.0 + pre_gate * (1.0 - sigma))
    gate_side = (hidden_grad * pre_up * slope).astype(BF16)
    up_side = (hidden_grad * activated).astype(BF16)
    sides_ref[:, :width] = gate_side
    sides_ref[:, width : 2 * width] = up_side
    sides_ref[:, 2 * width :] = (activated * pre_up).astype(BF16)
    across = ((1,), (1,))
    part = (dot(gate_side, gate_ref[...], across) + dot(up_side, up_ref[...], across)).astype(BF16)
    for k in range(SPLIT):
        parts[k][...] = part[k * rows : (k + 1) * rows]


def grads_kernel(*refs):
    xs, ss = refs[:SPLIT], refs[SPLIT : 2 * SPLIT]
    sides_ref, outs, token_ref = refs[2 * SPLIT], refs[2 * SPLIT + 1 : -5], refs[-5]
    held, sems = refs[-4:-1], refs[-1]
    half, width = held[0].shape
    block = half // CHUNKS
    first = ((0,), (0,))
    copies = []
    for c in range(CHUNKS):
        part = slice(c * block, (c + 1) * block)
        x = jnp.concatenate([ref[:, part] for ref in xs], axis=0)
        s = jnp.concatenate([ref[:, part] for ref in ss], axis=0)
        for i, rows in enumerate((x, x, s)):
            held[i][part, :] = dot(rows, sides_ref[:, i * width : (i + 1) * width], first).astype(BF16)
            copy = pltpu.make_async_copy(
                held[i].at[pl.ds(c * block, block)], outs[i].at[pl.ds(c * block, block)], sems.at[i, c]
            )
            copy.start()
            copies.append(copy)
    for copy in copies:
        copy.wait()
    token_ref[...] = jnp.zeros(token_ref.shape, F32)


def sum_kernel(live, *refs):
    parts, outs = refs[:SPLIT], refs[SPLIT + 1 :]
    total = parts[0][...].astype(F32)
    for part in parts[1:]:
        total = total + part[...].astype(F32)
    total = total.astype(BF16)
    rows, half = total.shape
    fold = half // FOLDS
    each = CORES * MOST
    size = FOLDS * each
    row = iota((live * size, 1), 0)
    d, part, at = row // size, lax.rem(row // each, FOLDS), lax.rem(row, each)
    moved = jnp.zeros((live * size, fold), F32)
    for f in range(FOLDS):
        pick = one_hot(jnp.where(part == f, d * each + at, -1), rows)
        moved = moved + dot(pick, total[:, f * fold : (f + 1) * fold])
    for d in range(live):
        outs[d][...] = moved[d * size : (d + 1) * size].astype(BF16)


def split_kernel(live, *refs):
    chunks, outs = refs[:live], refs[live:]
    me = lax.axis_index("dp")
    size, fold = chunks[0].shape
    stacked = jnp.concatenate([chunk[...].astype(F32) for chunk in chunks], axis=0).astype(BF16)
    rows = live * 8
    out = iota((CORES * rows, 1), 0)
    q, d, slot = out // rows, lax.rem(out, rows) // 8, lax.rem(out, 8)
    for f in range(FOLDS):
        wanted = d * size + (f * CORES + (q ^ me)) * MOST + slot
        picked = dot(one_hot(jnp.where(slot < MOST, wanted, -1), live * size), stacked).astype(BF16)
        for core in range(CORES):
            outs[core][:, f * fold : (f + 1) * fold] = picked[core * rows : (core + 1) * rows]


def place_kernel(hot_ref, mine_ref, other_ref, out_ref):
    me = lax.axis_index("dp")
    half = mine_ref.shape[1]
    hot = hot_ref[...].astype(BF16)
    for q, ref in enumerate((mine_ref, other_ref)):
        columns = pl.ds(pl.multiple_of((me ^ q) * half, 128), half)
        out_ref[:, columns] = dot(hot, ref[...], ((0,), (0,))).astype(BF16)


def like(shape, dtype):
    return jax.ShapeDtypeStruct(shape, dtype)


def body(
    layer_input, out_grad, routes, gate_values, keep_mask, gate_weight, up_weight, down_transposed
):
    devices = lax.axis_size("expert")
    live = devices // SPLIT
    tokens, model = layer_input.shape
    half, width = gate_weight.shape
    fold = half // FOLDS
    rows = CORES * live * MOST
    total = SPLIT * rows
    vmem, hbm = pl.BlockSpec(memory_space=pltpu.VMEM), pl.BlockSpec(memory_space=pltpu.HBM)

    def call(kernel, name, out_shape, operands, flops=0, moved=0):
        return pl.pallas_call(
            kernel,
            out_shape=out_shape,
            in_specs=[vmem] * len(operands),
            out_specs=jax.tree.map(lambda _: vmem, out_shape),
            compiler_params=params(),
            cost_estimate=cost(flops, moved) if flops else None,
            name=name,
        )(*operands)

    def swap_cores(array):
        return lax.ppermute(array, "dp", [(r, r ^ 1) for r in range(CORES)])

    def along_z(array, d):
        hop = [(i, (i + d * SPLIT) % devices) for i in range(devices)]
        return lax.ppermute(array, "expert", hop)

    def in_plane(array, k):
        hop = [(i, i // SPLIT * SPLIT + (i % SPLIT ^ k)) for i in range(devices)]
        return lax.ppermute(array, "expert", hop)

    gathered = like((live * SIDES * MOST, half), BF16)
    mine, other, hot = pl.pallas_call(
        lambda *refs: gather_kernel(live, *refs),
        out_shape=[gathered, gathered, like((live * 8, tokens), F32)],
        in_specs=[hbm] * 5,
        out_specs=[vmem] * 3,
        scratch_shapes=[
            pltpu.VMEM((TOP, tokens), jnp.int32),
            pltpu.VMEM((TOP, tokens), jnp.int32),
            pltpu.VMEM((TOP, tokens), F32),
            pltpu.VMEM((tokens, model), BF16),
            pltpu.VMEM((tokens, model), BF16),
            pltpu.SemaphoreType.DMA((5,)),
        ],
        compiler_params=params(FIRST_MIB),
        name="gather_rows",
    )(routes.T, keep_mask.T, gate_values.T, layer_input, out_grad)
    chunks = call(
        lambda *refs: chunk_kernel(live, *refs),
        "chunk_rows",
        [like((FOLDS * CORES * SIDES * MOST, fold), BF16)] * live,
        [mine, swap_cores(other)],
        4e9,
        8e6,
    )
    chunks = [chunks[0]] + [along_z(chunks[d], d) for d in range(1, live)]
    x, s = call(
        lambda *refs: merge_kernel(live, *refs), "merge_rows", [like((rows, half), BF16)] * 2, chunks, 4e9, 8e6
    )
    x1, s1, x2, s2 = in_plane(x, 1), in_plane(s, 1), in_plane(x, 2), in_plane(s, 2)
    xs = [x, x1, x2, in_plane(x1, 2)]
    ss = [s, s1, s2, in_plane(s2, 1)]
    mine = pl.pallas_call(
        partial_kernel,
        out_shape=like((total, 3 * width), F32),
        in_specs=[vmem] * (2 * SPLIT) + [hbm] * 3,
        out_specs=vmem,
        scratch_shapes=[pltpu.VMEM((half, width), BF16)] * 3 + [pltpu.SemaphoreType.DMA((3,))],
        compiler_params=params(),
        cost_estimate=cost(6 * total * half * width, 6 * half * width),
        name="partial_products",
    )(*xs, *ss, gate_weight, up_weight, down_transposed)
    sided = call(
        sides_kernel,
        "sides_and_parts",
        [like((rows, half), BF16)] * SPLIT + [like((total, 3 * width), BF16)],
        [mine, swap_cores(mine), gate_weight, up_weight],
        4 * total * half * width,
        4 * half * width,
    )
    parts, sides = sided[:SPLIT], sided[SPLIT]
    parts = [parts[0]] + [in_plane(parts[k], k) for k in range(1, SPLIT)]
    gate_grad, up_grad, down_grad, token = pl.pallas_call(
        grads_kernel,
        out_shape=[like((half, width), BF16)] * 3 + [like((8, 128), F32)],
        in_specs=[vmem] * (2 * SPLIT + 1),
        out_specs=[hbm] * 3 + [vmem],
        scratch_shapes=[pltpu.VMEM((half, width), BF16)] * 3 + [pltpu.SemaphoreType.DMA((3, CHUNKS))],
        compiler_params=params(),
        cost_estimate=cost(6 * total * half * width, 6 * half * width + 4 * total * half),
        name="weight_grads",
    )(*xs, *ss, sides)
    chunks = call(
        lambda *refs: sum_kernel(live, *refs),
        "sum_parts",
        [like((FOLDS * CORES * MOST, fold), BF16)] * live,
        [*parts, token],
    )
    chunks = [chunks[0]] + [along_z(chunks[d], -d) for d in range(1, live)]
    back, over = call(
        lambda *refs: split_kernel(live, *refs),
        "split_rows",
        [like((live * 8, half), BF16)] * 2,
        chunks,
    )
    input_grad = call(
        place_kernel, "place_rows", like((tokens, model), BF16), [hot, back, swap_cores(over)]
    )
    return (input_grad, gate_grad, up_grad, down_grad)


def solution(mesh):
    return jax.shard_map(
        body,
        mesh=mesh,
        in_specs=(
            P(("expert", "dp"), None),
            P(("expert", "dp"), None),
            P(("expert", "dp"), None),
            P(("expert", "dp"), None),
            P(("expert", "dp"), None),
            P("dp", "expert"),
            P("dp", "expert"),
            P("dp", "expert"),
        ),
        out_specs=(
            P(("expert", "dp"), None),
            P("dp", "expert"),
            P("dp", "expert"),
            P("dp", "expert"),
        ),
        check_vma=False,
    )
```

```python
import jax
import jax.numpy as jnp
from jax import lax
from jax.experimental import pallas as pl
from jax.experimental.pallas import tpu as pltpu
from jax.sharding import PartitionSpec as P

SPLIT = 4
MOST = 5
TOP = 8
SIDES = 2
CORES = 2
GROUPS = 2
FOLDS = 2
FIRST_MIB = 60
CHUNKS = 7

F32 = jnp.float32
BF16 = jnp.bfloat16


def params(mib=16):
    return pltpu.CompilerParams(vmem_limit_bytes=int(mib * 1024 * 1024))


def cost(flops, moved):
    return pl.CostEstimate(flops=int(flops), bytes_accessed=int(moved), transcendentals=0)


def iota(shape, axis):
    return lax.broadcasted_iota(jnp.int32, shape, axis)


def dot(a, b, dims=((1,), (0,))):
    return lax.dot_general(a, b, (dims, ((), ())), preferred_element_type=F32)


def one_hot(wanted, columns):
    return (iota((wanted.shape[0], columns), 1) == wanted).astype(F32).astype(BF16)


def pick_rows(routes, keep, gates, expert, slot, valid):
    rows, tokens = expert.shape[0], routes.shape[1]
    chosen = jnp.zeros((rows, tokens), F32)
    gate = jnp.zeros((rows, tokens), F32)
    for k in range(routes.shape[0]):
        hit = (routes[k : k + 1, :] == expert) & (keep[k : k + 1, :] == 1)
        chosen = jnp.where(hit, 1.0, chosen)
        gate = jnp.where(hit, gates[k : k + 1, :], gate)
    upto = (iota((tokens, tokens), 0) <= iota((tokens, tokens), 1)).astype(F32).astype(BF16)
    rank = dot(chosen.astype(BF16), upto)
    hot = (chosen > 0.5) & (rank == (slot + 1).astype(F32)) & valid
    return hot, gate


def gather_kernel(live, *refs):
    sources, outs, local, sems = refs[:5], refs[5:8], refs[8:13], refs[13]
    copies = [pltpu.make_async_copy(sources[i], local[i], sems.at[i]) for i in range(5)]
    for copy in copies:
        copy.start()
    routes_ref, keep_ref, gates_ref, x_ref, o_ref = local
    place, me = lax.axis_index("expert") // SPLIT, lax.axis_index("dp")
    half = x_ref.shape[1] // CORES
    for copy in copies[:3]:
        copy.wait()
    routes, keep, gates = routes_ref[...], keep_ref[...], gates_ref[...]

    row = iota((live * 8, 1), 0)
    expert, slot = place ^ (row // 8), lax.rem(row, 8)
    hot, _ = pick_rows(routes, keep, gates, expert, slot, slot < MOST)
    outs[2][...] = hot.astype(F32)

    row = iota((live * SIDES * MOST, 1), 0)
    expert = place ^ (row // (SIDES * MOST))
    side, slot = lax.rem(row // MOST, SIDES), lax.rem(row, MOST)
    hot, gate = pick_rows(routes, keep, gates, expert, slot, row >= 0)
    hot_x = (hot & (side == 0)).astype(F32).astype(BF16)
    hot_s = hot & (side == 1)
    scale = jnp.sum(jnp.where(hot_s, gate, 0.0), axis=1, keepdims=True)
    hot_s = hot_s.astype(F32).astype(BF16)
    for copy in copies[3:]:
        copy.wait()
    for q in range(CORES):
        columns = pl.ds(pl.multiple_of((me ^ q) * half, 128), half)
        rows = dot(hot_x, x_ref[:, columns]) + scale * dot(hot_s, o_ref[:, columns])
        outs[q][...] = rows.astype(BF16)


def chunk_kernel(live, mine_ref, other_ref, *outs):
    me = lax.axis_index("dp")
    rows, half = mine_ref.shape
    fold = half // FOLDS
    each = SIDES * MOST
    stacked = jnp.concatenate([mine_ref[...], other_ref[...]], axis=0)
    size = FOLDS * CORES * each
    row = iota((live * size, 1), 0)
    d, part, at = row // size, lax.rem(row // (CORES * each), FOLDS), lax.rem(row, CORES * each)
    wanted = (at // each ^ me) * rows + d * each + lax.rem(at, each)
    total = jnp.zeros((live * size, fold), F32)
    for f in range(FOLDS):
        pick = one_hot(jnp.where(part == f, wanted, -1), CORES * rows)
        total = total + dot(pick, stacked[:, f * fold : (f + 1) * fold])
    total = total.astype(BF16)
    for d in range(live):
        outs[d][...] = total[d * size : (d + 1) * size]


def merge_kernel(*refs):
    chunks, out_ref = refs[:-1], refs[-1]
    size, fold = chunks[0].shape
    stacked = jnp.concatenate([chunk[...] for chunk in chunks], axis=0)
    rows = len(chunks) * CORES * MOST
    out = iota((SIDES * rows, 1), 0)
    side, at = out // rows, lax.rem(out, rows)
    d, replica, slot = at // (CORES * MOST), lax.rem(at // MOST, CORES), lax.rem(at, MOST)
    for f in range(FOLDS):
        wanted = d * size + ((f * CORES + replica) * SIDES + side) * MOST + slot
        picked = dot(one_hot(wanted, len(chunks) * size), stacked)
        out_ref[:, f * fold : (f + 1) * fold] = picked.astype(BF16)


def partial_kernel(*refs):
    blocks, (gate_ref, up_ref, down_ref, out_ref), sided = refs[:SPLIT], refs[SPLIT:-2], refs[-2:]
    each, width = blocks[0].shape[0], gate_ref.shape[1]
    rows = each // SIDES
    stacked = jnp.concatenate([block[...] for block in blocks], axis=0)
    at = iota((SPLIT * rows, 1), 0)
    for side in range(SIDES):
        wanted = at // rows * each + side * rows + lax.rem(at, rows)
        sided[side][...] = dot(one_hot(wanted, SPLIT * each), stacked).astype(BF16)
    out_ref[:, :width] = dot(sided[0][...], gate_ref[...])
    out_ref[:, width : 2 * width] = dot(sided[0][...], up_ref[...])
    out_ref[:, 2 * width :] = dot(sided[1][...], down_ref[...])


def sides_kernel(*refs):
    sums, (gate_ref, up_ref), outs = refs[: 2 * GROUPS], refs[2 * GROUPS : 2 * GROUPS + 2], refs[2 * GROUPS + 2 :]
    parts, sides_ref = outs[:SPLIT], outs[SPLIT]
    width = gate_ref.shape[1]
    rows = parts[0].shape[0]
    total = [sums[i][...] + sums[GROUPS + i][...] for i in range(GROUPS)]
    total = jnp.concatenate(total, axis=0)
    pre_gate, pre_up = total[:, :width], total[:, width : 2 * width]
    hidden_grad = total[:, 2 * width :]
    sigma = jax.nn.sigmoid(pre_gate)
    activated = pre_gate * sigma
    slope = sigma * (1.0 + pre_gate * (1.0 - sigma))
    gate_side = (hidden_grad * pre_up * slope).astype(BF16)
    up_side = (hidden_grad * activated).astype(BF16)
    sides_ref[:, :width] = gate_side
    sides_ref[:, width : 2 * width] = up_side
    sides_ref[:, 2 * width :] = (activated * pre_up).astype(BF16)
    across = ((1,), (1,))
    at = iota((SPLIT * rows, 1), 0)
    k, group, row = at // rows, lax.rem(at, rows) // (rows // GROUPS), lax.rem(at, rows // GROUPS)
    order = one_hot((group * SPLIT + k) * (rows // GROUPS) + row, SPLIT * rows)
    gate_side, up_side = dot(order, gate_side).astype(BF16), dot(order, up_side).astype(BF16)
    part = (dot(gate_side, gate_ref[...], across) + dot(up_side, up_ref[...], across)).astype(BF16)
    for k in range(SPLIT):
        parts[k][...] = part[k * rows : (k + 1) * rows]


def grads_kernel(*refs):
    xs, ss = refs[:GROUPS], refs[GROUPS : 2 * GROUPS]
    sides_ref, outs, token_ref = refs[2 * GROUPS], refs[2 * GROUPS + 1 : -5], refs[-5]
    held, sems = refs[-4:-1], refs[-1]
    half, width = held[0].shape
    block = half // CHUNKS
    first = ((0,), (0,))
    copies = []
    for c in range(CHUNKS):
        part = slice(c * block, (c + 1) * block)
        x = jnp.concatenate([ref[:, part] for ref in xs], axis=0)
        s = jnp.concatenate([ref[:, part] for ref in ss], axis=0)
        for i, rows in enumerate((x, x, s)):
            held[i][part, :] = dot(rows, sides_ref[:, i * width : (i + 1) * width], first).astype(BF16)
            copy = pltpu.make_async_copy(
                held[i].at[pl.ds(c * block, block)], outs[i].at[pl.ds(c * block, block)], sems.at[i, c]
            )
            copy.start()
            copies.append(copy)
    for copy in copies:
        copy.wait()
    token_ref[...] = jnp.zeros(token_ref.shape, F32)


def sum_kernel(live, *refs):
    parts, outs = refs[:SPLIT], refs[SPLIT + 1 :]
    total = parts[0][...].astype(F32)
    for part in parts[1:]:
        total = total + part[...].astype(F32)
    total = total.astype(BF16)
    rows, half = total.shape
    fold = half // FOLDS
    each = CORES * MOST
    size = FOLDS * each
    row = iota((live * size, 1), 0)
    d, part, at = row // size, lax.rem(row // each, FOLDS), lax.rem(row, each)
    moved = jnp.zeros((live * size, fold), F32)
    for f in range(FOLDS):
        pick = one_hot(jnp.where(part == f, d * each + at, -1), rows)
        moved = moved + dot(pick, total[:, f * fold : (f + 1) * fold])
    for d in range(live):
        outs[d][...] = moved[d * size : (d + 1) * size].astype(BF16)


def split_kernel(live, *refs):
    chunks, outs = refs[:live], refs[live:]
    me = lax.axis_index("dp")
    size, fold = chunks[0].shape
    stacked = jnp.concatenate([chunk[...].astype(F32) for chunk in chunks], axis=0).astype(BF16)
    rows = live * 8
    out = iota((CORES * rows, 1), 0)
    q, d, slot = out // rows, lax.rem(out, rows) // 8, lax.rem(out, 8)
    for f in range(FOLDS):
        wanted = d * size + (f * CORES + (q ^ me)) * MOST + slot
        picked = dot(one_hot(jnp.where(slot < MOST, wanted, -1), live * size), stacked).astype(BF16)
        for core in range(CORES):
            outs[core][:, f * fold : (f + 1) * fold] = picked[core * rows : (core + 1) * rows]


def place_kernel(hot_ref, mine_ref, other_ref, out_ref):
    me = lax.axis_index("dp")
    half = mine_ref.shape[1]
    hot = hot_ref[...].astype(BF16)
    for q, ref in enumerate((mine_ref, other_ref)):
        columns = pl.ds(pl.multiple_of((me ^ q) * half, 128), half)
        out_ref[:, columns] = dot(hot, ref[...], ((0,), (0,))).astype(BF16)


def like(shape, dtype):
    return jax.ShapeDtypeStruct(shape, dtype)


def body(
    layer_input, out_grad, routes, gate_values, keep_mask, gate_weight, up_weight, down_transposed
):
    devices = lax.axis_size("expert")
    live = devices // SPLIT
    tokens, model = layer_input.shape
    half, width = gate_weight.shape
    fold = half // FOLDS
    rows = CORES * live * MOST
    total = SPLIT * rows
    vmem, hbm = pl.BlockSpec(memory_space=pltpu.VMEM), pl.BlockSpec(memory_space=pltpu.HBM)

    def call(kernel, name, out_shape, operands, flops=0, moved=0):
        return pl.pallas_call(
            kernel,
            out_shape=out_shape,
            in_specs=[vmem] * len(operands),
            out_specs=jax.tree.map(lambda _: vmem, out_shape),
            compiler_params=params(),
            cost_estimate=cost(flops, moved) if flops else None,
            name=name,
        )(*operands)

    def swap_cores(array):
        return lax.ppermute(array, "dp", [(r, r ^ 1) for r in range(CORES)])

    def along_z(array, d):
        hop = [(i, (i // SPLIT ^ d) * SPLIT + i % SPLIT) for i in range(devices)]
        return lax.ppermute(array, "expert", hop)

    def in_plane(array, k):
        hop = [(i, i // SPLIT * SPLIT + (i % SPLIT ^ k)) for i in range(devices)]
        return lax.ppermute(array, "expert", hop)

    gathered = like((live * SIDES * MOST, half), BF16)
    mine, other, hot = pl.pallas_call(
        lambda *refs: gather_kernel(live, *refs),
        out_shape=[gathered, gathered, like((live * 8, tokens), F32)],
        in_specs=[hbm] * 5,
        out_specs=[vmem] * 3,
        scratch_shapes=[
            pltpu.VMEM((TOP, tokens), jnp.int32),
            pltpu.VMEM((TOP, tokens), jnp.int32),
            pltpu.VMEM((TOP, tokens), F32),
            pltpu.VMEM((tokens, model), BF16),
            pltpu.VMEM((tokens, model), BF16),
            pltpu.SemaphoreType.DMA((5,)),
        ],
        compiler_params=params(FIRST_MIB),
        name="gather_rows",
    )(routes.T, keep_mask.T, gate_values.T, layer_input, out_grad)
    chunks = call(
        lambda *refs: chunk_kernel(live, *refs),
        "chunk_rows",
        [like((FOLDS * CORES * SIDES * MOST, fold), BF16)] * live,
        [mine, swap_cores(other)],
        1e10,
        2e7,
    )
    chunks = [chunks[0]] + [along_z(chunks[d], d) for d in range(1, live)]
    mines, others, xs, ss = [], [], [], []
    rows_in_group, planes = total // GROUPS, live // GROUPS
    for group in reversed(range(GROUPS)):
        rows_here = call(
            merge_kernel,
            "merge_rows",
            like((SIDES * rows // GROUPS, half), BF16),
            chunks[group * planes : (group + 1) * planes],
            1e8,
            1e6,
        )
        by_x, by_y = in_plane(rows_here, 1), in_plane(rows_here, 2)
        across = in_plane(by_y, 1) if group % 2 else in_plane(by_x, 2)
        mine, x, s = call(
            partial_kernel,
            "partial_products",
            [like((rows_in_group, 3 * width), F32)] + [like((rows_in_group, half), BF16)] * SIDES,
            [rows_here, by_x, by_y, across, gate_weight, up_weight, down_transposed],
            6 * rows_in_group * half * width,
            6 * half * width,
        )
        mines.append(mine)
        others.append(swap_cores(mine))
        xs.append(x)
        ss.append(s)
    mines, others, xs, ss = mines[::-1], others[::-1], xs[::-1], ss[::-1]
    sided = call(
        sides_kernel,
        "sides_and_parts",
        [like((rows, half), BF16)] * SPLIT + [like((total, 3 * width), BF16)],
        [*mines, *others, gate_weight, up_weight],
        4 * total * half * width,
        4 * half * width,
    )
    parts, sides = sided[:SPLIT], sided[SPLIT]
    parts = [parts[0]] + [in_plane(parts[k], k) for k in range(1, SPLIT)]
    gate_grad, up_grad, down_grad, token = pl.pallas_call(
        grads_kernel,
        out_shape=[like((half, width), BF16)] * 3 + [like((8, 128), F32)],
        in_specs=[vmem] * (2 * GROUPS + 1),
        out_specs=[hbm] * 3 + [vmem],
        scratch_shapes=[pltpu.VMEM((half, width), BF16)] * 3 + [pltpu.SemaphoreType.DMA((3, CHUNKS))],
        compiler_params=params(),
        cost_estimate=cost(6 * total * half * width, 6 * half * width + 4 * total * half),
        name="weight_grads",
    )(*xs, *ss, sides)
    chunks = call(
        lambda *refs: sum_kernel(live, *refs),
        "sum_parts",
        [like((FOLDS * CORES * MOST, fold), BF16)] * live,
        [*parts, token],
    )
    chunks = [chunks[0]] + [along_z(chunks[d], d) for d in range(1, live)]
    back, over = call(
        lambda *refs: split_kernel(live, *refs),
        "split_rows",
        [like((live * 8, half), BF16)] * 2,
        chunks,
    )
    input_grad = call(
        place_kernel, "place_rows", like((tokens, model), BF16), [hot, back, swap_cores(over)]
    )
    return (input_grad, gate_grad, up_grad, down_grad)


def solution(mesh):
    return jax.shard_map(
        body,
        mesh=mesh,
        in_specs=(
            P(("expert", "dp"), None),
            P(("expert", "dp"), None),
            P(("expert", "dp"), None),
            P(("expert", "dp"), None),
            P(("expert", "dp"), None),
            P("dp", "expert"),
            P("dp", "expert"),
            P("dp", "expert"),
        ),
        out_specs=(
            P(("expert", "dp"), None),
            P("dp", "expert"),
            P("dp", "expert"),
            P("dp", "expert"),
        ),
        check_vma=False,
    )
```

```python
import jax
import jax.numpy as jnp
from jax import lax
from jax.experimental import pallas as pl
from jax.experimental.pallas import tpu as pltpu
from jax.sharding import PartitionSpec as P

SPLIT = 4
MOST = 5
TOP = 8
SIDES = 2
CORES = 2
GROUPS = 2
FOLDS = 2
FIRST_MIB = 60
CHUNKS = 7

F32 = jnp.float32
BF16 = jnp.bfloat16


def params(mib=16):
    return pltpu.CompilerParams(vmem_limit_bytes=int(mib * 1024 * 1024))


def cost(flops, moved):
    return pl.CostEstimate(flops=int(flops), bytes_accessed=int(moved), transcendentals=0)


def iota(shape, axis):
    return lax.broadcasted_iota(jnp.int32, shape, axis)


def dot(a, b, dims=((1,), (0,))):
    return lax.dot_general(a, b, (dims, ((), ())), preferred_element_type=F32)


def one_hot(wanted, columns):
    return (iota((wanted.shape[0], columns), 1) == wanted).astype(F32).astype(BF16)


def pick_rows(routes, keep, gates, expert, slot, valid):
    rows, tokens = expert.shape[0], routes.shape[1]
    chosen = jnp.zeros((rows, tokens), F32)
    gate = jnp.zeros((rows, tokens), F32)
    for k in range(routes.shape[0]):
        hit = (routes[k : k + 1, :] == expert) & (keep[k : k + 1, :] == 1)
        chosen = jnp.where(hit, 1.0, chosen)
        gate = jnp.where(hit, gates[k : k + 1, :], gate)
    upto = (iota((tokens, tokens), 0) <= iota((tokens, tokens), 1)).astype(F32).astype(BF16)
    rank = dot(chosen.astype(BF16), upto)
    hot = (chosen > 0.5) & (rank == (slot + 1).astype(F32)) & valid
    return hot, gate


def gather_kernel(live, *refs):
    sources, outs, local, sems = refs[:5], refs[5:8], refs[8:13], refs[13]
    copies = [pltpu.make_async_copy(sources[i], local[i], sems.at[i]) for i in range(5)]
    for copy in copies:
        copy.start()
    routes_ref, keep_ref, gates_ref, x_ref, o_ref = local
    place, me = lax.axis_index("expert") // SPLIT, lax.axis_index("dp")
    half = x_ref.shape[1] // CORES
    for copy in copies[:3]:
        copy.wait()
    routes, keep, gates = routes_ref[...], keep_ref[...], gates_ref[...]

    row = iota((live * 8, 1), 0)
    expert, slot = place ^ (row // 8), lax.rem(row, 8)
    hot, _ = pick_rows(routes, keep, gates, expert, slot, slot < MOST)
    outs[2][...] = hot.astype(F32)

    row = iota((live * SIDES * MOST, 1), 0)
    expert = place ^ (row // (SIDES * MOST))
    side, slot = lax.rem(row // MOST, SIDES), lax.rem(row, MOST)
    hot, gate = pick_rows(routes, keep, gates, expert, slot, row >= 0)
    hot_x = (hot & (side == 0)).astype(F32).astype(BF16)
    hot_s = hot & (side == 1)
    scale = jnp.sum(jnp.where(hot_s, gate, 0.0), axis=1, keepdims=True)
    hot_s = hot_s.astype(F32).astype(BF16)
    for copy in copies[3:]:
        copy.wait()
    for q in range(CORES):
        columns = pl.ds(pl.multiple_of((me ^ q) * half, 128), half)
        rows = dot(hot_x, x_ref[:, columns]) + scale * dot(hot_s, o_ref[:, columns])
        outs[q][...] = rows.astype(BF16)


def chunk_kernel(live, mine_ref, other_ref, *outs):
    me = lax.axis_index("dp")
    rows, half = mine_ref.shape
    fold = half // FOLDS
    each = SIDES * MOST
    stacked = jnp.concatenate([mine_ref[...], other_ref[...]], axis=0)
    size = FOLDS * CORES * each
    row = iota((live * size, 1), 0)
    d, part, at = row // size, lax.rem(row // (CORES * each), FOLDS), lax.rem(row, CORES * each)
    wanted = (at // each ^ me) * rows + d * each + lax.rem(at, each)
    total = jnp.zeros((live * size, fold), F32)
    for f in range(FOLDS):
        pick = one_hot(jnp.where(part == f, wanted, -1), CORES * rows)
        total = total + dot(pick, stacked[:, f * fold : (f + 1) * fold])
    total = total.astype(BF16)
    for d in range(live):
        outs[d][...] = total[d * size : (d + 1) * size]


def merge_kernel(*refs):
    chunks, out_ref = refs[:-1], refs[-1]
    size, fold = chunks[0].shape
    stacked = jnp.concatenate([chunk[...] for chunk in chunks], axis=0)
    rows = len(chunks) * CORES * MOST
    out = iota((SIDES * rows, 1), 0)
    side, at = out // rows, lax.rem(out, rows)
    d, replica, slot = at // (CORES * MOST), lax.rem(at // MOST, CORES), lax.rem(at, MOST)
    for f in range(FOLDS):
        wanted = d * size + ((f * CORES + replica) * SIDES + side) * MOST + slot
        picked = dot(one_hot(wanted, len(chunks) * size), stacked)
        out_ref[:, f * fold : (f + 1) * fold] = picked.astype(BF16)


def partial_kernel(*refs):
    blocks, (gate_ref, up_ref, down_ref, out_ref), sided = refs[:SPLIT], refs[SPLIT:-2], refs[-2:]
    each, width = blocks[0].shape[0], gate_ref.shape[1]
    rows = each // SIDES
    stacked = jnp.concatenate([block[...] for block in blocks], axis=0)
    at = iota((SPLIT * rows, 1), 0)
    for side in range(SIDES):
        wanted = at // rows * each + side * rows + lax.rem(at, rows)
        sided[side][...] = dot(one_hot(wanted, SPLIT * each), stacked).astype(BF16)
    out_ref[:, :width] = dot(sided[0][...], gate_ref[...])
    out_ref[:, width : 2 * width] = dot(sided[0][...], up_ref[...])
    out_ref[:, 2 * width :] = dot(sided[1][...], down_ref[...])


def sides_kernel(*refs):
    sums, (gate_ref, up_ref), outs = refs[: 2 * GROUPS], refs[2 * GROUPS : 2 * GROUPS + 2], refs[2 * GROUPS + 2 :]
    parts, sides_ref = outs[:SPLIT], outs[SPLIT]
    width = gate_ref.shape[1]
    rows = parts[0].shape[0]
    total = [sums[i][...] + sums[GROUPS + i][...] for i in range(GROUPS)]
    total = jnp.concatenate(total, axis=0)
    pre_gate, pre_up = total[:, :width], total[:, width : 2 * width]
    hidden_grad = total[:, 2 * width :]
    sigma = jax.nn.sigmoid(pre_gate)
    activated = pre_gate * sigma
    slope = sigma * (1.0 + pre_gate * (1.0 - sigma))
    gate_side = (hidden_grad * pre_up * slope).astype(BF16)
    up_side = (hidden_grad * activated).astype(BF16)
    sides_ref[:, :width] = gate_side
    sides_ref[:, width : 2 * width] = up_side
    sides_ref[:, 2 * width :] = (activated * pre_up).astype(BF16)
    across = ((1,), (1,))
    at = iota((SPLIT * rows, 1), 0)
    k, group, row = at // rows, lax.rem(at, rows) // (rows // GROUPS), lax.rem(at, rows // GROUPS)
    order = one_hot(((GROUPS - 1 - group) * SPLIT + k) * (rows // GROUPS) + row, SPLIT * rows)
    gate_side, up_side = dot(order, gate_side).astype(BF16), dot(order, up_side).astype(BF16)
    part = (dot(gate_side, gate_ref[...], across) + dot(up_side, up_ref[...], across)).astype(BF16)
    for k in range(SPLIT):
        parts[k][...] = part[k * rows : (k + 1) * rows]


def grads_kernel(*refs):
    xs, ss = refs[:GROUPS], refs[GROUPS : 2 * GROUPS]
    sides_ref, outs, token_ref = refs[2 * GROUPS], refs[2 * GROUPS + 1 : -5], refs[-5]
    held, sems = refs[-4:-1], refs[-1]
    half, width = held[0].shape
    block = half // CHUNKS
    first = ((0,), (0,))
    copies = []
    for c in range(CHUNKS):
        part = slice(c * block, (c + 1) * block)
        x = jnp.concatenate([ref[:, part] for ref in xs], axis=0)
        s = jnp.concatenate([ref[:, part] for ref in ss], axis=0)
        for i, rows in enumerate((x, x, s)):
            held[i][part, :] = dot(rows, sides_ref[:, i * width : (i + 1) * width], first).astype(BF16)
            copy = pltpu.make_async_copy(
                held[i].at[pl.ds(c * block, block)], outs[i].at[pl.ds(c * block, block)], sems.at[i, c]
            )
            copy.start()
            copies.append(copy)
    for copy in copies:
        copy.wait()
    token_ref[...] = jnp.zeros(token_ref.shape, F32)


def sum_kernel(live, *refs):
    parts, outs = refs[:SPLIT], refs[SPLIT + 1 :]
    total = parts[0][...].astype(F32)
    for part in parts[1:]:
        total = total + part[...].astype(F32)
    total = total.astype(BF16)
    rows, half = total.shape
    fold = half // FOLDS
    each = CORES * MOST
    size = FOLDS * each
    row = iota((live * size, 1), 0)
    d, part, at = row // size, lax.rem(row // each, FOLDS), lax.rem(row, each)
    moved = jnp.zeros((live * size, fold), F32)
    for f in range(FOLDS):
        pick = one_hot(jnp.where(part == f, d * each + at, -1), rows)
        moved = moved + dot(pick, total[:, f * fold : (f + 1) * fold])
    for d in range(live):
        outs[d][...] = moved[d * size : (d + 1) * size].astype(BF16)


def split_kernel(live, *refs):
    chunks, outs = refs[:live], refs[live:]
    me = lax.axis_index("dp")
    size, fold = chunks[0].shape
    stacked = jnp.concatenate([chunk[...].astype(F32) for chunk in chunks], axis=0).astype(BF16)
    rows = live * 8
    out = iota((CORES * rows, 1), 0)
    q, d, slot = out // rows, lax.rem(out, rows) // 8, lax.rem(out, 8)
    for f in range(FOLDS):
        wanted = d * size + (f * CORES + (q ^ me)) * MOST + slot
        picked = dot(one_hot(jnp.where(slot < MOST, wanted, -1), live * size), stacked).astype(BF16)
        for core in range(CORES):
            outs[core][:, f * fold : (f + 1) * fold] = picked[core * rows : (core + 1) * rows]


def place_kernel(hot_ref, mine_ref, other_ref, out_ref):
    me = lax.axis_index("dp")
    half = mine_ref.shape[1]
    hot = hot_ref[...].astype(BF16)
    for q, ref in enumerate((mine_ref, other_ref)):
        columns = pl.ds(pl.multiple_of((me ^ q) * half, 128), half)
        out_ref[:, columns] = dot(hot, ref[...], ((0,), (0,))).astype(BF16)


def like(shape, dtype):
    return jax.ShapeDtypeStruct(shape, dtype)


def body(
    layer_input, out_grad, routes, gate_values, keep_mask, gate_weight, up_weight, down_transposed
):
    devices = lax.axis_size("expert")
    live = devices // SPLIT
    tokens, model = layer_input.shape
    half, width = gate_weight.shape
    fold = half // FOLDS
    rows = CORES * live * MOST
    total = SPLIT * rows
    vmem, hbm = pl.BlockSpec(memory_space=pltpu.VMEM), pl.BlockSpec(memory_space=pltpu.HBM)

    def call(kernel, name, out_shape, operands, flops=0, moved=0):
        return pl.pallas_call(
            kernel,
            out_shape=out_shape,
            in_specs=[vmem] * len(operands),
            out_specs=jax.tree.map(lambda _: vmem, out_shape),
            compiler_params=params(),
            cost_estimate=cost(flops, moved) if flops else None,
            name=name,
        )(*operands)

    def swap_cores(array):
        return lax.ppermute(array, "dp", [(r, r ^ 1) for r in range(CORES)])

    def along_z(array, d):
        hop = [(i, (i // SPLIT ^ d) * SPLIT + i % SPLIT) for i in range(devices)]
        return lax.ppermute(array, "expert", hop)

    def in_plane(array, k):
        hop = [(i, i // SPLIT * SPLIT + (i % SPLIT ^ k)) for i in range(devices)]
        return lax.ppermute(array, "expert", hop)

    gathered = like((live * SIDES * MOST, half), BF16)
    mine, other, hot = pl.pallas_call(
        lambda *refs: gather_kernel(live, *refs),
        out_shape=[gathered, gathered, like((live * 8, tokens), F32)],
        in_specs=[hbm] * 5,
        out_specs=[vmem] * 3,
        scratch_shapes=[
            pltpu.VMEM((TOP, tokens), jnp.int32),
            pltpu.VMEM((TOP, tokens), jnp.int32),
            pltpu.VMEM((TOP, tokens), F32),
            pltpu.VMEM((tokens, model), BF16),
            pltpu.VMEM((tokens, model), BF16),
            pltpu.SemaphoreType.DMA((5,)),
        ],
        compiler_params=params(FIRST_MIB),
        name="gather_rows",
    )(routes.T, keep_mask.T, gate_values.T, layer_input, out_grad)
    chunks = call(
        lambda *refs: chunk_kernel(live, *refs),
        "chunk_rows",
        [like((FOLDS * CORES * SIDES * MOST, fold), BF16)] * live,
        [mine, swap_cores(other)],
        1e10,
        2e7,
    )
    chunks = [chunks[0]] + [along_z(chunks[d], d) for d in range(1, live)]
    mines, others, xs, ss = [], [], [], []
    rows_in_group, planes = total // GROUPS, live // GROUPS
    for group in reversed(range(GROUPS)):
        rows_here = call(
            merge_kernel,
            "merge_rows",
            like((SIDES * rows // GROUPS, half), BF16),
            chunks[group * planes : (group + 1) * planes],
            1e8,
            1e6,
        )
        by_x, by_y = in_plane(rows_here, 1), in_plane(rows_here, 2)
        across = in_plane(by_y, 1) if group % 2 else in_plane(by_x, 2)
        mine, x, s = call(
            partial_kernel,
            "partial_products",
            [like((rows_in_group, 3 * width), F32)] + [like((rows_in_group, half), BF16)] * SIDES,
            [rows_here, by_x, by_y, across, gate_weight, up_weight, down_transposed],
            6 * rows_in_group * half * width,
            6 * half * width,
        )
        mines.append(mine)
        others.append(swap_cores(mine))
        xs.append(x)
        ss.append(s)
    sided = call(
        sides_kernel,
        "sides_and_parts",
        [like((rows, half), BF16)] * SPLIT + [like((total, 3 * width), BF16)],
        [*mines, *others, gate_weight, up_weight],
        4 * total * half * width,
        4 * half * width,
    )
    parts, sides = sided[:SPLIT], sided[SPLIT]
    parts = [parts[0]] + [in_plane(parts[k], k) for k in range(1, SPLIT)]
    gate_grad, up_grad, down_grad, token = pl.pallas_call(
        grads_kernel,
        out_shape=[like((half, width), BF16)] * 3 + [like((8, 128), F32)],
        in_specs=[vmem] * (2 * GROUPS + 1),
        out_specs=[hbm] * 3 + [vmem],
        scratch_shapes=[pltpu.VMEM((half, width), BF16)] * 3 + [pltpu.SemaphoreType.DMA((3, CHUNKS))],
        compiler_params=params(),
        cost_estimate=cost(6 * total * half * width, 6 * half * width + 4 * total * half),
        name="weight_grads",
    )(*xs, *ss, sides)
    chunks = call(
        lambda *refs: sum_kernel(live, *refs),
        "sum_parts",
        [like((FOLDS * CORES * MOST, fold), BF16)] * live,
        [*parts, token],
    )
    chunks = [chunks[0]] + [along_z(chunks[d], d) for d in range(1, live)]
    back, over = call(
        lambda *refs: split_kernel(live, *refs),
        "split_rows",
        [like((live * 8, half), BF16)] * 2,
        chunks,
    )
    input_grad = call(
        place_kernel, "place_rows", like((tokens, model), BF16), [hot, back, swap_cores(over)]
    )
    return (input_grad, gate_grad, up_grad, down_grad)


def solution(mesh):
    return jax.shard_map(
        body,
        mesh=mesh,
        in_specs=(
            P(("expert", "dp"), None),
            P(("expert", "dp"), None),
            P(("expert", "dp"), None),
            P(("expert", "dp"), None),
            P(("expert", "dp"), None),
            P("dp", "expert"),
            P("dp", "expert"),
            P("dp", "expert"),
        ),
        out_specs=(
            P(("expert", "dp"), None),
            P("dp", "expert"),
            P("dp", "expert"),
            P("dp", "expert"),
        ),
        check_vma=False,
    )
```

```python
import jax
import jax.numpy as jnp
from jax import lax
from jax.experimental import pallas as pl
from jax.experimental.pallas import tpu as pltpu
from jax.sharding import PartitionSpec as P

SPLIT = 4
MOST = 5
TOP = 8
SIDES = 2
CORES = 2
GROUPS = 2
FOLDS = 2
FIRST_MIB = 60
CHUNKS = 7

F32 = jnp.float32
BF16 = jnp.bfloat16


def params(mib=16):
    return pltpu.CompilerParams(vmem_limit_bytes=int(mib * 1024 * 1024))


def cost(flops, moved):
    return pl.CostEstimate(flops=int(flops), bytes_accessed=int(moved), transcendentals=0)


def iota(shape, axis):
    return lax.broadcasted_iota(jnp.int32, shape, axis)


def dot(a, b, dims=((1,), (0,))):
    return lax.dot_general(a, b, (dims, ((), ())), preferred_element_type=F32)


def one_hot(wanted, columns):
    return (iota((wanted.shape[0], columns), 1) == wanted).astype(F32).astype(BF16)


def pick_rows(routes, keep, gates, expert, slot, valid):
    rows, tokens = expert.shape[0], routes.shape[1]
    chosen = jnp.zeros((rows, tokens), F32)
    gate = jnp.zeros((rows, tokens), F32)
    for k in range(routes.shape[0]):
        hit = (routes[k : k + 1, :] == expert) & (keep[k : k + 1, :] == 1)
        chosen = jnp.where(hit, 1.0, chosen)
        gate = jnp.where(hit, gates[k : k + 1, :], gate)
    upto = (iota((tokens, tokens), 0) <= iota((tokens, tokens), 1)).astype(F32).astype(BF16)
    rank = dot(chosen.astype(BF16), upto)
    hot = (chosen > 0.5) & (rank == (slot + 1).astype(F32)) & valid
    return hot, gate


def near(k, core):
    if isinstance(core, int):
        return 3 - k if core and k in (1, 2) else k
    return jnp.where((core == 1) & (k > 0) & (k < 3), 3 - k, k)


def gather_kernel(live, *refs):
    sources, outs, local, sems = refs[:5], refs[5:8], refs[8:13], refs[13]
    copies = [pltpu.make_async_copy(sources[i], local[i], sems.at[i]) for i in range(5)]
    for copy in copies:
        copy.start()
    routes_ref, keep_ref, gates_ref, x_ref, o_ref = local
    place, me = lax.axis_index("expert") // SPLIT, lax.axis_index("dp")
    half = x_ref.shape[1] // CORES
    for copy in copies[:3]:
        copy.wait()
    routes, keep, gates = routes_ref[...], keep_ref[...], gates_ref[...]

    row = iota((live * 8, 1), 0)
    expert, slot = place ^ (row // 8), lax.rem(row, 8)
    hot, _ = pick_rows(routes, keep, gates, expert, slot, slot < MOST)
    outs[2][...] = hot.astype(F32)

    row = iota((live * SIDES * MOST, 1), 0)
    expert = place ^ (row // (SIDES * MOST))
    side, slot = lax.rem(row // MOST, SIDES), lax.rem(row, MOST)
    hot, gate = pick_rows(routes, keep, gates, expert, slot, row >= 0)
    hot_x = (hot & (side == 0)).astype(F32).astype(BF16)
    hot_s = hot & (side == 1)
    scale = jnp.sum(jnp.where(hot_s, gate, 0.0), axis=1, keepdims=True)
    hot_s = hot_s.astype(F32).astype(BF16)
    for copy in copies[3:]:
        copy.wait()
    for q in range(CORES):
        columns = pl.ds(pl.multiple_of((me ^ q) * half, 128), half)
        rows = dot(hot_x, x_ref[:, columns]) + scale * dot(hot_s, o_ref[:, columns])
        outs[q][...] = rows.astype(BF16)


def chunk_kernel(live, mine_ref, other_ref, *outs):
    me = lax.axis_index("dp")
    rows, half = mine_ref.shape
    fold = half // FOLDS
    each = SIDES * MOST
    stacked = jnp.concatenate([mine_ref[...], other_ref[...]], axis=0)
    size = FOLDS * CORES * each
    row = iota((live * size, 1), 0)
    d, part, at = row // size, lax.rem(row // (CORES * each), FOLDS), lax.rem(row, CORES * each)
    wanted = (at // each ^ me) * rows + d * each + lax.rem(at, each)
    total = jnp.zeros((live * size, fold), F32)
    for f in range(FOLDS):
        pick = one_hot(jnp.where(part == f, wanted, -1), CORES * rows)
        total = total + dot(pick, stacked[:, f * fold : (f + 1) * fold])
    total = total.astype(BF16)
    for d in range(live):
        outs[d][...] = total[d * size : (d + 1) * size]


def merge_kernel(*refs):
    chunks, out_ref = refs[:-1], refs[-1]
    size, fold = chunks[0].shape
    stacked = jnp.concatenate([chunk[...] for chunk in chunks], axis=0)
    rows = len(chunks) * CORES * MOST
    out = iota((SIDES * rows, 1), 0)
    side, at = out // rows, lax.rem(out, rows)
    d, replica, slot = at // (CORES * MOST), lax.rem(at // MOST, CORES), lax.rem(at, MOST)
    for f in range(FOLDS):
        wanted = d * size + ((f * CORES + replica) * SIDES + side) * MOST + slot
        picked = dot(one_hot(wanted, len(chunks) * size), stacked)
        out_ref[:, f * fold : (f + 1) * fold] = picked.astype(BF16)


def partial_kernel(*refs):
    blocks, (gate_ref, up_ref, down_ref, out_ref), sided = refs[:SPLIT], refs[SPLIT:-2], refs[-2:]
    each, width = blocks[0].shape[0], gate_ref.shape[1]
    rows = each // SIDES
    stacked = jnp.concatenate([block[...] for block in blocks], axis=0)
    at = iota((SPLIT * rows, 1), 0)
    block = near(at // rows, lax.axis_index("dp"))
    for side in range(SIDES):
        wanted = block * each + side * rows + lax.rem(at, rows)
        sided[side][...] = dot(one_hot(wanted, SPLIT * each), stacked).astype(BF16)
    out_ref[:, :width] = dot(sided[0][...], gate_ref[...])
    out_ref[:, width : 2 * width] = dot(sided[0][...], up_ref[...])
    out_ref[:, 2 * width :] = dot(sided[1][...], down_ref[...])


def sides_kernel(*refs):
    sums, (gate_ref, up_ref), outs = refs[: 2 * GROUPS], refs[2 * GROUPS : 2 * GROUPS + 2], refs[2 * GROUPS + 2 :]
    parts, sides_ref = outs[:SPLIT], outs[SPLIT]
    width = gate_ref.shape[1]
    rows = parts[0].shape[0]
    total = [sums[i][...] + sums[GROUPS + i][...] for i in range(GROUPS)]
    total = jnp.concatenate(total, axis=0)
    pre_gate, pre_up = total[:, :width], total[:, width : 2 * width]
    hidden_grad = total[:, 2 * width :]
    sigma = jax.nn.sigmoid(pre_gate)
    activated = pre_gate * sigma
    slope = sigma * (1.0 + pre_gate * (1.0 - sigma))
    gate_side = (hidden_grad * pre_up * slope).astype(BF16)
    up_side = (hidden_grad * activated).astype(BF16)
    sides_ref[:, :width] = gate_side
    sides_ref[:, width : 2 * width] = up_side
    sides_ref[:, 2 * width :] = (activated * pre_up).astype(BF16)
    across = ((1,), (1,))
    at = iota((SPLIT * rows, 1), 0)
    k = near(at // rows, lax.axis_index("dp"))
    group, row = lax.rem(at, rows) // (rows // GROUPS), lax.rem(at, rows // GROUPS)
    order = one_hot(((GROUPS - 1 - group) * SPLIT + k) * (rows // GROUPS) + row, SPLIT * rows)
    gate_side, up_side = dot(order, gate_side).astype(BF16), dot(order, up_side).astype(BF16)
    part = (dot(gate_side, gate_ref[...], across) + dot(up_side, up_ref[...], across)).astype(BF16)
    for k in range(SPLIT):
        parts[k][...] = part[k * rows : (k + 1) * rows]


def grads_kernel(*refs):
    xs, ss = refs[:GROUPS], refs[GROUPS : 2 * GROUPS]
    sides_ref, outs, token_ref = refs[2 * GROUPS], refs[2 * GROUPS + 1 : -5], refs[-5]
    held, sems = refs[-4:-1], refs[-1]
    half, width = held[0].shape
    block = half // CHUNKS
    first = ((0,), (0,))
    copies = []
    for c in range(CHUNKS):
        part = slice(c * block, (c + 1) * block)
        x = jnp.concatenate([ref[:, part] for ref in xs], axis=0)
        s = jnp.concatenate([ref[:, part] for ref in ss], axis=0)
        for i, rows in enumerate((x, x, s)):
            held[i][part, :] = dot(rows, sides_ref[:, i * width : (i + 1) * width], first).astype(BF16)
            copy = pltpu.make_async_copy(
                held[i].at[pl.ds(c * block, block)], outs[i].at[pl.ds(c * block, block)], sems.at[i, c]
            )
            copy.start()
            copies.append(copy)
    for copy in copies:
        copy.wait()
    token_ref[...] = jnp.zeros(token_ref.shape, F32)


def sum_kernel(live, *refs):
    parts, outs = refs[:SPLIT], refs[SPLIT + 1 :]
    total = parts[0][...].astype(F32)
    for part in parts[1:]:
        total = total + part[...].astype(F32)
    total = total.astype(BF16)
    rows, half = total.shape
    fold = half // FOLDS
    each = CORES * MOST
    size = FOLDS * each
    row = iota((live * size, 1), 0)
    d, part, at = row // size, lax.rem(row // each, FOLDS), lax.rem(row, each)
    moved = jnp.zeros((live * size, fold), F32)
    for f in range(FOLDS):
        pick = one_hot(jnp.where(part == f, d * each + at, -1), rows)
        moved = moved + dot(pick, total[:, f * fold : (f + 1) * fold])
    for d in range(live):
        outs[d][...] = moved[d * size : (d + 1) * size].astype(BF16)


def split_kernel(live, *refs):
    chunks, outs = refs[:live], refs[live:]
    me = lax.axis_index("dp")
    size, fold = chunks[0].shape
    stacked = jnp.concatenate([chunk[...].astype(F32) for chunk in chunks], axis=0).astype(BF16)
    rows = live * 8
    out = iota((CORES * rows, 1), 0)
    q, d, slot = out // rows, lax.rem(out, rows) // 8, lax.rem(out, 8)
    for f in range(FOLDS):
        wanted = d * size + (f * CORES + (q ^ me)) * MOST + slot
        picked = dot(one_hot(jnp.where(slot < MOST, wanted, -1), live * size), stacked).astype(BF16)
        for core in range(CORES):
            outs[core][:, f * fold : (f + 1) * fold] = picked[core * rows : (core + 1) * rows]


def place_kernel(hot_ref, mine_ref, other_ref, out_ref):
    me = lax.axis_index("dp")
    half = mine_ref.shape[1]
    hot = hot_ref[...].astype(BF16)
    for q, ref in enumerate((mine_ref, other_ref)):
        columns = pl.ds(pl.multiple_of((me ^ q) * half, 128), half)
        out_ref[:, columns] = dot(hot, ref[...], ((0,), (0,))).astype(BF16)


def like(shape, dtype):
    return jax.ShapeDtypeStruct(shape, dtype)


def body(
    layer_input, out_grad, routes, gate_values, keep_mask, gate_weight, up_weight, down_transposed
):
    devices = lax.axis_size("expert")
    live = devices // SPLIT
    tokens, model = layer_input.shape
    half, width = gate_weight.shape
    fold = half // FOLDS
    rows = CORES * live * MOST
    total = SPLIT * rows
    vmem, hbm = pl.BlockSpec(memory_space=pltpu.VMEM), pl.BlockSpec(memory_space=pltpu.HBM)

    def call(kernel, name, out_shape, operands, flops=0, moved=0):
        return pl.pallas_call(
            kernel,
            out_shape=out_shape,
            in_specs=[vmem] * len(operands),
            out_specs=jax.tree.map(lambda _: vmem, out_shape),
            compiler_params=params(),
            cost_estimate=cost(flops, moved) if flops else None,
            name=name,
        )(*operands)

    def swap_cores(array):
        return lax.ppermute(array, "dp", [(r, r ^ 1) for r in range(CORES)])

    def along_z(array, d):
        hop = [(i, (i // SPLIT ^ d) * SPLIT + i % SPLIT) for i in range(devices)]
        return lax.ppermute(array, "expert", hop)

    def in_plane(array, k):
        hop = []
        for i in range(devices):
            for r in range(CORES):
                hop.append((i * CORES + r, (i ^ near(k, r)) * CORES + r))
        return lax.ppermute(array, ("expert", "dp"), hop)

    gathered = like((live * SIDES * MOST, half), BF16)
    mine, other, hot = pl.pallas_call(
        lambda *refs: gather_kernel(live, *refs),
        out_shape=[gathered, gathered, like((live * 8, tokens), F32)],
        in_specs=[hbm] * 5,
        out_specs=[vmem] * 3,
        scratch_shapes=[
            pltpu.VMEM((TOP, tokens), jnp.int32),
            pltpu.VMEM((TOP, tokens), jnp.int32),
            pltpu.VMEM((TOP, tokens), F32),
            pltpu.VMEM((tokens, model), BF16),
            pltpu.VMEM((tokens, model), BF16),
            pltpu.SemaphoreType.DMA((5,)),
        ],
        compiler_params=params(FIRST_MIB),
        name="gather_rows",
    )(routes.T, keep_mask.T, gate_values.T, layer_input, out_grad)
    chunks = call(
        lambda *refs: chunk_kernel(live, *refs),
        "chunk_rows",
        [like((FOLDS * CORES * SIDES * MOST, fold), BF16)] * live,
        [mine, swap_cores(other)],
        1e10,
        2e7,
    )
    chunks = [chunks[0]] + [along_z(chunks[d], d) for d in range(1, live)]
    mines, others, xs, ss = [], [], [], []
    rows_in_group, planes = total // GROUPS, live // GROUPS
    for group in reversed(range(GROUPS)):
        rows_here = call(
            merge_kernel,
            "merge_rows",
            like((SIDES * rows // GROUPS, half), BF16),
            chunks[group * planes : (group + 1) * planes],
            1e8,
            1e6,
        )
        first, second = in_plane(rows_here, 1), in_plane(rows_here, 2)
        across = in_plane(first, 2)
        mine, x, s = call(
            partial_kernel,
            "partial_products",
            [like((rows_in_group, 3 * width), F32)] + [like((rows_in_group, half), BF16)] * SIDES,
            [rows_here, first, second, across, gate_weight, up_weight, down_transposed],
            6 * rows_in_group * half * width,
            6 * half * width,
        )
        mines.append(mine)
        others.append(swap_cores(mine))
        xs.append(x)
        ss.append(s)
    sided = call(
        sides_kernel,
        "sides_and_parts",
        [like((rows, half), BF16)] * SPLIT + [like((total, 3 * width), BF16)],
        [*mines, *others, gate_weight, up_weight],
        4 * total * half * width,
        4 * half * width,
    )
    parts, sides = sided[:SPLIT], sided[SPLIT]
    parts = [parts[0]] + [in_plane(parts[k], k) for k in range(1, SPLIT)]
    gate_grad, up_grad, down_grad, token = pl.pallas_call(
        grads_kernel,
        out_shape=[like((half, width), BF16)] * 3 + [like((8, 128), F32)],
        in_specs=[vmem] * (2 * GROUPS + 1),
        out_specs=[hbm] * 3 + [vmem],
        scratch_shapes=[pltpu.VMEM((half, width), BF16)] * 3 + [pltpu.SemaphoreType.DMA((3, CHUNKS))],
        compiler_params=params(),
        cost_estimate=cost(6 * total * half * width, 6 * half * width + 4 * total * half),
        name="weight_grads",
    )(*xs, *ss, sides)
    chunks = call(
        lambda *refs: sum_kernel(live, *refs),
        "sum_parts",
        [like((FOLDS * CORES * MOST, fold), BF16)] * live,
        [*parts, token],
    )
    chunks = [chunks[0]] + [along_z(chunks[d], d) for d in range(1, live)]
    back, over = call(
        lambda *refs: split_kernel(live, *refs),
        "split_rows",
        [like((live * 8, half), BF16)] * 2,
        chunks,
    )
    input_grad = call(
        place_kernel, "place_rows", like((tokens, model), BF16), [hot, back, swap_cores(over)]
    )
    return (input_grad, gate_grad, up_grad, down_grad)


def solution(mesh):
    return jax.shard_map(
        body,
        mesh=mesh,
        in_specs=(
            P(("expert", "dp"), None),
            P(("expert", "dp"), None),
            P(("expert", "dp"), None),
            P(("expert", "dp"), None),
            P(("expert", "dp"), None),
            P("dp", "expert"),
            P("dp", "expert"),
            P("dp", "expert"),
        ),
        out_specs=(
            P(("expert", "dp"), None),
            P("dp", "expert"),
            P("dp", "expert"),
            P("dp", "expert"),
        ),
        check_vma=False,
    )
```

```python
import functools

import jax
import jax.numpy as jnp
from jax import lax
from jax.experimental import pallas as pl
from jax.experimental.pallas import tpu as pltpu
from jax.sharding import PartitionSpec as P

SPLIT = 4
MOST = 5
TOP = 8
SIDES = 2
CORES = 2
GROUPS = 2
FIRST_BLOCKS = 3
FOLDS = 2
FIRST_MIB = 60
CHUNKS = 7

F32 = jnp.float32
BF16 = jnp.bfloat16


def params(mib=16):
    return pltpu.CompilerParams(vmem_limit_bytes=int(mib * 1024 * 1024))


def cost(flops, moved):
    return pl.CostEstimate(flops=int(flops), bytes_accessed=int(moved), transcendentals=0)


def iota(shape, axis):
    return lax.broadcasted_iota(jnp.int32, shape, axis)


def dot(a, b, dims=((1,), (0,))):
    return lax.dot_general(a, b, (dims, ((), ())), preferred_element_type=F32)


def one_hot(wanted, columns):
    return (iota((wanted.shape[0], columns), 1) == wanted).astype(F32).astype(BF16)


def pick_rows(routes, keep, gates, expert, slot, valid):
    rows, tokens = expert.shape[0], routes.shape[1]
    chosen = jnp.zeros((rows, tokens), F32)
    gate = jnp.zeros((rows, tokens), F32)
    for k in range(routes.shape[0]):
        hit = (routes[k : k + 1, :] == expert) & (keep[k : k + 1, :] == 1)
        chosen = jnp.where(hit, 1.0, chosen)
        gate = jnp.where(hit, gates[k : k + 1, :], gate)
    upto = (iota((tokens, tokens), 0) <= iota((tokens, tokens), 1)).astype(F32).astype(BF16)
    rank = dot(chosen.astype(BF16), upto)
    hot = (chosen > 0.5) & (rank == (slot + 1).astype(F32)) & valid
    return hot, gate


def hop(d, live):
    return (live - d) % live if isinstance(d, int) else lax.rem(live - d, live)


def near(k, core):
    if isinstance(core, int):
        return 3 - k if core and k in (1, 2) else k
    return jnp.where((core == 1) & (k > 0) & (k < 3), 3 - k, k)


def gather_kernel(live, *refs):
    sources, outs, local, sems = refs[:5], refs[5:8], refs[8:13], refs[13]
    copies = [pltpu.make_async_copy(sources[i], local[i], sems.at[i]) for i in range(5)]
    for copy in copies:
        copy.start()
    routes_ref, keep_ref, gates_ref, x_ref, o_ref = local
    place, me = lax.axis_index("expert") // SPLIT, lax.axis_index("dp")
    half = x_ref.shape[1] // CORES
    for copy in copies[:3]:
        copy.wait()
    routes, keep, gates = routes_ref[...], keep_ref[...], gates_ref[...]

    row = iota((live * 8, 1), 0)
    expert, slot = place ^ hop(row // 8, live), lax.rem(row, 8)
    hot, _ = pick_rows(routes, keep, gates, expert, slot, slot < MOST)
    outs[2][...] = hot.astype(F32)

    row = iota((live * SIDES * MOST, 1), 0)
    expert = place ^ hop(row // (SIDES * MOST), live)
    side, slot = lax.rem(row // MOST, SIDES), lax.rem(row, MOST)
    hot, gate = pick_rows(routes, keep, gates, expert, slot, row >= 0)
    hot_x = (hot & (side == 0)).astype(F32).astype(BF16)
    hot_s = hot & (side == 1)
    scale = jnp.sum(jnp.where(hot_s, gate, 0.0), axis=1, keepdims=True)
    hot_s = hot_s.astype(F32).astype(BF16)
    for copy in copies[3:]:
        copy.wait()
    for q in range(CORES):
        columns = pl.ds(pl.multiple_of((me ^ q) * half, 128), half)
        rows = dot(hot_x, x_ref[:, columns]) + scale * dot(hot_s, o_ref[:, columns])
        outs[q][...] = rows.astype(BF16)


def chunk_kernel(live, mine_ref, other_ref, *outs):
    me = lax.axis_index("dp")
    rows, half = mine_ref.shape
    fold = half // FOLDS
    each = SIDES * MOST
    stacked = jnp.concatenate([mine_ref[...], other_ref[...]], axis=0)
    size = FOLDS * CORES * each
    row = iota((live * size, 1), 0)
    d, part, at = row // size, lax.rem(row // (CORES * each), FOLDS), lax.rem(row, CORES * each)
    wanted = (at // each ^ me) * rows + d * each + lax.rem(at, each)
    total = jnp.zeros((live * size, fold), F32)
    for f in range(FOLDS):
        pick = one_hot(jnp.where(part == f, wanted, -1), CORES * rows)
        total = total + dot(pick, stacked[:, f * fold : (f + 1) * fold])
    total = total.astype(BF16)
    for d in range(live):
        outs[d][...] = total[d * size : (d + 1) * size]


def merge_kernel(*refs):
    chunks, out_ref = refs[:-1], refs[-1]
    size, fold = chunks[0].shape
    stacked = jnp.concatenate([chunk[...] for chunk in chunks], axis=0)
    rows = len(chunks) * CORES * MOST
    out = iota((SIDES * rows, 1), 0)
    side, at = out // rows, lax.rem(out, rows)
    d, replica, slot = at // (CORES * MOST), lax.rem(at // MOST, CORES), lax.rem(at, MOST)
    for f in range(FOLDS):
        wanted = d * size + ((f * CORES + replica) * SIDES + side) * MOST + slot
        picked = dot(one_hot(wanted, len(chunks) * size), stacked)
        out_ref[:, f * fold : (f + 1) * fold] = picked.astype(BF16)


def partial_kernel(swap, *refs):
    (gate_ref, up_ref, down_ref, out_ref), sided = refs[-6:-2], refs[-2:]
    blocks = [ref[...] for ref in refs[:-6]]
    each, width = blocks[0].shape[0], gate_ref.shape[1]
    rows, count = each // SIDES, len(blocks)
    stacked = jnp.concatenate(blocks, axis=0)
    at = iota((count * rows, 1), 0)
    block = at // rows
    if swap:
        block = near(block, lax.axis_index("dp"))
    for side in range(SIDES):
        wanted = block * each + side * rows + lax.rem(at, rows)
        sided[side][...] = dot(one_hot(wanted, count * each), stacked).astype(BF16)
    out_ref[:, :width] = dot(sided[0][...], gate_ref[...])
    out_ref[:, width : 2 * width] = dot(sided[0][...], up_ref[...])
    out_ref[:, 2 * width :] = dot(sided[1][...], down_ref[...])


def sides_kernel(*refs):
    sums, (gate_ref, up_ref), outs = refs[: 2 * GROUPS], refs[2 * GROUPS : 2 * GROUPS + 2], refs[2 * GROUPS + 2 :]
    parts, sides_ref = outs[:SPLIT], outs[SPLIT]
    width = gate_ref.shape[1]
    rows = parts[0].shape[0]
    total = [sums[i][...] + sums[GROUPS + i][...] for i in range(GROUPS)]
    total = jnp.concatenate(total, axis=0)
    pre_gate, pre_up = total[:, :width], total[:, width : 2 * width]
    hidden_grad = total[:, 2 * width :]
    sigma = jax.nn.sigmoid(pre_gate)
    activated = pre_gate * sigma
    slope = sigma * (1.0 + pre_gate * (1.0 - sigma))
    gate_side = (hidden_grad * pre_up * slope).astype(BF16)
    up_side = (hidden_grad * activated).astype(BF16)
    sides_ref[:, :width] = gate_side
    sides_ref[:, width : 2 * width] = up_side
    sides_ref[:, 2 * width :] = (activated * pre_up).astype(BF16)
    across = ((1,), (1,))
    part = (dot(gate_side, gate_ref[...], across) + dot(up_side, up_ref[...], across)).astype(BF16)
    swapped = lax.axis_index("dp") == 1
    parts[0][...] = part[:rows]
    parts[1][...] = jnp.where(swapped, part[2 * rows : 3 * rows], part[rows : 2 * rows])
    parts[2][...] = jnp.where(swapped, part[rows : 2 * rows], part[2 * rows : 3 * rows])
    parts[3][...] = part[3 * rows :]


def grads_kernel(*refs):
    xs, ss = refs[:GROUPS], refs[GROUPS : 2 * GROUPS]
    sides_ref, outs, token_ref = refs[2 * GROUPS], refs[2 * GROUPS + 1 : -5], refs[-5]
    held, sems = refs[-4:-1], refs[-1]
    half, width = held[0].shape
    block = half // CHUNKS
    first = ((0,), (0,))
    copies = []
    for c in range(CHUNKS):
        part = slice(c * block, (c + 1) * block)
        x = jnp.concatenate([ref[:, part] for ref in xs], axis=0)
        s = jnp.concatenate([ref[:, part] for ref in ss], axis=0)
        for i, rows in enumerate((x, x, s)):
            held[i][part, :] = dot(rows, sides_ref[:, i * width : (i + 1) * width], first).astype(BF16)
            copy = pltpu.make_async_copy(
                held[i].at[pl.ds(c * block, block)], outs[i].at[pl.ds(c * block, block)], sems.at[i, c]
            )
            copy.start()
            copies.append(copy)
    for copy in copies:
        copy.wait()
    token_ref[...] = jnp.zeros(token_ref.shape, F32)


def sum_kernel(live, *refs):
    parts, outs = refs[:SPLIT], refs[SPLIT + 1 :]
    total = parts[0][...].astype(F32)
    for part in parts[1:]:
        total = total + part[...].astype(F32)
    total = total.astype(BF16)
    rows, half = total.shape
    fold = half // FOLDS
    each = CORES * MOST
    size = FOLDS * each
    row = iota((live * size, 1), 0)
    d, part, at = row // size, lax.rem(row // each, FOLDS), lax.rem(row, each)
    moved = jnp.zeros((live * size, fold), F32)
    for f in range(FOLDS):
        pick = one_hot(jnp.where(part == f, d * each + at, -1), rows)
        moved = moved + dot(pick, total[:, f * fold : (f + 1) * fold])
    for d in range(live):
        outs[d][...] = moved[d * size : (d + 1) * size].astype(BF16)


def split_kernel(live, *refs):
    chunks, outs = refs[:live], refs[live:]
    me = lax.axis_index("dp")
    size, fold = chunks[0].shape
    stacked = jnp.concatenate([chunk[...].astype(F32) for chunk in chunks], axis=0).astype(BF16)
    rows = live * 8
    out = iota((CORES * rows, 1), 0)
    q, d, slot = out // rows, lax.rem(out, rows) // 8, lax.rem(out, 8)
    for f in range(FOLDS):
        wanted = d * size + (f * CORES + (q ^ me)) * MOST + slot
        picked = dot(one_hot(jnp.where(slot < MOST, wanted, -1), live * size), stacked).astype(BF16)
        for core in range(CORES):
            outs[core][:, f * fold : (f + 1) * fold] = picked[core * rows : (core + 1) * rows]


def place_kernel(hot_ref, mine_ref, other_ref, out_ref):
    me = lax.axis_index("dp")
    half = mine_ref.shape[1]
    hot = hot_ref[...].astype(BF16)
    for q, ref in enumerate((mine_ref, other_ref)):
        columns = pl.ds(pl.multiple_of((me ^ q) * half, 128), half)
        out_ref[:, columns] = dot(hot, ref[...], ((0,), (0,))).astype(BF16)


def like(shape, dtype):
    return jax.ShapeDtypeStruct(shape, dtype)


def body(
    layer_input, out_grad, routes, gate_values, keep_mask, gate_weight, up_weight, down_transposed
):
    devices = lax.axis_size("expert")
    live = devices // SPLIT
    tokens, model = layer_input.shape
    half, width = gate_weight.shape
    fold = half // FOLDS
    rows = CORES * live * MOST
    total = SPLIT * rows
    vmem, hbm = pl.BlockSpec(memory_space=pltpu.VMEM), pl.BlockSpec(memory_space=pltpu.HBM)

    def call(kernel, name, out_shape, operands, flops=0, moved=0):
        return pl.pallas_call(
            kernel,
            out_shape=out_shape,
            in_specs=[vmem] * len(operands),
            out_specs=jax.tree.map(lambda _: vmem, out_shape),
            compiler_params=params(),
            cost_estimate=cost(flops, moved) if flops else None,
            name=name,
        )(*operands)

    def swap_cores(array):
        return lax.ppermute(array, "dp", [(r, r ^ 1) for r in range(CORES)])

    def along_z(array, d):
        moves = [(i, (i // SPLIT ^ hop(d, live)) * SPLIT + i % SPLIT) for i in range(devices)]
        return lax.ppermute(array, "expert", moves)

    def in_plane(array, k):
        moves = []
        for i in range(devices):
            for r in range(CORES):
                moves.append((i * CORES + r, (i ^ near(k, r)) * CORES + r))
        return lax.ppermute(array, ("expert", "dp"), moves)

    gathered = like((live * SIDES * MOST, half), BF16)
    mine, other, hot = pl.pallas_call(
        lambda *refs: gather_kernel(live, *refs),
        out_shape=[gathered, gathered, like((live * 8, tokens), F32)],
        in_specs=[hbm] * 5,
        out_specs=[vmem] * 3,
        scratch_shapes=[
            pltpu.VMEM((TOP, tokens), jnp.int32),
            pltpu.VMEM((TOP, tokens), jnp.int32),
            pltpu.VMEM((TOP, tokens), F32),
            pltpu.VMEM((tokens, model), BF16),
            pltpu.VMEM((tokens, model), BF16),
            pltpu.SemaphoreType.DMA((5,)),
        ],
        compiler_params=params(FIRST_MIB),
        name="gather_rows",
    )(routes.T, keep_mask.T, gate_values.T, layer_input, out_grad)
    chunks = call(
        lambda *refs: chunk_kernel(live, *refs),
        "chunk_rows",
        [like((FOLDS * CORES * SIDES * MOST, fold), BF16)] * live,
        [mine, swap_cores(other)],
        1e10,
        2e7,
    )
    chunks = [chunks[0]] + [along_z(chunks[d], d) for d in range(1, live)]
    own = call(merge_kernel, "merge_rows", like((SIDES * rows, half), BF16), chunks, 1e8, 1e6)
    first, second = in_plane(own, 1), in_plane(own, 2)
    blocks = [own, first, second, in_plane(first, 2)]
    mines, others, xs, ss = [], [], [], []
    for group in (blocks[:FIRST_BLOCKS], blocks[FIRST_BLOCKS:]):
        count = len(group) * rows
        mine, x, s = call(
            functools.partial(partial_kernel, len(group) == FIRST_BLOCKS),
            "partial_products",
            [like((count, 3 * width), F32)] + [like((count, half), BF16)] * SIDES,
            [*group, gate_weight, up_weight, down_transposed],
            (1 if len(group) == FIRST_BLOCKS else 16) * 6 * count * half * width,
            6 * half * width,
        )
        mines.append(mine)
        others.append(swap_cores(mine))
        xs.append(x)
        ss.append(s)
    sided = call(
        sides_kernel,
        "sides_and_parts",
        [like((rows, half), BF16)] * SPLIT + [like((total, 3 * width), BF16)],
        [*mines, *others, gate_weight, up_weight],
        4 * total * half * width,
        4 * half * width,
    )
    parts, sides = sided[:SPLIT], sided[SPLIT]
    parts = [parts[0]] + [in_plane(parts[k], k) for k in reversed(range(1, SPLIT))]
    gate_grad, up_grad, down_grad, token = pl.pallas_call(
        grads_kernel,
        out_shape=[like((half, width), BF16)] * 3 + [like((8, 128), F32)],
        in_specs=[vmem] * (2 * GROUPS + 1),
        out_specs=[hbm] * 3 + [vmem],
        scratch_shapes=[pltpu.VMEM((half, width), BF16)] * 3 + [pltpu.SemaphoreType.DMA((3, CHUNKS))],
        compiler_params=params(),
        cost_estimate=cost(6 * total * half * width, 6 * half * width + 4 * total * half),
        name="weight_grads",
    )(*xs, *ss, sides)
    chunks = call(
        lambda *refs: sum_kernel(live, *refs),
        "sum_parts",
        [like((FOLDS * CORES * MOST, fold), BF16)] * live,
        [*parts, token],
    )
    chunks = [chunks[0]] + [along_z(chunks[d], d) for d in range(1, live)]
    back, over = call(
        lambda *refs: split_kernel(live, *refs),
        "split_rows",
        [like((live * 8, half), BF16)] * 2,
        chunks,
    )
    input_grad = call(
        place_kernel, "place_rows", like((tokens, model), BF16), [hot, back, swap_cores(over)]
    )
    return (input_grad, gate_grad, up_grad, down_grad)


def solution(mesh):
    return jax.shard_map(
        body,
        mesh=mesh,
        in_specs=(
            P(("expert", "dp"), None),
            P(("expert", "dp"), None),
            P(("expert", "dp"), None),
            P(("expert", "dp"), None),
            P(("expert", "dp"), None),
            P("dp", "expert"),
            P("dp", "expert"),
            P("dp", "expert"),
        ),
        out_specs=(
            P(("expert", "dp"), None),
            P("dp", "expert"),
            P("dp", "expert"),
            P("dp", "expert"),
        ),
        check_vma=False,
    )
```

```python
import jax
import jax.numpy as jnp
from jax import lax
from jax.experimental import pallas as pl
from jax.experimental.pallas import tpu as pltpu
from jax.sharding import PartitionSpec as P

SPLIT = 4
MOST = 5
TOP = 8
SIDES = 2
CORES = 2
GROUPS = 2
FOLDS = 2
FIRST_MIB = 60
CHUNKS = 7

F32 = jnp.float32
BF16 = jnp.bfloat16


def params(mib=16):
    return pltpu.CompilerParams(vmem_limit_bytes=int(mib * 1024 * 1024))


def cost(flops, moved):
    return pl.CostEstimate(flops=int(flops), bytes_accessed=int(moved), transcendentals=0)


def iota(shape, axis):
    return lax.broadcasted_iota(jnp.int32, shape, axis)


def dot(a, b, dims=((1,), (0,))):
    return lax.dot_general(a, b, (dims, ((), ())), preferred_element_type=F32)


def one_hot(wanted, columns):
    return (iota((wanted.shape[0], columns), 1) == wanted).astype(F32).astype(BF16)


def pick_rows(routes, keep, gates, expert, slot, valid):
    rows, tokens = expert.shape[0], routes.shape[1]
    chosen = jnp.zeros((rows, tokens), F32)
    gate = jnp.zeros((rows, tokens), F32)
    for k in range(routes.shape[0]):
        hit = (routes[k : k + 1, :] == expert) & (keep[k : k + 1, :] == 1)
        chosen = jnp.where(hit, 1.0, chosen)
        gate = jnp.where(hit, gates[k : k + 1, :], gate)
    upto = (iota((tokens, tokens), 0) <= iota((tokens, tokens), 1)).astype(F32).astype(BF16)
    rank = dot(chosen.astype(BF16), upto)
    hot = (chosen > 0.5) & (rank == (slot + 1).astype(F32)) & valid
    return hot, gate


def near(k, core):
    if isinstance(core, int):
        return 3 - k if core and k in (1, 2) else k
    return jnp.where((core == 1) & (k > 0) & (k < 3), 3 - k, k)


def gather_kernel(live, *refs):
    sources, outs, local, sems = refs[:5], refs[5:8], refs[8:13], refs[13]
    copies = [pltpu.make_async_copy(sources[i], local[i], sems.at[i]) for i in range(5)]
    for copy in copies:
        copy.start()
    routes_ref, keep_ref, gates_ref, x_ref, o_ref = local
    place, me = lax.axis_index("expert") // SPLIT, lax.axis_index("dp")
    half = x_ref.shape[1] // CORES
    for copy in copies[:3]:
        copy.wait()
    routes, keep, gates = routes_ref[...], keep_ref[...], gates_ref[...]

    row = iota((live * 8, 1), 0)
    expert, slot = place ^ (row // 8), lax.rem(row, 8)
    hot, _ = pick_rows(routes, keep, gates, expert, slot, slot < MOST)
    outs[2][...] = hot.astype(F32)

    row = iota((live * SIDES * MOST, 1), 0)
    expert = place ^ (row // (SIDES * MOST))
    side, slot = lax.rem(row // MOST, SIDES), lax.rem(row, MOST)
    hot, gate = pick_rows(routes, keep, gates, expert, slot, row >= 0)
    hot_x = (hot & (side == 0)).astype(F32).astype(BF16)
    hot_s = hot & (side == 1)
    scale = jnp.sum(jnp.where(hot_s, gate, 0.0), axis=1, keepdims=True)
    hot_s = hot_s.astype(F32).astype(BF16)
    for copy in copies[3:]:
        copy.wait()
    for q in range(CORES):
        columns = pl.ds(pl.multiple_of((me ^ q) * half, 128), half)
        rows = dot(hot_x, x_ref[:, columns]) + scale * dot(hot_s, o_ref[:, columns])
        outs[q][...] = rows.astype(BF16)


def chunk_kernel(live, mine_ref, other_ref, *outs):
    me = lax.axis_index("dp")
    rows, half = mine_ref.shape
    fold = half // FOLDS
    each = SIDES * MOST
    stacked = jnp.concatenate([mine_ref[...], other_ref[...]], axis=0)
    size = FOLDS * CORES * each
    row = iota((live * size, 1), 0)
    d, part, at = row // size, lax.rem(row // (CORES * each), FOLDS), lax.rem(row, CORES * each)
    wanted = (at // each ^ me) * rows + d * each + lax.rem(at, each)
    total = jnp.zeros((live * size, fold), F32)
    for f in range(FOLDS):
        pick = one_hot(jnp.where(part == f, wanted, -1), CORES * rows)
        total = total + dot(pick, stacked[:, f * fold : (f + 1) * fold])
    total = total.astype(BF16)
    for d in range(live):
        outs[d][...] = total[d * size : (d + 1) * size]


def merge_kernel(*refs):
    chunks, out_ref = refs[:-1], refs[-1]
    size, fold = chunks[0].shape
    stacked = jnp.concatenate([chunk[...] for chunk in chunks], axis=0)
    rows = len(chunks) * CORES * MOST
    out = iota((SIDES * rows, 1), 0)
    side, at = out // rows, lax.rem(out, rows)
    d, replica, slot = at // (CORES * MOST), lax.rem(at // MOST, CORES), lax.rem(at, MOST)
    for f in range(FOLDS):
        wanted = d * size + ((f * CORES + replica) * SIDES + side) * MOST + slot
        picked = dot(one_hot(wanted, len(chunks) * size), stacked)
        out_ref[:, f * fold : (f + 1) * fold] = picked.astype(BF16)


def partial_kernel(*refs):
    blocks, (gate_ref, up_ref, down_ref, out_ref), sided = refs[:SPLIT], refs[SPLIT:-2], refs[-2:]
    each, width = blocks[0].shape[0], gate_ref.shape[1]
    rows = each // SIDES
    stacked = jnp.concatenate([block[...] for block in blocks], axis=0)
    at = iota((SPLIT * rows, 1), 0)
    block = near(at // rows, lax.axis_index("dp"))
    for side in range(SIDES):
        wanted = block * each + side * rows + lax.rem(at, rows)
        sided[side][...] = dot(one_hot(wanted, SPLIT * each), stacked).astype(BF16)
    out_ref[:, :width] = dot(sided[0][...], gate_ref[...])
    out_ref[:, width : 2 * width] = dot(sided[0][...], up_ref[...])
    out_ref[:, 2 * width :] = dot(sided[1][...], down_ref[...])


def sides_kernel(*refs):
    sums, (gate_ref, up_ref), outs = refs[: 2 * GROUPS], refs[2 * GROUPS : 2 * GROUPS + 2], refs[2 * GROUPS + 2 :]
    parts, sides_ref = outs[:SPLIT], outs[SPLIT]
    width = gate_ref.shape[1]
    rows = parts[0].shape[0]
    total = [sums[i][...] + sums[GROUPS + i][...] for i in range(GROUPS)]
    total = jnp.concatenate(total, axis=0)
    pre_gate, pre_up = total[:, :width], total[:, width : 2 * width]
    hidden_grad = total[:, 2 * width :]
    sigma = jax.nn.sigmoid(pre_gate)
    activated = pre_gate * sigma
    slope = sigma * (1.0 + pre_gate * (1.0 - sigma))
    gate_side = (hidden_grad * pre_up * slope).astype(BF16)
    up_side = (hidden_grad * activated).astype(BF16)
    sides_ref[:, :width] = gate_side
    sides_ref[:, width : 2 * width] = up_side
    sides_ref[:, 2 * width :] = (activated * pre_up).astype(BF16)
    across = ((1,), (1,))
    at = iota((SPLIT * rows, 1), 0)
    k = near(at // rows, lax.axis_index("dp"))
    group, row = lax.rem(at, rows) // (rows // GROUPS), lax.rem(at, rows // GROUPS)
    order = one_hot(((GROUPS - 1 - group) * SPLIT + k) * (rows // GROUPS) + row, SPLIT * rows)
    gate_side, up_side = dot(order, gate_side).astype(BF16), dot(order, up_side).astype(BF16)
    part = (dot(gate_side, gate_ref[...], across) + dot(up_side, up_ref[...], across)).astype(BF16)
    for k in range(SPLIT):
        parts[k][...] = part[k * rows : (k + 1) * rows]


def grads_kernel(*refs):
    xs, ss = refs[:GROUPS], refs[GROUPS : 2 * GROUPS]
    sides_ref, outs, token_ref = refs[2 * GROUPS], refs[2 * GROUPS + 1 : -5], refs[-5]
    held, sems = refs[-4:-1], refs[-1]
    half, width = held[0].shape
    block = half // CHUNKS
    first = ((0,), (0,))
    copies = []
    for c in range(CHUNKS):
        part = slice(c * block, (c + 1) * block)
        x = jnp.concatenate([ref[:, part] for ref in xs], axis=0)
        s = jnp.concatenate([ref[:, part] for ref in ss], axis=0)
        for i, rows in enumerate((x, x, s)):
            held[i][part, :] = dot(rows, sides_ref[:, i * width : (i + 1) * width], first).astype(BF16)
            copy = pltpu.make_async_copy(
                held[i].at[pl.ds(c * block, block)], outs[i].at[pl.ds(c * block, block)], sems.at[i, c]
            )
            copy.start()
            copies.append(copy)
    for copy in copies:
        copy.wait()
    token_ref[...] = jnp.zeros(token_ref.shape, F32)


def sum_kernel(live, *refs):
    parts, outs = refs[:SPLIT], refs[SPLIT + 1 :]
    total = parts[0][...].astype(F32)
    for part in parts[1:]:
        total = total + part[...].astype(F32)
    total = total.astype(BF16)
    rows, half = total.shape
    fold = half // FOLDS
    each = CORES * MOST
    size = FOLDS * each
    row = iota((live * size, 1), 0)
    d, part, at = row // size, lax.rem(row // each, FOLDS), lax.rem(row, each)
    moved = jnp.zeros((live * size, fold), F32)
    for f in range(FOLDS):
        pick = one_hot(jnp.where(part == f, d * each + at, -1), rows)
        moved = moved + dot(pick, total[:, f * fold : (f + 1) * fold])
    for d in range(live):
        outs[d][...] = moved[d * size : (d + 1) * size].astype(BF16)


def split_kernel(live, *refs):
    chunks, outs = refs[:live], refs[live:]
    me = lax.axis_index("dp")
    size, fold = chunks[0].shape
    stacked = jnp.concatenate([chunk[...].astype(F32) for chunk in chunks], axis=0).astype(BF16)
    rows = live * 8
    out = iota((CORES * rows, 1), 0)
    q, d, slot = out // rows, lax.rem(out, rows) // 8, lax.rem(out, 8)
    for f in range(FOLDS):
        wanted = lax.rem(live - d, live) * size + (f * CORES + (q ^ me)) * MOST + slot
        picked = dot(one_hot(jnp.where(slot < MOST, wanted, -1), live * size), stacked).astype(BF16)
        for core in range(CORES):
            outs[core][:, f * fold : (f + 1) * fold] = picked[core * rows : (core + 1) * rows]


def place_kernel(hot_ref, mine_ref, other_ref, out_ref):
    me = lax.axis_index("dp")
    half = mine_ref.shape[1]
    hot = hot_ref[...].astype(BF16)
    for q, ref in enumerate((mine_ref, other_ref)):
        columns = pl.ds(pl.multiple_of((me ^ q) * half, 128), half)
        out_ref[:, columns] = dot(hot, ref[...], ((0,), (0,))).astype(BF16)


def like(shape, dtype):
    return jax.ShapeDtypeStruct(shape, dtype)


def body(
    layer_input, out_grad, routes, gate_values, keep_mask, gate_weight, up_weight, down_transposed
):
    devices = lax.axis_size("expert")
    live = devices // SPLIT
    tokens, model = layer_input.shape
    half, width = gate_weight.shape
    fold = half // FOLDS
    rows = CORES * live * MOST
    total = SPLIT * rows
    vmem, hbm = pl.BlockSpec(memory_space=pltpu.VMEM), pl.BlockSpec(memory_space=pltpu.HBM)

    def call(kernel, name, out_shape, operands, flops=0, moved=0):
        return pl.pallas_call(
            kernel,
            out_shape=out_shape,
            in_specs=[vmem] * len(operands),
            out_specs=jax.tree.map(lambda _: vmem, out_shape),
            compiler_params=params(),
            cost_estimate=cost(flops, moved) if flops else None,
            name=name,
        )(*operands)

    def swap_cores(array):
        return lax.ppermute(array, "dp", [(r, r ^ 1) for r in range(CORES)])

    def along_z(array, d):
        hop = [(i, (i // SPLIT ^ d) * SPLIT + i % SPLIT) for i in range(devices)]
        return lax.ppermute(array, "expert", hop)

    def in_plane(array, k):
        hop = []
        for i in range(devices):
            for r in range(CORES):
                hop.append((i * CORES + r, (i ^ near(k, r)) * CORES + r))
        return lax.ppermute(array, ("expert", "dp"), hop)

    gathered = like((live * SIDES * MOST, half), BF16)
    mine, other, hot = pl.pallas_call(
        lambda *refs: gather_kernel(live, *refs),
        out_shape=[gathered, gathered, like((live * 8, tokens), F32)],
        in_specs=[hbm] * 5,
        out_specs=[vmem] * 3,
        scratch_shapes=[
            pltpu.VMEM((TOP, tokens), jnp.int32),
            pltpu.VMEM((TOP, tokens), jnp.int32),
            pltpu.VMEM((TOP, tokens), F32),
            pltpu.VMEM((tokens, model), BF16),
            pltpu.VMEM((tokens, model), BF16),
            pltpu.SemaphoreType.DMA((5,)),
        ],
        compiler_params=params(FIRST_MIB),
        name="gather_rows",
    )(routes.T, keep_mask.T, gate_values.T, layer_input, out_grad)
    chunks = call(
        lambda *refs: chunk_kernel(live, *refs),
        "chunk_rows",
        [like((FOLDS * CORES * SIDES * MOST, fold), BF16)] * live,
        [mine, swap_cores(other)],
        1e10,
        2e7,
    )
    chunks = [chunks[0]] + [along_z(chunks[d], d) for d in range(1, live)]
    mines, others, xs, ss = [], [], [], []
    rows_in_group, planes = total // GROUPS, live // GROUPS
    for group in range(GROUPS):
        rows_here = call(
            merge_kernel,
            "merge_rows",
            like((SIDES * rows // GROUPS, half), BF16),
            chunks[group * planes : (group + 1) * planes],
            1e10 if group else 1e8,
            1e6,
        )
        if group:
            rows_here, _ = lax.optimization_barrier((rows_here, second))
        first, second = in_plane(rows_here, 1), in_plane(rows_here, 2)
        across = in_plane(first, 2)
        mine, x, s = call(
            partial_kernel,
            "partial_products",
            [like((rows_in_group, 3 * width), F32)] + [like((rows_in_group, half), BF16)] * SIDES,
            [rows_here, first, second, across, gate_weight, up_weight, down_transposed],
            6 * rows_in_group * half * width,
            6 * half * width,
        )
        mines.append(mine)
        others.append(swap_cores(mine))
        xs.append(x)
        ss.append(s)
    mines, others, xs, ss = mines[::-1], others[::-1], xs[::-1], ss[::-1]
    sided = call(
        sides_kernel,
        "sides_and_parts",
        [like((rows, half), BF16)] * SPLIT + [like((total, 3 * width), BF16)],
        [*mines, *others, gate_weight, up_weight],
        4 * total * half * width,
        4 * half * width,
    )
    parts, sides = sided[:SPLIT], sided[SPLIT]
    parts = [parts[0]] + [in_plane(parts[k], k) for k in reversed(range(1, SPLIT))]
    gate_grad, up_grad, down_grad, token = pl.pallas_call(
        grads_kernel,
        out_shape=[like((half, width), BF16)] * 3 + [like((8, 128), F32)],
        in_specs=[vmem] * (2 * GROUPS + 1),
        out_specs=[hbm] * 3 + [vmem],
        scratch_shapes=[pltpu.VMEM((half, width), BF16)] * 3 + [pltpu.SemaphoreType.DMA((3, CHUNKS))],
        compiler_params=params(),
        cost_estimate=cost(6 * total * half * width, 6 * half * width + 4 * total * half),
        name="weight_grads",
    )(*xs, *ss, sides)
    chunks = call(
        lambda *refs: sum_kernel(live, *refs),
        "sum_parts",
        [like((FOLDS * CORES * MOST, fold), BF16)] * live,
        [*parts, token],
    )
    chunks = [chunks[0]] + [along_z(chunks[d], d) for d in reversed(range(1, live))]
    back, over = call(
        lambda *refs: split_kernel(live, *refs),
        "split_rows",
        [like((live * 8, half), BF16)] * 2,
        chunks,
    )
    input_grad = call(
        place_kernel, "place_rows", like((tokens, model), BF16), [hot, back, swap_cores(over)]
    )
    return (input_grad, gate_grad, up_grad, down_grad)


def solution(mesh):
    return jax.shard_map(
        body,
        mesh=mesh,
        in_specs=(
            P(("expert", "dp"), None),
            P(("expert", "dp"), None),
            P(("expert", "dp"), None),
            P(("expert", "dp"), None),
            P(("expert", "dp"), None),
            P("dp", "expert"),
            P("dp", "expert"),
            P("dp", "expert"),
        ),
        out_specs=(
            P(("expert", "dp"), None),
            P("dp", "expert"),
            P("dp", "expert"),
            P("dp", "expert"),
        ),
        check_vma=False,
    )
```

```python
import functools

import jax
import jax.numpy as jnp
from jax import lax
from jax.experimental import pallas as pl
from jax.experimental.pallas import tpu as pltpu
from jax.sharding import PartitionSpec as P

SPLIT = 4
MOST = 5
TOP = 8
SIDES = 2
CORES = 2
TOKEN_GROUP = 0
GROUPS = 2
FOLDS = 2
FIRST_MIB = 60
CHUNKS = 7

F32 = jnp.float32
BF16 = jnp.bfloat16


def params(mib=16):
    return pltpu.CompilerParams(vmem_limit_bytes=int(mib * 1024 * 1024))


def cost(flops, moved):
    return pl.CostEstimate(flops=int(flops), bytes_accessed=int(moved), transcendentals=0)


def iota(shape, axis):
    return lax.broadcasted_iota(jnp.int32, shape, axis)


def dot(a, b, dims=((1,), (0,))):
    return lax.dot_general(a, b, (dims, ((), ())), preferred_element_type=F32)


def one_hot(wanted, columns):
    return (iota((wanted.shape[0], columns), 1) == wanted).astype(F32).astype(BF16)


def pick_rows(routes, keep, gates, expert, slot, valid):
    rows, tokens = expert.shape[0], routes.shape[1]
    chosen = jnp.zeros((rows, tokens), F32)
    gate = jnp.zeros((rows, tokens), F32)
    for k in range(routes.shape[0]):
        hit = (routes[k : k + 1, :] == expert) & (keep[k : k + 1, :] == 1)
        chosen = jnp.where(hit, 1.0, chosen)
        gate = jnp.where(hit, gates[k : k + 1, :], gate)
    upto = (iota((tokens, tokens), 0) <= iota((tokens, tokens), 1)).astype(F32).astype(BF16)
    rank = dot(chosen.astype(BF16), upto)
    hot = (chosen > 0.5) & (rank == (slot + 1).astype(F32)) & valid
    return hot, gate


def near(k, core):
    if isinstance(core, int):
        return 3 - k if core and k in (1, 2) else k
    return jnp.where((core == 1) & (k > 0) & (k < 3), 3 - k, k)


def gather_kernel(live, *refs):
    sources, outs, local, sems = refs[:5], refs[5:8], refs[8:13], refs[13]
    copies = [pltpu.make_async_copy(sources[i], local[i], sems.at[i]) for i in range(5)]
    for copy in copies:
        copy.start()
    routes_ref, keep_ref, gates_ref, x_ref, o_ref = local
    place, me = lax.axis_index("expert") // SPLIT, lax.axis_index("dp")
    half = x_ref.shape[1] // CORES
    for copy in copies[:3]:
        copy.wait()
    routes, keep, gates = routes_ref[...], keep_ref[...], gates_ref[...]

    row = iota((live * 8, 1), 0)
    expert, slot = place ^ (row // 8), lax.rem(row, 8)
    hot, _ = pick_rows(routes, keep, gates, expert, slot, slot < MOST)
    outs[2][...] = hot.astype(F32)

    row = iota((live * SIDES * MOST, 1), 0)
    expert = place ^ (row // (SIDES * MOST))
    side, slot = lax.rem(row // MOST, SIDES), lax.rem(row, MOST)
    hot, gate = pick_rows(routes, keep, gates, expert, slot, row >= 0)
    hot_x = (hot & (side == 0)).astype(F32).astype(BF16)
    hot_s = hot & (side == 1)
    scale = jnp.sum(jnp.where(hot_s, gate, 0.0), axis=1, keepdims=True)
    hot_s = hot_s.astype(F32).astype(BF16)
    for copy in copies[3:]:
        copy.wait()
    for q in range(CORES):
        columns = pl.ds(pl.multiple_of((me ^ q) * half, 128), half)
        rows = dot(hot_x, x_ref[:, columns]) + scale * dot(hot_s, o_ref[:, columns])
        outs[q][...] = rows.astype(BF16)


def chunk_kernel(live, mine_ref, other_ref, *outs):
    me = lax.axis_index("dp")
    rows, half = mine_ref.shape
    fold = half // FOLDS
    each = SIDES * MOST
    stacked = jnp.concatenate([mine_ref[...], other_ref[...]], axis=0)
    size = FOLDS * CORES * each
    row = iota((live * size, 1), 0)
    d, part, at = row // size, lax.rem(row // (CORES * each), FOLDS), lax.rem(row, CORES * each)
    wanted = (at // each ^ me) * rows + d * each + lax.rem(at, each)
    total = jnp.zeros((live * size, fold), F32)
    for f in range(FOLDS):
        pick = one_hot(jnp.where(part == f, wanted, -1), CORES * rows)
        total = total + dot(pick, stacked[:, f * fold : (f + 1) * fold])
    total = total.astype(BF16)
    for d in range(live):
        outs[d][...] = total[d * size : (d + 1) * size]


def merge_kernel(*refs):
    chunks, out_ref = refs[:-1], refs[-1]
    size, fold = chunks[0].shape
    stacked = jnp.concatenate([chunk[...] for chunk in chunks], axis=0)
    rows = len(chunks) * CORES * MOST
    out = iota((SIDES * rows, 1), 0)
    side, at = out // rows, lax.rem(out, rows)
    d, replica, slot = at // (CORES * MOST), lax.rem(at // MOST, CORES), lax.rem(at, MOST)
    for f in range(FOLDS):
        wanted = d * size + ((f * CORES + replica) * SIDES + side) * MOST + slot
        picked = dot(one_hot(wanted, len(chunks) * size), stacked)
        out_ref[:, f * fold : (f + 1) * fold] = picked.astype(BF16)


def partial_kernel(*refs):
    blocks, (gate_ref, up_ref, down_ref, out_ref), sided = refs[:SPLIT], refs[SPLIT:-2], refs[-2:]
    each, width = blocks[0].shape[0], gate_ref.shape[1]
    rows = each // SIDES
    stacked = jnp.concatenate([block[...] for block in blocks], axis=0)
    at = iota((SPLIT * rows, 1), 0)
    block = near(at // rows, lax.axis_index("dp"))
    for side in range(SIDES):
        wanted = block * each + side * rows + lax.rem(at, rows)
        sided[side][...] = dot(one_hot(wanted, SPLIT * each), stacked).astype(BF16)
    out_ref[:, :width] = dot(sided[0][...], gate_ref[...])
    out_ref[:, width : 2 * width] = dot(sided[0][...], up_ref[...])
    out_ref[:, 2 * width :] = dot(sided[1][...], down_ref[...])


def sides_kernel(*refs):
    sums, (gate_ref, up_ref), outs = refs[: 2 * GROUPS], refs[2 * GROUPS : 2 * GROUPS + 2], refs[2 * GROUPS + 2 :]
    parts, sides_ref = outs[:-1], outs[-1]
    width = gate_ref.shape[1]
    rows = parts[0].shape[0] * GROUPS
    total = [sums[i][...] + sums[GROUPS + i][...] for i in range(GROUPS)]
    total = jnp.concatenate(total, axis=0)
    pre_gate, pre_up = total[:, :width], total[:, width : 2 * width]
    hidden_grad = total[:, 2 * width :]
    sigma = jax.nn.sigmoid(pre_gate)
    activated = pre_gate * sigma
    slope = sigma * (1.0 + pre_gate * (1.0 - sigma))
    gate_side = (hidden_grad * pre_up * slope).astype(BF16)
    up_side = (hidden_grad * activated).astype(BF16)
    sides_ref[:, :width] = gate_side
    sides_ref[:, width : 2 * width] = up_side
    sides_ref[:, 2 * width :] = (activated * pre_up).astype(BF16)
    across = ((1,), (1,))
    at = iota((SPLIT * rows, 1), 0)
    k = near(at // rows, lax.axis_index("dp"))
    group, row = lax.rem(at, rows) // (rows // GROUPS), lax.rem(at, rows // GROUPS)
    order = one_hot(((GROUPS - 1 - group) * SPLIT + k) * (rows // GROUPS) + row, SPLIT * rows)
    gate_side, up_side = dot(order, gate_side).astype(BF16), dot(order, up_side).astype(BF16)
    part = dot(gate_side, gate_ref[...], across) + dot(up_side, up_ref[...], across)
    each = rows // GROUPS
    for k in range(SPLIT):
        for group in range(GROUPS):
            start = (k * GROUPS + group) * each
            parts[group * SPLIT + k][...] = part[start : start + each].astype(BF16)


def grads_kernel(*refs):
    xs, ss = refs[:GROUPS], refs[GROUPS : 2 * GROUPS]
    sides_ref, outs, token_ref = refs[2 * GROUPS], refs[2 * GROUPS + 1 : -5], refs[-5]
    held, sems = refs[-4:-1], refs[-1]
    half, width = held[0].shape
    block = half // CHUNKS
    first = ((0,), (0,))
    copies = []
    for c in range(CHUNKS):
        part = slice(c * block, (c + 1) * block)
        x = jnp.concatenate([ref[:, part] for ref in xs], axis=0)
        s = jnp.concatenate([ref[:, part] for ref in ss], axis=0)
        for i, rows in enumerate((x, x, s)):
            held[i][part, :] = dot(rows, sides_ref[:, i * width : (i + 1) * width], first).astype(BF16)
            copy = pltpu.make_async_copy(
                held[i].at[pl.ds(c * block, block)], outs[i].at[pl.ds(c * block, block)], sems.at[i, c]
            )
            copy.start()
            copies.append(copy)
    for copy in copies:
        copy.wait()
    token_ref[...] = jnp.zeros(token_ref.shape, F32)


def sum_kernel(count, ordered, *refs):
    parts, outs = refs[:SPLIT], refs[SPLIT + ordered :]
    total = parts[0][...].astype(F32)
    for part in parts[1:]:
        total = total + part[...].astype(F32)
    total = total.astype(BF16)
    rows, half = total.shape
    fold = half // FOLDS
    each = CORES * MOST
    size = FOLDS * each
    row = iota((count * size, 1), 0)
    d, part, at = row // size, lax.rem(row // each, FOLDS), lax.rem(row, each)
    moved = jnp.zeros((count * size, fold), F32)
    for f in range(FOLDS):
        pick = one_hot(jnp.where(part == f, d * each + at, -1), rows)
        moved = moved + dot(pick, total[:, f * fold : (f + 1) * fold])
    for d in range(count):
        outs[d][...] = moved[d * size : (d + 1) * size].astype(BF16)


def split_kernel(*refs):
    chunks, outs = refs[:-CORES], refs[-CORES:]
    me = lax.axis_index("dp")
    size, fold = chunks[0].shape
    stacked = jnp.concatenate([chunk[...].astype(F32) for chunk in chunks], axis=0).astype(BF16)
    rows = len(chunks) * 8
    out = iota((CORES * rows, 1), 0)
    q, d, slot = out // rows, lax.rem(out, rows) // 8, lax.rem(out, 8)
    for f in range(FOLDS):
        wanted = d * size + (f * CORES + (q ^ me)) * MOST + slot
        pick = one_hot(jnp.where(slot < MOST, wanted, -1), len(chunks) * size)
        picked = dot(pick, stacked).astype(BF16)
        for core in range(CORES):
            outs[core][:, f * fold : (f + 1) * fold] = picked[core * rows : (core + 1) * rows]


def place_kernel(hot_ref, *refs):
    sources, out_ref = refs[:-1], refs[-1]
    me = lax.axis_index("dp")
    half = out_ref.shape[1] // CORES
    hot = hot_ref[...].astype(BF16)
    for q in range(CORES):
        rows = jnp.concatenate([ref[...] for ref in sources[q * GROUPS : (q + 1) * GROUPS]], axis=0)
        columns = pl.ds(pl.multiple_of((me ^ q) * half, 128), half)
        out_ref[:, columns] = dot(hot, rows, ((0,), (0,))).astype(BF16)


def like(shape, dtype):
    return jax.ShapeDtypeStruct(shape, dtype)


def body(
    layer_input, out_grad, routes, gate_values, keep_mask, gate_weight, up_weight, down_transposed
):
    devices = lax.axis_size("expert")
    live = devices // SPLIT
    tokens, model = layer_input.shape
    half, width = gate_weight.shape
    fold = half // FOLDS
    rows = CORES * live * MOST
    total = SPLIT * rows
    vmem, hbm = pl.BlockSpec(memory_space=pltpu.VMEM), pl.BlockSpec(memory_space=pltpu.HBM)

    def call(kernel, name, out_shape, operands, flops=0, moved=0):
        return pl.pallas_call(
            kernel,
            out_shape=out_shape,
            in_specs=[vmem] * len(operands),
            out_specs=jax.tree.map(lambda _: vmem, out_shape),
            compiler_params=params(),
            cost_estimate=cost(flops, moved) if flops else None,
            name=name,
        )(*operands)

    def swap_cores(array):
        return lax.ppermute(array, "dp", [(r, r ^ 1) for r in range(CORES)])

    def along_z(array, d):
        hop = [(i, (i // SPLIT ^ d) * SPLIT + i % SPLIT) for i in range(devices)]
        return lax.ppermute(array, "expert", hop)

    def in_plane(array, k):
        hop = []
        for i in range(devices):
            for r in range(CORES):
                hop.append((i * CORES + r, (i ^ near(k, r)) * CORES + r))
        return lax.ppermute(array, ("expert", "dp"), hop)

    gathered = like((live * SIDES * MOST, half), BF16)
    mine, other, hot = pl.pallas_call(
        lambda *refs: gather_kernel(live, *refs),
        out_shape=[gathered, gathered, like((live * 8, tokens), F32)],
        in_specs=[hbm] * 5,
        out_specs=[vmem] * 3,
        scratch_shapes=[
            pltpu.VMEM((TOP, tokens), jnp.int32),
            pltpu.VMEM((TOP, tokens), jnp.int32),
            pltpu.VMEM((TOP, tokens), F32),
            pltpu.VMEM((tokens, model), BF16),
            pltpu.VMEM((tokens, model), BF16),
            pltpu.SemaphoreType.DMA((5,)),
        ],
        compiler_params=params(FIRST_MIB),
        name="gather_rows",
    )(routes.T, keep_mask.T, gate_values.T, layer_input, out_grad)
    chunks = call(
        lambda *refs: chunk_kernel(live, *refs),
        "chunk_rows",
        [like((FOLDS * CORES * SIDES * MOST, fold), BF16)] * live,
        [mine, swap_cores(other)],
        1e10,
        2e7,
    )
    chunks = [chunks[0]] + [along_z(chunks[d], d) for d in range(1, live)]
    mines, others, xs, ss = [], [], [], []
    rows_in_group, planes = total // GROUPS, live // GROUPS
    for group in reversed(range(GROUPS)):
        rows_here = call(
            merge_kernel,
            "merge_rows",
            like((SIDES * rows // GROUPS, half), BF16),
            chunks[group * planes : (group + 1) * planes],
            1e8,
            1e6,
        )
        first, second = in_plane(rows_here, 1), in_plane(rows_here, 2)
        across = in_plane(first, 2)
        mine, x, s = call(
            partial_kernel,
            "partial_products",
            [like((rows_in_group, 3 * width), F32)] + [like((rows_in_group, half), BF16)] * SIDES,
            [rows_here, first, second, across, gate_weight, up_weight, down_transposed],
            6 * rows_in_group * half * width,
            6 * half * width,
        )
        mines.append(mine)
        others.append(swap_cores(mine))
        xs.append(x)
        ss.append(s)
    sided = call(
        sides_kernel,
        "sides_and_parts",
        [like((rows // GROUPS, half), BF16)] * (GROUPS * SPLIT) + [like((total, 3 * width), BF16)],
        [*mines, *others, gate_weight, up_weight],
        4 * total * half * width,
        4 * half * width,
    )
    parts, sides = [], sided[-1]
    for group in range(GROUPS):
        mine = sided[group * SPLIT : (group + 1) * SPLIT]
        parts.append([mine[0]] + [in_plane(mine[k], k) for k in reversed(range(1, SPLIT))])
    gate_grad, up_grad, down_grad, token = pl.pallas_call(
        grads_kernel,
        out_shape=[like((half, width), BF16)] * 3 + [like((8, 128), F32)],
        in_specs=[vmem] * (2 * GROUPS + 1),
        out_specs=[hbm] * 3 + [vmem],
        scratch_shapes=[pltpu.VMEM((half, width), BF16)] * 3 + [pltpu.SemaphoreType.DMA((3, CHUNKS))],
        compiler_params=params(),
        cost_estimate=cost(6 * total * half * width, 6 * half * width + 4 * total * half),
        name="weight_grads",
    )(*xs, *ss, sides)
    back, over = [], []
    for group in range(GROUPS):
        ordered = group == TOKEN_GROUP
        chunks = call(
            functools.partial(sum_kernel, planes, ordered),
            "sum_parts",
            [like((FOLDS * CORES * MOST, fold), BF16)] * planes,
            parts[group] + [token] * ordered,
        )
        first = group * planes
        chunks = [along_z(chunks[d], first + d) if first + d else chunks[0] for d in range(planes)]
        mine, other = call(
            split_kernel,
            "split_rows",
            [like((planes * 8, half), BF16)] * CORES,
            chunks,
            1e10 if group else 1e8,
            1e6,
        )
        back.append(mine)
        over.append(swap_cores(other))
    input_grad = call(place_kernel, "place_rows", like((tokens, model), BF16), [hot, *back, *over])
    return (input_grad, gate_grad, up_grad, down_grad)


def solution(mesh):
    return jax.shard_map(
        body,
        mesh=mesh,
        in_specs=(
            P(("expert", "dp"), None),
            P(("expert", "dp"), None),
            P(("expert", "dp"), None),
            P(("expert", "dp"), None),
            P(("expert", "dp"), None),
            P("dp", "expert"),
            P("dp", "expert"),
            P("dp", "expert"),
        ),
        out_specs=(
            P(("expert", "dp"), None),
            P("dp", "expert"),
            P("dp", "expert"),
            P("dp", "expert"),
        ),
        check_vma=False,
    )
```

```python
import functools

import jax
import jax.numpy as jnp
from jax import lax
from jax.experimental import pallas as pl
from jax.experimental.pallas import tpu as pltpu
from jax.sharding import PartitionSpec as P

SPLIT = 4
MOST = 5
TOP = 8
SIDES = 2
CORES = 2
TOKEN_GROUP = 1
GROUPS = 2
FOLDS = 2
FIRST_MIB = 60
CHUNKS = 7

F32 = jnp.float32
BF16 = jnp.bfloat16


def params(mib=16):
    return pltpu.CompilerParams(vmem_limit_bytes=int(mib * 1024 * 1024))


def cost(flops, moved):
    return pl.CostEstimate(flops=int(flops), bytes_accessed=int(moved), transcendentals=0)


def iota(shape, axis):
    return lax.broadcasted_iota(jnp.int32, shape, axis)


def dot(a, b, dims=((1,), (0,))):
    return lax.dot_general(a, b, (dims, ((), ())), preferred_element_type=F32)


def one_hot(wanted, columns):
    return (iota((wanted.shape[0], columns), 1) == wanted).astype(F32).astype(BF16)


def pick_rows(routes, keep, gates, expert, slot, valid):
    rows, tokens = expert.shape[0], routes.shape[1]
    chosen = jnp.zeros((rows, tokens), F32)
    gate = jnp.zeros((rows, tokens), F32)
    for k in range(routes.shape[0]):
        hit = (routes[k : k + 1, :] == expert) & (keep[k : k + 1, :] == 1)
        chosen = jnp.where(hit, 1.0, chosen)
        gate = jnp.where(hit, gates[k : k + 1, :], gate)
    upto = (iota((tokens, tokens), 0) <= iota((tokens, tokens), 1)).astype(F32).astype(BF16)
    rank = dot(chosen.astype(BF16), upto)
    hot = (chosen > 0.5) & (rank == (slot + 1).astype(F32)) & valid
    return hot, gate


def near(k, core):
    if isinstance(core, int):
        return 3 - k if core and k in (1, 2) else k
    return jnp.where((core == 1) & (k > 0) & (k < 3), 3 - k, k)


def gather_kernel(live, *refs):
    sources, outs, local, sems = refs[:5], refs[5:8], refs[8:13], refs[13]
    copies = [pltpu.make_async_copy(sources[i], local[i], sems.at[i]) for i in range(5)]
    for copy in copies:
        copy.start()
    routes_ref, keep_ref, gates_ref, x_ref, o_ref = local
    place, me = lax.axis_index("expert") // SPLIT, lax.axis_index("dp")
    half = x_ref.shape[1] // CORES
    for copy in copies[:3]:
        copy.wait()
    routes, keep, gates = routes_ref[...], keep_ref[...], gates_ref[...]

    row = iota((live * 8, 1), 0)
    expert, slot = place ^ (row // 8), lax.rem(row, 8)
    hot, _ = pick_rows(routes, keep, gates, expert, slot, slot < MOST)
    outs[2][...] = hot.astype(F32)

    row = iota((live * SIDES * MOST, 1), 0)
    expert = place ^ (row // (SIDES * MOST))
    side, slot = lax.rem(row // MOST, SIDES), lax.rem(row, MOST)
    hot, gate = pick_rows(routes, keep, gates, expert, slot, row >= 0)
    hot_x = (hot & (side == 0)).astype(F32).astype(BF16)
    hot_s = hot & (side == 1)
    scale = jnp.sum(jnp.where(hot_s, gate, 0.0), axis=1, keepdims=True)
    hot_s = hot_s.astype(F32).astype(BF16)
    for copy in copies[3:]:
        copy.wait()
    for q in range(CORES):
        columns = pl.ds(pl.multiple_of((me ^ q) * half, 128), half)
        rows = dot(hot_x, x_ref[:, columns]) + scale * dot(hot_s, o_ref[:, columns])
        outs[q][...] = rows.astype(BF16)


def chunk_kernel(live, mine_ref, other_ref, *outs):
    me = lax.axis_index("dp")
    rows, half = mine_ref.shape
    fold = half // FOLDS
    each = SIDES * MOST
    stacked = jnp.concatenate([mine_ref[...], other_ref[...]], axis=0)
    size = FOLDS * CORES * each
    row = iota((live * size, 1), 0)
    d, part, at = row // size, lax.rem(row // (CORES * each), FOLDS), lax.rem(row, CORES * each)
    wanted = (at // each ^ me) * rows + d * each + lax.rem(at, each)
    total = jnp.zeros((live * size, fold), F32)
    for f in range(FOLDS):
        pick = one_hot(jnp.where(part == f, wanted, -1), CORES * rows)
        total = total + dot(pick, stacked[:, f * fold : (f + 1) * fold])
    total = total.astype(BF16)
    for d in range(live):
        outs[d][...] = total[d * size : (d + 1) * size]


def merge_kernel(*refs):
    chunks, out_ref = refs[:-1], refs[-1]
    size, fold = chunks[0].shape
    stacked = jnp.concatenate([chunk[...] for chunk in chunks], axis=0)
    rows = len(chunks) * CORES * MOST
    out = iota((SIDES * rows, 1), 0)
    side, at = out // rows, lax.rem(out, rows)
    d, replica, slot = at // (CORES * MOST), lax.rem(at // MOST, CORES), lax.rem(at, MOST)
    for f in range(FOLDS):
        wanted = d * size + ((f * CORES + replica) * SIDES + side) * MOST + slot
        picked = dot(one_hot(wanted, len(chunks) * size), stacked)
        out_ref[:, f * fold : (f + 1) * fold] = picked.astype(BF16)


def partial_kernel(*refs):
    blocks, (gate_ref, up_ref, down_ref, out_ref), sided = refs[:SPLIT], refs[SPLIT:-2], refs[-2:]
    each, width = blocks[0].shape[0], gate_ref.shape[1]
    rows = each // SIDES
    stacked = jnp.concatenate([block[...] for block in blocks], axis=0)
    at = iota((SPLIT * rows, 1), 0)
    block = near(at // rows, lax.axis_index("dp"))
    for side in range(SIDES):
        wanted = block * each + side * rows + lax.rem(at, rows)
        sided[side][...] = dot(one_hot(wanted, SPLIT * each), stacked).astype(BF16)
    out_ref[:, :width] = dot(sided[0][...], gate_ref[...])
    out_ref[:, width : 2 * width] = dot(sided[0][...], up_ref[...])
    out_ref[:, 2 * width :] = dot(sided[1][...], down_ref[...])


def sides_kernel(*refs):
    sums, (gate_ref, up_ref), outs = refs[: 2 * GROUPS], refs[2 * GROUPS : 2 * GROUPS + 2], refs[2 * GROUPS + 2 :]
    parts, sides_ref = outs[:-1], outs[-1]
    width = gate_ref.shape[1]
    rows = parts[0].shape[0] * GROUPS
    total = [sums[i][...] + sums[GROUPS + i][...] for i in range(GROUPS)]
    total = jnp.concatenate(total, axis=0)
    pre_gate, pre_up = total[:, :width], total[:, width : 2 * width]
    hidden_grad = total[:, 2 * width :]
    sigma = jax.nn.sigmoid(pre_gate)
    activated = pre_gate * sigma
    slope = sigma * (1.0 + pre_gate * (1.0 - sigma))
    gate_side = (hidden_grad * pre_up * slope).astype(BF16)
    up_side = (hidden_grad * activated).astype(BF16)
    sides_ref[:, :width] = gate_side
    sides_ref[:, width : 2 * width] = up_side
    sides_ref[:, 2 * width :] = (activated * pre_up).astype(BF16)
    across = ((1,), (1,))
    at = iota((SPLIT * rows, 1), 0)
    k = near(at // rows, lax.axis_index("dp"))
    group, row = lax.rem(at, rows) // (rows // GROUPS), lax.rem(at, rows // GROUPS)
    order = one_hot(((GROUPS - 1 - group) * SPLIT + k) * (rows // GROUPS) + row, SPLIT * rows)
    gate_side, up_side = dot(order, gate_side).astype(BF16), dot(order, up_side).astype(BF16)
    part = dot(gate_side, gate_ref[...], across) + dot(up_side, up_ref[...], across)
    each = rows // GROUPS
    for k in range(SPLIT):
        for group in range(GROUPS):
            start = (k * GROUPS + group) * each
            parts[group * SPLIT + k][...] = part[start : start + each].astype(BF16)


def grads_kernel(*refs):
    xs, ss = refs[:GROUPS], refs[GROUPS : 2 * GROUPS]
    sides_ref, outs, token_ref = refs[2 * GROUPS], refs[2 * GROUPS + 1 : -5], refs[-5]
    held, sems = refs[-4:-1], refs[-1]
    half, width = held[0].shape
    block = half // CHUNKS
    first = ((0,), (0,))
    copies = []
    for c in range(CHUNKS):
        part = slice(c * block, (c + 1) * block)
        x = jnp.concatenate([ref[:, part] for ref in xs], axis=0)
        s = jnp.concatenate([ref[:, part] for ref in ss], axis=0)
        for i, rows in enumerate((x, x, s)):
            held[i][part, :] = dot(rows, sides_ref[:, i * width : (i + 1) * width], first).astype(BF16)
            copy = pltpu.make_async_copy(
                held[i].at[pl.ds(c * block, block)], outs[i].at[pl.ds(c * block, block)], sems.at[i, c]
            )
            copy.start()
            copies.append(copy)
    for copy in copies:
        copy.wait()
    token_ref[...] = jnp.zeros(token_ref.shape, F32)


def sum_kernel(count, *refs):
    parts, outs = refs[:SPLIT], refs[SPLIT:]
    total = parts[0][...].astype(F32)
    for part in parts[1:]:
        total = total + part[...].astype(F32)
    total = total.astype(BF16)
    rows, half = total.shape
    fold = half // FOLDS
    each = CORES * MOST
    size = FOLDS * each
    row = iota((count * size, 1), 0)
    d, part, at = row // size, lax.rem(row // each, FOLDS), lax.rem(row, each)
    moved = jnp.zeros((count * size, fold), F32)
    for f in range(FOLDS):
        pick = one_hot(jnp.where(part == f, d * each + at, -1), rows)
        moved = moved + dot(pick, total[:, f * fold : (f + 1) * fold])
    for d in range(count):
        outs[d][...] = moved[d * size : (d + 1) * size].astype(BF16)


def split_kernel(count, *refs):
    chunks, outs = refs[:count], refs[-CORES:]
    me = lax.axis_index("dp")
    size, fold = chunks[0].shape
    stacked = jnp.concatenate([chunk[...].astype(F32) for chunk in chunks], axis=0).astype(BF16)
    rows = len(chunks) * 8
    out = iota((CORES * rows, 1), 0)
    q, d, slot = out // rows, lax.rem(out, rows) // 8, lax.rem(out, 8)
    for f in range(FOLDS):
        wanted = d * size + (f * CORES + (q ^ me)) * MOST + slot
        pick = one_hot(jnp.where(slot < MOST, wanted, -1), len(chunks) * size)
        picked = dot(pick, stacked).astype(BF16)
        for core in range(CORES):
            outs[core][:, f * fold : (f + 1) * fold] = picked[core * rows : (core + 1) * rows]


def place_kernel(hot_ref, *refs):
    sources, out_ref = refs[:-1], refs[-1]
    me = lax.axis_index("dp")
    half = out_ref.shape[1] // CORES
    hot = hot_ref[...].astype(BF16)
    for q in range(CORES):
        rows = jnp.concatenate([ref[...] for ref in sources[q * GROUPS : (q + 1) * GROUPS]], axis=0)
        columns = pl.ds(pl.multiple_of((me ^ q) * half, 128), half)
        out_ref[:, columns] = dot(hot, rows, ((0,), (0,))).astype(BF16)


def like(shape, dtype):
    return jax.ShapeDtypeStruct(shape, dtype)


def body(
    layer_input, out_grad, routes, gate_values, keep_mask, gate_weight, up_weight, down_transposed
):
    devices = lax.axis_size("expert")
    live = devices // SPLIT
    tokens, model = layer_input.shape
    half, width = gate_weight.shape
    fold = half // FOLDS
    rows = CORES * live * MOST
    total = SPLIT * rows
    vmem, hbm = pl.BlockSpec(memory_space=pltpu.VMEM), pl.BlockSpec(memory_space=pltpu.HBM)

    def call(kernel, name, out_shape, operands, flops=0, moved=0):
        return pl.pallas_call(
            kernel,
            out_shape=out_shape,
            in_specs=[vmem] * len(operands),
            out_specs=jax.tree.map(lambda _: vmem, out_shape),
            compiler_params=params(),
            cost_estimate=cost(flops, moved) if flops else None,
            name=name,
        )(*operands)

    def swap_cores(array):
        return lax.ppermute(array, "dp", [(r, r ^ 1) for r in range(CORES)])

    def along_z(array, d):
        hop = [(i, (i // SPLIT ^ d) * SPLIT + i % SPLIT) for i in range(devices)]
        return lax.ppermute(array, "expert", hop)

    def in_plane(array, k):
        hop = []
        for i in range(devices):
            for r in range(CORES):
                hop.append((i * CORES + r, (i ^ near(k, r)) * CORES + r))
        return lax.ppermute(array, ("expert", "dp"), hop)

    gathered = like((live * SIDES * MOST, half), BF16)
    mine, other, hot = pl.pallas_call(
        lambda *refs: gather_kernel(live, *refs),
        out_shape=[gathered, gathered, like((live * 8, tokens), F32)],
        in_specs=[hbm] * 5,
        out_specs=[vmem] * 3,
        scratch_shapes=[
            pltpu.VMEM((TOP, tokens), jnp.int32),
            pltpu.VMEM((TOP, tokens), jnp.int32),
            pltpu.VMEM((TOP, tokens), F32),
            pltpu.VMEM((tokens, model), BF16),
            pltpu.VMEM((tokens, model), BF16),
            pltpu.SemaphoreType.DMA((5,)),
        ],
        compiler_params=params(FIRST_MIB),
        name="gather_rows",
    )(routes.T, keep_mask.T, gate_values.T, layer_input, out_grad)
    chunks = call(
        lambda *refs: chunk_kernel(live, *refs),
        "chunk_rows",
        [like((FOLDS * CORES * SIDES * MOST, fold), BF16)] * live,
        [mine, swap_cores(other)],
        1e10,
        2e7,
    )
    chunks = [chunks[0]] + [along_z(chunks[d], d) for d in range(1, live)]
    mines, others, xs, ss = [], [], [], []
    rows_in_group, planes = total // GROUPS, live // GROUPS
    for group in reversed(range(GROUPS)):
        rows_here = call(
            merge_kernel,
            "merge_rows",
            like((SIDES * rows // GROUPS, half), BF16),
            chunks[group * planes : (group + 1) * planes],
            1e8,
            1e6,
        )
        first, second = in_plane(rows_here, 1), in_plane(rows_here, 2)
        across = in_plane(first, 2)
        mine, x, s = call(
            partial_kernel,
            "partial_products",
            [like((rows_in_group, 3 * width), F32)] + [like((rows_in_group, half), BF16)] * SIDES,
            [rows_here, first, second, across, gate_weight, up_weight, down_transposed],
            6 * rows_in_group * half * width,
            6 * half * width,
        )
        mines.append(mine)
        others.append(swap_cores(mine))
        xs.append(x)
        ss.append(s)
    sided = call(
        sides_kernel,
        "sides_and_parts",
        [like((rows // GROUPS, half), BF16)] * (GROUPS * SPLIT) + [like((total, 3 * width), BF16)],
        [*mines, *others, gate_weight, up_weight],
        4 * total * half * width,
        4 * half * width,
    )
    parts, sides = [], sided[-1]
    for group in range(GROUPS):
        mine = sided[group * SPLIT : (group + 1) * SPLIT]
        parts.append([mine[0]] + [in_plane(mine[k], k) for k in reversed(range(1, SPLIT))])
    gate_grad, up_grad, down_grad, token = pl.pallas_call(
        grads_kernel,
        out_shape=[like((half, width), BF16)] * 3 + [like((8, 128), F32)],
        in_specs=[vmem] * (2 * GROUPS + 1),
        out_specs=[hbm] * 3 + [vmem],
        scratch_shapes=[pltpu.VMEM((half, width), BF16)] * 3 + [pltpu.SemaphoreType.DMA((3, CHUNKS))],
        compiler_params=params(),
        cost_estimate=cost(6 * total * half * width, 6 * half * width + 4 * total * half),
        name="weight_grads",
    )(*xs, *ss, sides)
    back, over = [], []
    for group in range(GROUPS):
        ordered = group == TOKEN_GROUP
        chunks = call(
            functools.partial(sum_kernel, planes),
            "sum_parts",
            [like((FOLDS * CORES * MOST, fold), BF16)] * planes,
            parts[group],
        )
        first = group * planes
        chunks = [along_z(chunks[d], first + d) if first + d else chunks[0] for d in range(planes)]
        mine, other = call(
            functools.partial(split_kernel, planes),
            "split_rows",
            [like((planes * 8, half), BF16)] * CORES,
            chunks + [token] * ordered,
            1e10 if group else 1e8,
            1e6,
        )
        back.append(mine)
        over.append(swap_cores(other))
    input_grad = call(place_kernel, "place_rows", like((tokens, model), BF16), [hot, *back, *over])
    return (input_grad, gate_grad, up_grad, down_grad)


def solution(mesh):
    return jax.shard_map(
        body,
        mesh=mesh,
        in_specs=(
            P(("expert", "dp"), None),
            P(("expert", "dp"), None),
            P(("expert", "dp"), None),
            P(("expert", "dp"), None),
            P(("expert", "dp"), None),
            P("dp", "expert"),
            P("dp", "expert"),
            P("dp", "expert"),
        ),
        out_specs=(
            P(("expert", "dp"), None),
            P("dp", "expert"),
            P("dp", "expert"),
            P("dp", "expert"),
        ),
        check_vma=False,
    )
```

```python
import functools

import jax
import jax.numpy as jnp
from jax import lax
from jax.experimental import pallas as pl
from jax.experimental.pallas import tpu as pltpu
from jax.sharding import PartitionSpec as P

SPLIT = 4
MOST = 5
TOP = 8
SIDES = 2
CORES = 2
TOKEN_GROUP = 1
GROUPS = 2
FOLDS = 2
FIRST_MIB = 60
CHUNKS = 7

F32 = jnp.float32
BF16 = jnp.bfloat16


def params(mib=16):
    return pltpu.CompilerParams(vmem_limit_bytes=int(mib * 1024 * 1024))


def cost(flops, moved):
    return pl.CostEstimate(flops=int(flops), bytes_accessed=int(moved), transcendentals=0)


def iota(shape, axis):
    return lax.broadcasted_iota(jnp.int32, shape, axis)


def dot(a, b, dims=((1,), (0,))):
    return lax.dot_general(a, b, (dims, ((), ())), preferred_element_type=F32)


def one_hot(wanted, columns):
    return (iota((wanted.shape[0], columns), 1) == wanted).astype(F32).astype(BF16)


def pick_rows(routes, keep, gates, expert, slot, valid):
    rows, tokens = expert.shape[0], routes.shape[1]
    chosen = jnp.zeros((rows, tokens), F32)
    gate = jnp.zeros((rows, tokens), F32)
    for k in range(routes.shape[0]):
        hit = (routes[k : k + 1, :] == expert) & (keep[k : k + 1, :] == 1)
        chosen = jnp.where(hit, 1.0, chosen)
        gate = jnp.where(hit, gates[k : k + 1, :], gate)
    upto = (iota((tokens, tokens), 0) <= iota((tokens, tokens), 1)).astype(F32).astype(BF16)
    rank = dot(chosen.astype(BF16), upto)
    hot = (chosen > 0.5) & (rank == (slot + 1).astype(F32)) & valid
    return hot, gate


def near(k, core):
    if isinstance(core, int):
        return 3 - k if core and k in (1, 2) else k
    return jnp.where((core == 1) & (k > 0) & (k < 3), 3 - k, k)


def gather_kernel(live, *refs):
    sources, outs, local, sems = refs[:5], refs[5:8], refs[8:13], refs[13]
    copies = [pltpu.make_async_copy(sources[i], local[i], sems.at[i]) for i in range(5)]
    for copy in copies:
        copy.start()
    routes_ref, keep_ref, gates_ref, x_ref, o_ref = local
    place, me = lax.axis_index("expert") // SPLIT, lax.axis_index("dp")
    half = x_ref.shape[1] // CORES
    for copy in copies[:3]:
        copy.wait()
    routes, keep, gates = routes_ref[...], keep_ref[...], gates_ref[...]

    row = iota((live * 8, 1), 0)
    expert, slot = place ^ (row // 8), lax.rem(row, 8)
    hot, _ = pick_rows(routes, keep, gates, expert, slot, slot < MOST)
    outs[2][...] = hot.astype(F32)

    row = iota((live * SIDES * MOST, 1), 0)
    expert = place ^ (row // (SIDES * MOST))
    side, slot = lax.rem(row // MOST, SIDES), lax.rem(row, MOST)
    hot, gate = pick_rows(routes, keep, gates, expert, slot, row >= 0)
    hot_x = (hot & (side == 0)).astype(F32).astype(BF16)
    hot_s = hot & (side == 1)
    scale = jnp.sum(jnp.where(hot_s, gate, 0.0), axis=1, keepdims=True)
    hot_s = hot_s.astype(F32).astype(BF16)
    for copy in copies[3:]:
        copy.wait()
    for q in range(CORES):
        columns = pl.ds(pl.multiple_of((me ^ q) * half, 128), half)
        rows = dot(hot_x, x_ref[:, columns]) + scale * dot(hot_s, o_ref[:, columns])
        outs[q][...] = rows.astype(BF16)


def chunk_kernel(live, mine_ref, other_ref, *outs):
    me = lax.axis_index("dp")
    rows, half = mine_ref.shape
    fold = half // FOLDS
    each = SIDES * MOST
    stacked = jnp.concatenate([mine_ref[...], other_ref[...]], axis=0)
    size = FOLDS * CORES * each
    row = iota((live * size, 1), 0)
    d, part, at = row // size, lax.rem(row // (CORES * each), FOLDS), lax.rem(row, CORES * each)
    wanted = (at // each ^ me) * rows + d * each + lax.rem(at, each)
    total = jnp.zeros((live * size, fold), F32)
    for f in range(FOLDS):
        pick = one_hot(jnp.where(part == f, wanted, -1), CORES * rows)
        total = total + dot(pick, stacked[:, f * fold : (f + 1) * fold])
    total = total.astype(BF16)
    for d in range(live):
        outs[d][...] = total[d * size : (d + 1) * size]


def merge_kernel(*refs):
    chunks, out_ref = refs[:-1], refs[-1]
    size, fold = chunks[0].shape
    stacked = jnp.concatenate([chunk[...] for chunk in chunks], axis=0)
    rows = len(chunks) * CORES * MOST
    out = iota((SIDES * rows, 1), 0)
    side, at = out // rows, lax.rem(out, rows)
    d, replica, slot = at // (CORES * MOST), lax.rem(at // MOST, CORES), lax.rem(at, MOST)
    for f in range(FOLDS):
        wanted = d * size + ((f * CORES + replica) * SIDES + side) * MOST + slot
        picked = dot(one_hot(wanted, len(chunks) * size), stacked)
        out_ref[:, f * fold : (f + 1) * fold] = picked.astype(BF16)


def partial_kernel(*refs):
    blocks, (gate_ref, up_ref, down_ref, out_ref), sided = refs[:SPLIT], refs[SPLIT:-2], refs[-2:]
    each, width = blocks[0].shape[0], gate_ref.shape[1]
    rows = each // SIDES
    stacked = jnp.concatenate([block[...] for block in blocks], axis=0)
    at = iota((SPLIT * rows, 1), 0)
    block = near(at // rows, lax.axis_index("dp"))
    for side in range(SIDES):
        wanted = block * each + side * rows + lax.rem(at, rows)
        sided[side][...] = dot(one_hot(wanted, SPLIT * each), stacked).astype(BF16)
    out_ref[:, :width] = dot(sided[0][...], gate_ref[...])
    out_ref[:, width : 2 * width] = dot(sided[0][...], up_ref[...])
    out_ref[:, 2 * width :] = dot(sided[1][...], down_ref[...])


def sides_kernel(*refs):
    sums, (gate_ref, up_ref), outs = refs[: 2 * GROUPS], refs[2 * GROUPS : 2 * GROUPS + 2], refs[2 * GROUPS + 2 :]
    parts, sides_ref = outs[:-1], outs[-1]
    width = gate_ref.shape[1]
    rows = parts[0].shape[0] // FOLDS * GROUPS
    total = [sums[i][...] + sums[GROUPS + i][...] for i in range(GROUPS)]
    total = jnp.concatenate(total, axis=0)
    pre_gate, pre_up = total[:, :width], total[:, width : 2 * width]
    hidden_grad = total[:, 2 * width :]
    sigma = jax.nn.sigmoid(pre_gate)
    activated = pre_gate * sigma
    slope = sigma * (1.0 + pre_gate * (1.0 - sigma))
    gate_side = (hidden_grad * pre_up * slope).astype(BF16)
    up_side = (hidden_grad * activated).astype(BF16)
    sides_ref[:, :width] = gate_side
    sides_ref[:, width : 2 * width] = up_side
    sides_ref[:, 2 * width :] = (activated * pre_up).astype(BF16)
    across = ((1,), (1,))
    at = iota((SPLIT * rows, 1), 0)
    k = near(at // rows, lax.axis_index("dp"))
    group, row = lax.rem(at, rows) // (rows // GROUPS), lax.rem(at, rows // GROUPS)
    order = one_hot(((GROUPS - 1 - group) * SPLIT + k) * (rows // GROUPS) + row, SPLIT * rows)
    gate_side, up_side = dot(order, gate_side).astype(BF16), dot(order, up_side).astype(BF16)
    part = dot(gate_side, gate_ref[...], across) + dot(up_side, up_ref[...], across)
    each, fold = rows // GROUPS, parts[0].shape[1]
    for k in range(SPLIT):
        for group in range(GROUPS):
            start = (k * GROUPS + group) * each
            folds = [part[start : start + each, f * fold : (f + 1) * fold] for f in range(FOLDS)]
            parts[group * SPLIT + k][...] = jnp.concatenate(folds, axis=0).astype(BF16)


def grads_kernel(*refs):
    xs, ss = refs[:GROUPS], refs[GROUPS : 2 * GROUPS]
    sides_ref, outs, token_ref = refs[2 * GROUPS], refs[2 * GROUPS + 1 : -5], refs[-5]
    held, sems = refs[-4:-1], refs[-1]
    half, width = held[0].shape
    block = half // CHUNKS
    first = ((0,), (0,))
    copies = []
    for c in range(CHUNKS):
        part = slice(c * block, (c + 1) * block)
        x = jnp.concatenate([ref[:, part] for ref in xs], axis=0)
        s = jnp.concatenate([ref[:, part] for ref in ss], axis=0)
        for i, rows in enumerate((x, x, s)):
            held[i][part, :] = dot(rows, sides_ref[:, i * width : (i + 1) * width], first).astype(BF16)
            copy = pltpu.make_async_copy(
                held[i].at[pl.ds(c * block, block)], outs[i].at[pl.ds(c * block, block)], sems.at[i, c]
            )
            copy.start()
            copies.append(copy)
    for copy in copies:
        copy.wait()
    token_ref[...] = jnp.zeros(token_ref.shape, F32)


def sum_kernel(count, *refs):
    parts, outs = refs[:SPLIT], refs[SPLIT:]
    total = parts[0][...].astype(F32)
    for part in parts[1:]:
        total = total + part[...].astype(F32)
    total = total.astype(BF16)
    rows, fold = total.shape
    blocks = fold // 128
    each = CORES * MOST
    size = FOLDS * blocks * each
    row = iota((count * size, 1), 0)
    d, part, at = row // size, lax.rem(row // (blocks * each), FOLDS), lax.rem(row, each)
    block = lax.rem(row // each, blocks)
    wanted = (part * count + d) * each + at
    moved = jnp.zeros((count * size, 128), F32)
    for c in range(blocks):
        pick = one_hot(jnp.where(block == c, wanted, -1), rows)
        moved = moved + dot(pick, total[:, c * 128 : (c + 1) * 128])
    for d in range(count):
        outs[d][...] = moved[d * size : (d + 1) * size].astype(BF16)


def split_kernel(count, *refs):
    chunks, outs = refs[:count], refs[-CORES:]
    me = lax.axis_index("dp")
    size = chunks[0].shape[0]
    stacked = jnp.concatenate([chunk[...].astype(F32) for chunk in chunks], axis=0).astype(BF16)
    rows = count * 8
    out = iota((CORES * rows, 1), 0)
    q, d, slot = out // rows, lax.rem(out, rows) // 8, lax.rem(out, 8)
    first = jnp.where(slot < MOST, d * size + (q ^ me) * MOST + slot, -size)
    for c in range(outs[0].shape[1] // 128):
        picked = dot(one_hot(first + c * CORES * MOST, count * size), stacked).astype(BF16)
        for core in range(CORES):
            outs[core][:, c * 128 : (c + 1) * 128] = picked[core * rows : (core + 1) * rows]


def place_kernel(hot_ref, *refs):
    sources, out_ref = refs[:-1], refs[-1]
    me = lax.axis_index("dp")
    half = out_ref.shape[1] // CORES
    hot = hot_ref[...].astype(BF16)
    for q in range(CORES):
        rows = jnp.concatenate([ref[...] for ref in sources[q * GROUPS : (q + 1) * GROUPS]], axis=0)
        columns = pl.ds(pl.multiple_of((me ^ q) * half, 128), half)
        out_ref[:, columns] = dot(hot, rows, ((0,), (0,))).astype(BF16)


def like(shape, dtype):
    return jax.ShapeDtypeStruct(shape, dtype)


def body(
    layer_input, out_grad, routes, gate_values, keep_mask, gate_weight, up_weight, down_transposed
):
    devices = lax.axis_size("expert")
    live = devices // SPLIT
    tokens, model = layer_input.shape
    half, width = gate_weight.shape
    fold = half // FOLDS
    rows = CORES * live * MOST
    total = SPLIT * rows
    vmem, hbm = pl.BlockSpec(memory_space=pltpu.VMEM), pl.BlockSpec(memory_space=pltpu.HBM)

    def call(kernel, name, out_shape, operands, flops=0, moved=0):
        return pl.pallas_call(
            kernel,
            out_shape=out_shape,
            in_specs=[vmem] * len(operands),
            out_specs=jax.tree.map(lambda _: vmem, out_shape),
            compiler_params=params(),
            cost_estimate=cost(flops, moved) if flops else None,
            name=name,
        )(*operands)

    def swap_cores(array):
        return lax.ppermute(array, "dp", [(r, r ^ 1) for r in range(CORES)])

    def along_z(array, d):
        hop = [(i, (i // SPLIT ^ d) * SPLIT + i % SPLIT) for i in range(devices)]
        return lax.ppermute(array, "expert", hop)

    def in_plane(array, k):
        hop = []
        for i in range(devices):
            for r in range(CORES):
                hop.append((i * CORES + r, (i ^ near(k, r)) * CORES + r))
        return lax.ppermute(array, ("expert", "dp"), hop)

    gathered = like((live * SIDES * MOST, half), BF16)
    mine, other, hot = pl.pallas_call(
        lambda *refs: gather_kernel(live, *refs),
        out_shape=[gathered, gathered, like((live * 8, tokens), F32)],
        in_specs=[hbm] * 5,
        out_specs=[vmem] * 3,
        scratch_shapes=[
            pltpu.VMEM((TOP, tokens), jnp.int32),
            pltpu.VMEM((TOP, tokens), jnp.int32),
            pltpu.VMEM((TOP, tokens), F32),
            pltpu.VMEM((tokens, model), BF16),
            pltpu.VMEM((tokens, model), BF16),
            pltpu.SemaphoreType.DMA((5,)),
        ],
        compiler_params=params(FIRST_MIB),
        name="gather_rows",
    )(routes.T, keep_mask.T, gate_values.T, layer_input, out_grad)
    chunks = call(
        lambda *refs: chunk_kernel(live, *refs),
        "chunk_rows",
        [like((FOLDS * CORES * SIDES * MOST, fold), BF16)] * live,
        [mine, swap_cores(other)],
        1e10,
        2e7,
    )
    chunks = [chunks[0]] + [along_z(chunks[d], d) for d in range(1, live)]
    mines, others, xs, ss = [], [], [], []
    rows_in_group, planes = total // GROUPS, live // GROUPS
    for group in reversed(range(GROUPS)):
        rows_here = call(
            merge_kernel,
            "merge_rows",
            like((SIDES * rows // GROUPS, half), BF16),
            chunks[group * planes : (group + 1) * planes],
            1e8,
            1e6,
        )
        first, second = in_plane(rows_here, 1), in_plane(rows_here, 2)
        across = in_plane(first, 2)
        mine, x, s = call(
            partial_kernel,
            "partial_products",
            [like((rows_in_group, 3 * width), F32)] + [like((rows_in_group, half), BF16)] * SIDES,
            [rows_here, first, second, across, gate_weight, up_weight, down_transposed],
            6 * rows_in_group * half * width,
            6 * half * width,
        )
        mines.append(mine)
        others.append(swap_cores(mine))
        xs.append(x)
        ss.append(s)
    sided = call(
        sides_kernel,
        "sides_and_parts",
        [like((rows // GROUPS * FOLDS, fold), BF16)] * (GROUPS * SPLIT)
        + [like((total, 3 * width), BF16)],
        [*mines, *others, gate_weight, up_weight],
        4 * total * half * width,
        4 * half * width,
    )
    parts, sides = [], sided[-1]
    for group in range(GROUPS):
        mine = sided[group * SPLIT : (group + 1) * SPLIT]
        parts.append([mine[0]] + [in_plane(mine[k], k) for k in reversed(range(1, SPLIT))])
    gate_grad, up_grad, down_grad, token = pl.pallas_call(
        grads_kernel,
        out_shape=[like((half, width), BF16)] * 3 + [like((8, 128), F32)],
        in_specs=[vmem] * (2 * GROUPS + 1),
        out_specs=[hbm] * 3 + [vmem],
        scratch_shapes=[pltpu.VMEM((half, width), BF16)] * 3 + [pltpu.SemaphoreType.DMA((3, CHUNKS))],
        compiler_params=params(),
        cost_estimate=cost(6 * total * half * width, 6 * half * width + 4 * total * half),
        name="weight_grads",
    )(*xs, *ss, sides)
    back, over = [], []
    for group in range(GROUPS):
        ordered = group == TOKEN_GROUP
        chunks = call(
            functools.partial(sum_kernel, planes),
            "sum_parts",
            [like((half // 128 * CORES * MOST, 128), BF16)] * planes,
            parts[group],
        )
        first = group * planes
        chunks = [along_z(chunks[d], first + d) if first + d else chunks[0] for d in range(planes)]
        mine, other = call(
            functools.partial(split_kernel, planes),
            "split_rows",
            [like((planes * 8, half), BF16)] * CORES,
            chunks + [token] * ordered,
            1e10 if group else 1e8,
            1e6,
        )
        back.append(mine)
        over.append(swap_cores(other))
    input_grad = call(place_kernel, "place_rows", like((tokens, model), BF16), [hot, *back, *over])
    return (input_grad, gate_grad, up_grad, down_grad)


def solution(mesh):
    return jax.shard_map(
        body,
        mesh=mesh,
        in_specs=(
            P(("expert", "dp"), None),
            P(("expert", "dp"), None),
            P(("expert", "dp"), None),
            P(("expert", "dp"), None),
            P(("expert", "dp"), None),
            P("dp", "expert"),
            P("dp", "expert"),
            P("dp", "expert"),
        ),
        out_specs=(
            P(("expert", "dp"), None),
            P("dp", "expert"),
            P("dp", "expert"),
            P("dp", "expert"),
        ),
        check_vma=False,
    )
```

```python
import functools

import jax
import jax.numpy as jnp
from jax import lax
from jax.experimental import pallas as pl
from jax.experimental.pallas import tpu as pltpu
from jax.sharding import PartitionSpec as P

SPLIT = 4
MOST = 5
TOP = 8
SIDES = 2
CORES = 2
TOKEN_GROUP = 1
GROUPS = 2
FOLDS = 2
FIRST_MIB = 60
CHUNKS = 7

F32 = jnp.float32
BF16 = jnp.bfloat16


def params(mib=16):
    return pltpu.CompilerParams(vmem_limit_bytes=int(mib * 1024 * 1024))


def cost(flops, moved):
    return pl.CostEstimate(flops=int(flops), bytes_accessed=int(moved), transcendentals=0)


def iota(shape, axis):
    return lax.broadcasted_iota(jnp.int32, shape, axis)


def dot(a, b, dims=((1,), (0,))):
    return lax.dot_general(a, b, (dims, ((), ())), preferred_element_type=F32)


def one_hot(wanted, columns):
    return (iota((wanted.shape[0], columns), 1) == wanted).astype(F32).astype(BF16)


def pick_rows(routes, keep, gates, expert, slot, valid):
    rows, tokens = expert.shape[0], routes.shape[1]
    chosen = jnp.zeros((rows, tokens), F32)
    gate = jnp.zeros((rows, tokens), F32)
    for k in range(routes.shape[0]):
        hit = (routes[k : k + 1, :] == expert) & (keep[k : k + 1, :] == 1)
        chosen = jnp.where(hit, 1.0, chosen)
        gate = jnp.where(hit, gates[k : k + 1, :], gate)
    upto = (iota((tokens, tokens), 0) <= iota((tokens, tokens), 1)).astype(F32).astype(BF16)
    rank = dot(chosen.astype(BF16), upto)
    hot = (chosen > 0.5) & (rank == (slot + 1).astype(F32)) & valid
    return hot, gate


def near(k, core):
    if isinstance(core, int):
        return 3 - k if core and k in (1, 2) else k
    return jnp.where((core == 1) & (k > 0) & (k < 3), 3 - k, k)


def gather_kernel(live, *refs):
    sources, outs, local, sems = refs[:5], refs[5:-6], refs[-6:-1], refs[-1]
    copies = [pltpu.make_async_copy(sources[i], local[i], sems.at[i]) for i in range(5)]
    for copy in copies:
        copy.start()
    routes_ref, keep_ref, gates_ref, x_ref, o_ref = local
    place, me = lax.axis_index("expert") // SPLIT, lax.axis_index("dp")
    half = x_ref.shape[1] // CORES
    for copy in copies[:3]:
        copy.wait()
    routes, keep, gates = routes_ref[...], keep_ref[...], gates_ref[...]

    row = iota((live * 8, 1), 0)
    expert, slot = place ^ (row // 8), lax.rem(row, 8)
    hot, _ = pick_rows(routes, keep, gates, expert, slot, slot < MOST)
    outs[-1][...] = hot.astype(F32)

    row = iota((live * SIDES * MOST, 1), 0)
    expert = place ^ (row // (SIDES * MOST))
    side, slot = lax.rem(row // MOST, SIDES), lax.rem(row, MOST)
    hot, gate = pick_rows(routes, keep, gates, expert, slot, row >= 0)
    hot_x = (hot & (side == 0)).astype(F32).astype(BF16)
    hot_s = hot & (side == 1)
    scale = jnp.sum(jnp.where(hot_s, gate, 0.0), axis=1, keepdims=True)
    hot_s = hot_s.astype(F32).astype(BF16)
    for copy in copies[3:]:
        copy.wait()
    fold = half // FOLDS
    each = SIDES * MOST
    folds = []
    for f in range(CORES * FOLDS):
        start = (me ^ (f // FOLDS)) * half + f % FOLDS * fold
        columns = pl.ds(pl.multiple_of(start, 128), fold)
        folds.append(dot(hot_x, x_ref[:, columns]) + scale * dot(hot_s, o_ref[:, columns]))
    count = live // GROUPS * each
    for q in range(CORES):
        for f in range(FOLDS):
            outs[q][:, f * fold : (f + 1) * fold] = folds[q * FOLDS + f][:count].astype(BF16)
    for d in range(live // GROUPS, live):
        chunk = [rows[d * each : (d + 1) * each] for rows in folds]
        outs[CORES + d - live // GROUPS][...] = jnp.concatenate(chunk, axis=0).astype(BF16)


def chunk_kernel(planes, mine_ref, other_ref, *outs):
    me = lax.axis_index("dp")
    rows, half = mine_ref.shape
    fold = half // FOLDS
    each = SIDES * MOST
    stacked = jnp.concatenate([mine_ref[...], other_ref[...]], axis=0)
    size = FOLDS * CORES * each
    row = iota((planes * size, 1), 0)
    d, part, at = row // size, lax.rem(row // (CORES * each), FOLDS), lax.rem(row, CORES * each)
    wanted = (at // each ^ me) * rows + d * each + lax.rem(at, each)
    total = jnp.zeros((planes * size, fold), F32)
    for f in range(FOLDS):
        pick = one_hot(jnp.where(part == f, wanted, -1), CORES * rows)
        total = total + dot(pick, stacked[:, f * fold : (f + 1) * fold])
    total = total.astype(BF16)
    for d in range(planes):
        outs[d][...] = total[d * size : (d + 1) * size]


def merge_near_kernel(*refs):
    chunks, out_ref = refs[:-1], refs[-1]
    size, fold = chunks[0].shape
    stacked = jnp.concatenate([chunk[...] for chunk in chunks], axis=0)
    rows = len(chunks) * CORES * MOST
    out = iota((SIDES * rows, 1), 0)
    side, at = out // rows, lax.rem(out, rows)
    d, replica, slot = at // (CORES * MOST), lax.rem(at // MOST, CORES), lax.rem(at, MOST)
    for f in range(FOLDS):
        wanted = d * size + ((f * CORES + replica) * SIDES + side) * MOST + slot
        picked = dot(one_hot(wanted, len(chunks) * size), stacked)
        out_ref[:, f * fold : (f + 1) * fold] = picked.astype(BF16)


def merge_far_kernel(*refs):
    chunks, out_ref = refs[:-1], refs[-1]
    me = lax.axis_index("dp")
    planes, (size, fold) = len(chunks) // CORES, chunks[0].shape
    stacked = jnp.concatenate([chunk[...] for chunk in chunks], axis=0)
    rows = planes * CORES * MOST
    out = iota((SIDES * rows, 1), 0)
    side, at = out // rows, lax.rem(out, rows)
    d, replica, slot = at // (CORES * MOST), lax.rem(at // MOST, CORES), lax.rem(at, MOST)
    q = replica ^ me
    first = (q * planes + d) * size + (q * FOLDS * SIDES + side) * MOST + slot
    for f in range(FOLDS):
        picked = dot(one_hot(first + f * SIDES * MOST, len(chunks) * size), stacked)
        out_ref[:, f * fold : (f + 1) * fold] = picked.astype(BF16)


def partial_kernel(*refs):
    blocks, (gate_ref, up_ref, down_ref, out_ref), sided = refs[:SPLIT], refs[SPLIT:-2], refs[-2:]
    each, width = blocks[0].shape[0], gate_ref.shape[1]
    rows = each // SIDES
    stacked = jnp.concatenate([block[...] for block in blocks], axis=0)
    at = iota((SPLIT * rows, 1), 0)
    block = near(at // rows, lax.axis_index("dp"))
    for side in range(SIDES):
        wanted = block * each + side * rows + lax.rem(at, rows)
        sided[side][...] = dot(one_hot(wanted, SPLIT * each), stacked).astype(BF16)
    out_ref[:, :width] = dot(sided[0][...], gate_ref[...])
    out_ref[:, width : 2 * width] = dot(sided[0][...], up_ref[...])
    out_ref[:, 2 * width :] = dot(sided[1][...], down_ref[...])


def sides_kernel(*refs):
    sums, (gate_ref, up_ref), outs = refs[: 2 * GROUPS], refs[2 * GROUPS : 2 * GROUPS + 2], refs[2 * GROUPS + 2 :]
    parts, sides_ref = outs[:-1], outs[-1]
    width = gate_ref.shape[1]
    rows = parts[0].shape[0] // FOLDS * GROUPS
    total = [sums[i][...] + sums[GROUPS + i][...] for i in range(GROUPS)]
    total = jnp.concatenate(total, axis=0)
    pre_gate, pre_up = total[:, :width], total[:, width : 2 * width]
    hidden_grad = total[:, 2 * width :]
    sigma = jax.nn.sigmoid(pre_gate)
    activated = pre_gate * sigma
    slope = sigma * (1.0 + pre_gate * (1.0 - sigma))
    gate_side = (hidden_grad * pre_up * slope).astype(BF16)
    up_side = (hidden_grad * activated).astype(BF16)
    sides_ref[:, :width] = gate_side
    sides_ref[:, width : 2 * width] = up_side
    sides_ref[:, 2 * width :] = (activated * pre_up).astype(BF16)
    across = ((1,), (1,))
    at = iota((SPLIT * rows, 1), 0)
    k = near(at // rows, lax.axis_index("dp"))
    group, row = lax.rem(at, rows) // (rows // GROUPS), lax.rem(at, rows // GROUPS)
    order = one_hot(((GROUPS - 1 - group) * SPLIT + k) * (rows // GROUPS) + row, SPLIT * rows)
    gate_side, up_side = dot(order, gate_side).astype(BF16), dot(order, up_side).astype(BF16)
    part = dot(gate_side, gate_ref[...], across) + dot(up_side, up_ref[...], across)
    each, fold = rows // GROUPS, parts[0].shape[1]
    for k in range(SPLIT):
        for group in range(GROUPS):
            start = (k * GROUPS + group) * each
            folds = [part[start : start + each, f * fold : (f + 1) * fold] for f in range(FOLDS)]
            parts[group * SPLIT + k][...] = jnp.concatenate(folds, axis=0).astype(BF16)


def grads_kernel(*refs):
    xs, ss = refs[:GROUPS], refs[GROUPS : 2 * GROUPS]
    sides_ref, outs, token_ref = refs[2 * GROUPS], refs[2 * GROUPS + 1 : -5], refs[-5]
    held, sems = refs[-4:-1], refs[-1]
    half, width = held[0].shape
    block = half // CHUNKS
    first = ((0,), (0,))
    copies = []
    for c in range(CHUNKS):
        part = slice(c * block, (c + 1) * block)
        x = jnp.concatenate([ref[:, part] for ref in xs], axis=0)
        s = jnp.concatenate([ref[:, part] for ref in ss], axis=0)
        for i, rows in enumerate((x, x, s)):
            held[i][part, :] = dot(rows, sides_ref[:, i * width : (i + 1) * width], first).astype(BF16)
            copy = pltpu.make_async_copy(
                held[i].at[pl.ds(c * block, block)], outs[i].at[pl.ds(c * block, block)], sems.at[i, c]
            )
            copy.start()
            copies.append(copy)
    for copy in copies:
        copy.wait()
    token_ref[...] = jnp.zeros(token_ref.shape, F32)


def sum_kernel(count, *refs):
    parts, outs = refs[:SPLIT], refs[SPLIT:]
    total = parts[0][...].astype(F32)
    for part in parts[1:]:
        total = total + part[...].astype(F32)
    total = total.astype(BF16)
    rows, fold = total.shape
    blocks = fold // 128
    each = CORES * MOST
    size = FOLDS * blocks * each
    row = iota((count * size, 1), 0)
    d, part, at = row // size, lax.rem(row // (blocks * each), FOLDS), lax.rem(row, each)
    block = lax.rem(row // each, blocks)
    wanted = (part * count + d) * each + at
    moved = jnp.zeros((count * size, 128), F32)
    for c in range(blocks):
        pick = one_hot(jnp.where(block == c, wanted, -1), rows)
        moved = moved + dot(pick, total[:, c * 128 : (c + 1) * 128])
    for d in range(count):
        outs[d][...] = moved[d * size : (d + 1) * size].astype(BF16)


def split_kernel(count, *refs):
    chunks, outs = refs[:count], refs[-CORES:]
    me = lax.axis_index("dp")
    size = chunks[0].shape[0]
    stacked = jnp.concatenate([chunk[...].astype(F32) for chunk in chunks], axis=0).astype(BF16)
    rows = count * 8
    out = iota((CORES * rows, 1), 0)
    q, d, slot = out // rows, lax.rem(out, rows) // 8, lax.rem(out, 8)
    first = jnp.where(slot < MOST, d * size + (q ^ me) * MOST + slot, -size)
    for c in range(outs[0].shape[1] // 128):
        picked = dot(one_hot(first + c * CORES * MOST, count * size), stacked).astype(BF16)
        for core in range(CORES):
            outs[core][:, c * 128 : (c + 1) * 128] = picked[core * rows : (core + 1) * rows]


def place_kernel(hot_ref, *refs):
    sources, out_ref = refs[:-1], refs[-1]
    me = lax.axis_index("dp")
    half = out_ref.shape[1] // CORES
    hot = hot_ref[...].astype(BF16)
    for q in range(CORES):
        rows = jnp.concatenate([ref[...] for ref in sources[q * GROUPS : (q + 1) * GROUPS]], axis=0)
        columns = pl.ds(pl.multiple_of((me ^ q) * half, 128), half)
        out_ref[:, columns] = dot(hot, rows, ((0,), (0,))).astype(BF16)


def like(shape, dtype):
    return jax.ShapeDtypeStruct(shape, dtype)


def body(
    layer_input, out_grad, routes, gate_values, keep_mask, gate_weight, up_weight, down_transposed
):
    devices = lax.axis_size("expert")
    live = devices // SPLIT
    tokens, model = layer_input.shape
    half, width = gate_weight.shape
    fold = half // FOLDS
    rows = CORES * live * MOST
    total = SPLIT * rows
    planes = live // GROUPS
    vmem, hbm = pl.BlockSpec(memory_space=pltpu.VMEM), pl.BlockSpec(memory_space=pltpu.HBM)

    def call(kernel, name, out_shape, operands, flops=0, moved=0):
        return pl.pallas_call(
            kernel,
            out_shape=out_shape,
            in_specs=[vmem] * len(operands),
            out_specs=jax.tree.map(lambda _: vmem, out_shape),
            compiler_params=params(),
            cost_estimate=cost(flops, moved) if flops else None,
            name=name,
        )(*operands)

    def swap_cores(array):
        return lax.ppermute(array, "dp", [(r, r ^ 1) for r in range(CORES)])

    def along_z(array, d):
        hop = [(i, (i // SPLIT ^ d) * SPLIT + i % SPLIT) for i in range(devices)]
        return lax.ppermute(array, "expert", hop)

    def in_plane(array, k):
        hop = []
        for i in range(devices):
            for r in range(CORES):
                hop.append((i * CORES + r, (i ^ near(k, r)) * CORES + r))
        return lax.ppermute(array, ("expert", "dp"), hop)

    size = FOLDS * CORES * SIDES * MOST
    near_rows = like((planes * SIDES * MOST, half), BF16)
    mine, other, *far, hot = pl.pallas_call(
        functools.partial(gather_kernel, live),
        out_shape=[near_rows] * CORES
        + [like((size, fold), BF16)] * (live - planes)
        + [like((live * 8, tokens), F32)],
        in_specs=[hbm] * 5,
        out_specs=[vmem] * (CORES + live - planes + 1),
        scratch_shapes=[
            pltpu.VMEM((TOP, tokens), jnp.int32),
            pltpu.VMEM((TOP, tokens), jnp.int32),
            pltpu.VMEM((TOP, tokens), F32),
            pltpu.VMEM((tokens, model), BF16),
            pltpu.VMEM((tokens, model), BF16),
            pltpu.SemaphoreType.DMA((5,)),
        ],
        compiler_params=params(FIRST_MIB),
        name="gather_rows",
    )(routes.T, keep_mask.T, gate_values.T, layer_input, out_grad)
    far = [along_z(chunk, planes + d) for d, chunk in enumerate(far)]
    near_chunks = call(
        functools.partial(chunk_kernel, planes),
        "chunk_rows",
        [like((size, fold), BF16)] * planes,
        [mine, swap_cores(other)],
        1e10,
        2e7,
    )
    near_chunks = [near_chunks[0]] + [along_z(near_chunks[d], d) for d in range(1, planes)]
    mines, others, xs, ss = [], [], [], []
    rows_in_group = total // GROUPS
    for group in reversed(range(GROUPS)):
        here = far + [swap_cores(chunk) for chunk in far] if group else near_chunks
        rows_here = call(
            merge_far_kernel if group else merge_near_kernel,
            "merge_rows",
            like((SIDES * rows // GROUPS, half), BF16),
            here,
            1e8,
            1e6,
        )
        first, second = in_plane(rows_here, 1), in_plane(rows_here, 2)
        across = in_plane(first, 2)
        mine, x, s = call(
            partial_kernel,
            "partial_products",
            [like((rows_in_group, 3 * width), F32)] + [like((rows_in_group, half), BF16)] * SIDES,
            [rows_here, first, second, across, gate_weight, up_weight, down_transposed],
            6 * rows_in_group * half * width,
            6 * half * width,
        )
        mines.append(mine)
        others.append(swap_cores(mine))
        xs.append(x)
        ss.append(s)
    sided = call(
        sides_kernel,
        "sides_and_parts",
        [like((rows // GROUPS * FOLDS, fold), BF16)] * (GROUPS * SPLIT)
        + [like((total, 3 * width), BF16)],
        [*mines, *others, gate_weight, up_weight],
        4 * total * half * width,
        4 * half * width,
    )
    parts, sides = [], sided[-1]
    for group in range(GROUPS):
        mine = sided[group * SPLIT : (group + 1) * SPLIT]
        parts.append([mine[0]] + [in_plane(mine[k], k) for k in reversed(range(1, SPLIT))])
    gate_grad, up_grad, down_grad, token = pl.pallas_call(
        grads_kernel,
        out_shape=[like((half, width), BF16)] * 3 + [like((8, 128), F32)],
        in_specs=[vmem] * (2 * GROUPS + 1),
        out_specs=[hbm] * 3 + [vmem],
        scratch_shapes=[pltpu.VMEM((half, width), BF16)] * 3 + [pltpu.SemaphoreType.DMA((3, CHUNKS))],
        compiler_params=params(),
        cost_estimate=cost(6 * total * half * width, 6 * half * width + 4 * total * half),
        name="weight_grads",
    )(*xs, *ss, sides)
    back, over = [], []
    for group in range(GROUPS):
        ordered = group == TOKEN_GROUP
        chunks = call(
            functools.partial(sum_kernel, planes),
            "sum_parts",
            [like((half // 128 * CORES * MOST, 128), BF16)] * planes,
            parts[group],
        )
        first = group * planes
        chunks = [along_z(chunks[d], first + d) if first + d else chunks[0] for d in range(planes)]
        mine, other = call(
            functools.partial(split_kernel, planes),
            "split_rows",
            [like((planes * 8, half), BF16)] * CORES,
            chunks + [token] * ordered,
            1e10 if group else 1e8,
            1e6,
        )
        back.append(mine)
        over.append(swap_cores(other))
    input_grad = call(place_kernel, "place_rows", like((tokens, model), BF16), [hot, *back, *over])
    return (input_grad, gate_grad, up_grad, down_grad)


def solution(mesh):
    return jax.shard_map(
        body,
        mesh=mesh,
        in_specs=(
            P(("expert", "dp"), None),
            P(("expert", "dp"), None),
            P(("expert", "dp"), None),
            P(("expert", "dp"), None),
            P(("expert", "dp"), None),
            P("dp", "expert"),
            P("dp", "expert"),
            P("dp", "expert"),
        ),
        out_specs=(
            P(("expert", "dp"), None),
            P("dp", "expert"),
            P("dp", "expert"),
            P("dp", "expert"),
        ),
        check_vma=False,
    )
```

```python
import functools

import jax
import jax.numpy as jnp
from jax import lax
from jax.experimental import pallas as pl
from jax.experimental.pallas import tpu as pltpu
from jax.sharding import PartitionSpec as P

SPLIT = 4
MOST = 5
TOP = 8
SIDES = 2
CORES = 2
TOKEN_GROUP = 1
OWN_COST = 1e10
GROUPS = 2
FOLDS = 2
FIRST_MIB = 60
CHUNKS = 7

F32 = jnp.float32
BF16 = jnp.bfloat16


def params(mib=16):
    return pltpu.CompilerParams(vmem_limit_bytes=int(mib * 1024 * 1024))


def cost(flops, moved):
    return pl.CostEstimate(flops=int(flops), bytes_accessed=int(moved), transcendentals=0)


def iota(shape, axis):
    return lax.broadcasted_iota(jnp.int32, shape, axis)


def dot(a, b, dims=((1,), (0,))):
    return lax.dot_general(a, b, (dims, ((), ())), preferred_element_type=F32)


def one_hot(wanted, columns):
    return (iota((wanted.shape[0], columns), 1) == wanted).astype(F32).astype(BF16)


def pick_rows(routes, keep, gates, expert, slot, valid):
    rows, tokens = expert.shape[0], routes.shape[1]
    chosen = jnp.zeros((rows, tokens), F32)
    gate = jnp.zeros((rows, tokens), F32)
    for k in range(routes.shape[0]):
        hit = (routes[k : k + 1, :] == expert) & (keep[k : k + 1, :] == 1)
        chosen = jnp.where(hit, 1.0, chosen)
        gate = jnp.where(hit, gates[k : k + 1, :], gate)
    upto = (iota((tokens, tokens), 0) <= iota((tokens, tokens), 1)).astype(F32).astype(BF16)
    rank = dot(chosen.astype(BF16), upto)
    hot = (chosen > 0.5) & (rank == (slot + 1).astype(F32)) & valid
    return hot, gate


def near(k, core):
    if isinstance(core, int):
        return 3 - k if core and k in (1, 2) else k
    return jnp.where((core == 1) & (k > 0) & (k < 3), 3 - k, k)


def gather_kernel(live, *refs):
    sources, outs, local, sems = refs[:5], refs[5:-6], refs[-6:-1], refs[-1]
    copies = [pltpu.make_async_copy(sources[i], local[i], sems.at[i]) for i in range(5)]
    for copy in copies:
        copy.start()
    routes_ref, keep_ref, gates_ref, x_ref, o_ref = local
    place, me = lax.axis_index("expert") // SPLIT, lax.axis_index("dp")
    half = x_ref.shape[1] // CORES
    for copy in copies[:3]:
        copy.wait()
    routes, keep, gates = routes_ref[...], keep_ref[...], gates_ref[...]

    row = iota((live * 8, 1), 0)
    expert, slot = place ^ (row // 8), lax.rem(row, 8)
    hot, _ = pick_rows(routes, keep, gates, expert, slot, slot < MOST)
    outs[-1][...] = hot.astype(F32)

    row = iota((live * SIDES * MOST, 1), 0)
    expert = place ^ (row // (SIDES * MOST))
    side, slot = lax.rem(row // MOST, SIDES), lax.rem(row, MOST)
    hot, gate = pick_rows(routes, keep, gates, expert, slot, row >= 0)
    hot_x = (hot & (side == 0)).astype(F32).astype(BF16)
    hot_s = hot & (side == 1)
    scale = jnp.sum(jnp.where(hot_s, gate, 0.0), axis=1, keepdims=True)
    hot_s = hot_s.astype(F32).astype(BF16)
    for copy in copies[3:]:
        copy.wait()
    fold = half // FOLDS
    each = SIDES * MOST
    folds = []
    for f in range(CORES * FOLDS):
        start = (me ^ (f // FOLDS)) * half + f % FOLDS * fold
        columns = pl.ds(pl.multiple_of(start, 128), fold)
        folds.append(dot(hot_x, x_ref[:, columns]) + scale * dot(hot_s, o_ref[:, columns]))
    for q in range(CORES):
        for f in range(FOLDS):
            outs[q][:, f * fold : (f + 1) * fold] = folds[q * FOLDS + f][:each].astype(BF16)
    for d in range(1, live):
        chunk = [rows[d * each : (d + 1) * each] for rows in folds]
        outs[CORES + d - 1][...] = jnp.concatenate(chunk, axis=0).astype(BF16)


def own_kernel(mine_ref, other_ref, out_ref):
    me = lax.axis_index("dp")
    rows, half = mine_ref.shape
    fold = half // FOLDS
    stacked = jnp.concatenate([mine_ref[...].astype(F32), other_ref[...].astype(F32)], axis=0).astype(BF16)
    out = iota((CORES * rows, 1), 0)
    side, replica, slot = out // (CORES * MOST), lax.rem(out // MOST, CORES), lax.rem(out, MOST)
    picked = dot(one_hot((replica ^ me) * rows + side * MOST + slot, CORES * rows), stacked)
    folds = [picked[:, f * fold : (f + 1) * fold] for f in range(FOLDS)]
    out_ref[...] = jnp.concatenate(folds, axis=0).astype(BF16)


def merge_kernel(*refs):
    chunks, out_ref = refs[:-1], refs[-1]
    me = lax.axis_index("dp")
    planes, size = len(chunks) // CORES, chunks[0].shape[0]
    stacked = jnp.concatenate([chunk[...] for chunk in chunks], axis=0)
    rows = planes * CORES * MOST
    out = iota((out_ref.shape[0], 1), 0)
    f, side, at = out // (SIDES * rows), lax.rem(out // rows, SIDES), lax.rem(out, rows)
    d, replica, slot = at // (CORES * MOST), lax.rem(at // MOST, CORES), lax.rem(at, MOST)
    q = replica ^ me
    wanted = (q * planes + d) * size + ((q * FOLDS + f) * SIDES + side) * MOST + slot
    out_ref[...] = dot(one_hot(wanted, len(chunks) * size), stacked).astype(BF16)


def partial_kernel(*refs):
    blocks, (gate_ref, up_ref, down_ref, out_ref), sided = refs[:SPLIT], refs[SPLIT:-2], refs[-2:]
    (each, fold), width = blocks[0].shape, gate_ref.shape[1]
    rows = each // (FOLDS * SIDES)
    stacked = jnp.concatenate([block[...] for block in blocks], axis=0)
    at = iota((SPLIT * rows, 1), 0)
    block = near(at // rows, lax.axis_index("dp"))
    for side in range(SIDES):
        for f in range(FOLDS):
            wanted = (f * SIDES + side) * rows + lax.rem(at, rows)
            if SPLIT * each <= 1024:
                picked = dot(one_hot(block * each + wanted, SPLIT * each), stacked)
            else:
                picked = jnp.zeros((SPLIT * rows, fold), F32)
                for b in range(SPLIT):
                    here = jnp.where(block == b, wanted, -1)
                    picked = picked + dot(one_hot(here, each), blocks[b][...])
            sided[side][:, f * fold : (f + 1) * fold] = picked.astype(BF16)
    out_ref[:, :width] = dot(sided[0][...], gate_ref[...])
    out_ref[:, width : 2 * width] = dot(sided[0][...], up_ref[...])
    out_ref[:, 2 * width :] = dot(sided[1][...], down_ref[...])


def sides_kernel(*refs):
    sums, (gate_ref, up_ref), outs = refs[: 2 * GROUPS], refs[2 * GROUPS : 2 * GROUPS + 2], refs[2 * GROUPS + 2 :]
    parts, sides_ref = outs[:-1], outs[-1]
    width = gate_ref.shape[1]
    rows = parts[0].shape[0] // FOLDS * GROUPS
    total = [sums[i][...] + sums[GROUPS + i][...] for i in range(GROUPS)]
    total = jnp.concatenate(total, axis=0)
    pre_gate, pre_up = total[:, :width], total[:, width : 2 * width]
    hidden_grad = total[:, 2 * width :]
    sigma = jax.nn.sigmoid(pre_gate)
    activated = pre_gate * sigma
    slope = sigma * (1.0 + pre_gate * (1.0 - sigma))
    gate_side = (hidden_grad * pre_up * slope).astype(BF16)
    up_side = (hidden_grad * activated).astype(BF16)
    sides_ref[:, :width] = gate_side
    sides_ref[:, width : 2 * width] = up_side
    sides_ref[:, 2 * width :] = (activated * pre_up).astype(BF16)
    across = ((1,), (1,))
    at = iota((SPLIT * rows, 1), 0)
    k = near(at // rows, lax.axis_index("dp"))
    each, row = CORES * MOST, lax.rem(at, rows)
    others = rows - each
    source = jnp.where(row < each, SPLIT * others + k * each + row, k * others + row - each)
    order = one_hot(source, SPLIT * rows)
    gate_side, up_side = dot(order, gate_side).astype(BF16), dot(order, up_side).astype(BF16)
    part = dot(gate_side, gate_ref[...], across) + dot(up_side, up_ref[...], across)
    each, fold = rows // GROUPS, parts[0].shape[1]
    for k in range(SPLIT):
        for group in range(GROUPS):
            start = (k * GROUPS + group) * each
            folds = [part[start : start + each, f * fold : (f + 1) * fold] for f in range(FOLDS)]
            parts[group * SPLIT + k][...] = jnp.concatenate(folds, axis=0).astype(BF16)


def grads_kernel(*refs):
    xs, ss = refs[:GROUPS], refs[GROUPS : 2 * GROUPS]
    sides_ref, outs, token_ref = refs[2 * GROUPS], refs[2 * GROUPS + 1 : -5], refs[-5]
    held, sems = refs[-4:-1], refs[-1]
    half, width = held[0].shape
    block = half // CHUNKS
    first = ((0,), (0,))
    copies = []
    for c in range(CHUNKS):
        part = slice(c * block, (c + 1) * block)
        x = jnp.concatenate([ref[:, part] for ref in xs], axis=0)
        s = jnp.concatenate([ref[:, part] for ref in ss], axis=0)
        for i, rows in enumerate((x, x, s)):
            held[i][part, :] = dot(rows, sides_ref[:, i * width : (i + 1) * width], first).astype(BF16)
            copy = pltpu.make_async_copy(
                held[i].at[pl.ds(c * block, block)], outs[i].at[pl.ds(c * block, block)], sems.at[i, c]
            )
            copy.start()
            copies.append(copy)
    for copy in copies:
        copy.wait()
    token_ref[...] = jnp.zeros(token_ref.shape, F32)


def sum_kernel(count, *refs):
    parts, outs = refs[:SPLIT], refs[SPLIT:]
    total = parts[0][...].astype(F32)
    for part in parts[1:]:
        total = total + part[...].astype(F32)
    total = total.astype(BF16)
    rows, fold = total.shape
    blocks = fold // 128
    each = CORES * MOST
    size = FOLDS * blocks * each
    row = iota((count * size, 1), 0)
    d, part, at = row // size, lax.rem(row // (blocks * each), FOLDS), lax.rem(row, each)
    block = lax.rem(row // each, blocks)
    wanted = (part * count + d) * each + at
    moved = jnp.zeros((count * size, 128), F32)
    for c in range(blocks):
        pick = one_hot(jnp.where(block == c, wanted, -1), rows)
        moved = moved + dot(pick, total[:, c * 128 : (c + 1) * 128])
    for d in range(count):
        outs[d][...] = moved[d * size : (d + 1) * size].astype(BF16)


def split_kernel(count, *refs):
    chunks, outs = refs[:count], refs[-CORES:]
    me = lax.axis_index("dp")
    size = chunks[0].shape[0]
    stacked = jnp.concatenate([chunk[...].astype(F32) for chunk in chunks], axis=0).astype(BF16)
    rows = count * 8
    out = iota((CORES * rows, 1), 0)
    q, d, slot = out // rows, lax.rem(out, rows) // 8, lax.rem(out, 8)
    first = jnp.where(slot < MOST, d * size + (q ^ me) * MOST + slot, -size)
    for c in range(outs[0].shape[1] // 128):
        picked = dot(one_hot(first + c * CORES * MOST, count * size), stacked).astype(BF16)
        for core in range(CORES):
            outs[core][:, c * 128 : (c + 1) * 128] = picked[core * rows : (core + 1) * rows]


def place_kernel(hot_ref, *refs):
    sources, out_ref = refs[:-1], refs[-1]
    me = lax.axis_index("dp")
    half = out_ref.shape[1] // CORES
    hot = hot_ref[...].astype(BF16)
    for q in range(CORES):
        rows = jnp.concatenate([ref[...] for ref in sources[q * GROUPS : (q + 1) * GROUPS]], axis=0)
        columns = pl.ds(pl.multiple_of((me ^ q) * half, 128), half)
        out_ref[:, columns] = dot(hot, rows, ((0,), (0,))).astype(BF16)


def like(shape, dtype):
    return jax.ShapeDtypeStruct(shape, dtype)


def body(
    layer_input, out_grad, routes, gate_values, keep_mask, gate_weight, up_weight, down_transposed
):
    devices = lax.axis_size("expert")
    live = devices // SPLIT
    tokens, model = layer_input.shape
    half, width = gate_weight.shape
    fold = half // FOLDS
    rows = CORES * live * MOST
    total = SPLIT * rows
    planes = live // GROUPS
    vmem, hbm = pl.BlockSpec(memory_space=pltpu.VMEM), pl.BlockSpec(memory_space=pltpu.HBM)

    def call(kernel, name, out_shape, operands, flops=0, moved=0):
        return pl.pallas_call(
            kernel,
            out_shape=out_shape,
            in_specs=[vmem] * len(operands),
            out_specs=jax.tree.map(lambda _: vmem, out_shape),
            compiler_params=params(min(60, 4 * live)),
            cost_estimate=cost(flops, moved) if flops else None,
            name=name,
        )(*operands)

    def swap_cores(array):
        return lax.ppermute(array, "dp", [(r, r ^ 1) for r in range(CORES)])

    def along_z(array, d):
        hop = [(i, (i // SPLIT ^ d) * SPLIT + i % SPLIT) for i in range(devices)]
        return lax.ppermute(array, "expert", hop)

    def in_plane(array, k):
        hop = []
        for i in range(devices):
            for r in range(CORES):
                hop.append((i * CORES + r, (i ^ near(k, r)) * CORES + r))
        return lax.ppermute(array, ("expert", "dp"), hop)

    size = FOLDS * CORES * SIDES * MOST
    own_rows = like((SIDES * MOST, half), BF16)
    mine, other, *far, hot = pl.pallas_call(
        functools.partial(gather_kernel, live),
        out_shape=[own_rows] * CORES
        + [like((size, fold), BF16)] * (live - 1)
        + [like((live * 8, tokens), F32)],
        in_specs=[hbm] * 5,
        out_specs=[vmem] * (CORES + live),
        scratch_shapes=[
            pltpu.VMEM((TOP, tokens), jnp.int32),
            pltpu.VMEM((TOP, tokens), jnp.int32),
            pltpu.VMEM((TOP, tokens), F32),
            pltpu.VMEM((tokens, model), BF16),
            pltpu.VMEM((tokens, model), BF16),
            pltpu.SemaphoreType.DMA((5,)),
        ],
        compiler_params=params(FIRST_MIB),
        name="gather_rows",
    )(routes.T, keep_mask.T, gate_values.T, layer_input, out_grad)
    moved = {d: along_z(far[d - 1], d) for d in [*range(2, live), 1]}
    far = [moved[d] for d in range(1, live)]
    mines, others, xs, ss = [], [], [], []
    first = second = across = rows_here = None
    for group in range(GROUPS):
        count = live - 1 if group else 1
        rows_in_group = SPLIT * CORES * MOST * count
        rows_in = far + [swap_cores(chunk) for chunk in far] if group else [mine, swap_cores(other)]
        if group:
            rows_in = lax.optimization_barrier((rows_in, (second, across)))[0]
        rows_here = call(
            merge_kernel if group else own_kernel,
            "merge_rows",
            like((size * count, fold), BF16),
            rows_in,
            1e8 if group else OWN_COST,
            1e6,
        )
        first, second = in_plane(rows_here, 1), in_plane(rows_here, 2)
        across = in_plane(first, 2)
        product, x, s = call(
            partial_kernel,
            "partial_products",
            [like((rows_in_group, 3 * width), F32)] + [like((rows_in_group, half), BF16)] * SIDES,
            [rows_here, first, second, across, gate_weight, up_weight, down_transposed],
            6 * rows_in_group * half * width,
            6 * half * width,
        )
        mines.append(product)
        others.append(swap_cores(product))
        xs.append(x)
        ss.append(s)
    mines, others, xs, ss = mines[::-1], others[::-1], xs[::-1], ss[::-1]
    sided = call(
        sides_kernel,
        "sides_and_parts",
        [like((rows // GROUPS * FOLDS, fold), BF16)] * (GROUPS * SPLIT)
        + [like((total, 3 * width), BF16)],
        [*mines, *others, gate_weight, up_weight],
        4 * total * half * width,
        4 * half * width,
    )
    parts, sides = [], sided[-1]
    for group in range(GROUPS):
        mine = sided[group * SPLIT : (group + 1) * SPLIT]
        parts.append([mine[0]] + [in_plane(mine[k], k) for k in reversed(range(1, SPLIT))])
    gate_grad, up_grad, down_grad, token = pl.pallas_call(
        grads_kernel,
        out_shape=[like((half, width), BF16)] * 3 + [like((8, 128), F32)],
        in_specs=[vmem] * (2 * GROUPS + 1),
        out_specs=[hbm] * 3 + [vmem],
        scratch_shapes=[pltpu.VMEM((half, width), BF16)] * 3 + [pltpu.SemaphoreType.DMA((3, CHUNKS))],
        compiler_params=params(),
        cost_estimate=cost(6 * total * half * width, 6 * half * width + 4 * total * half),
        name="weight_grads",
    )(*xs, *ss, sides)
    back, over = [], []
    for group in range(GROUPS):
        ordered = group == TOKEN_GROUP
        chunks = call(
            functools.partial(sum_kernel, planes),
            "sum_parts",
            [like((half // 128 * CORES * MOST, 128), BF16)] * planes,
            parts[group],
        )
        first = group * planes
        chunks = [along_z(chunks[d], first + d) if first + d else chunks[0] for d in range(planes)]
        mine, other = call(
            functools.partial(split_kernel, planes),
            "split_rows",
            [like((planes * 8, half), BF16)] * CORES,
            chunks + [token] * ordered,
            1e10 if group else 1e8,
            1e6,
        )
        back.append(mine)
        over.append(swap_cores(other))
    input_grad = call(place_kernel, "place_rows", like((tokens, model), BF16), [hot, *back, *over])
    return (input_grad, gate_grad, up_grad, down_grad)


def solution(mesh):
    return jax.shard_map(
        body,
        mesh=mesh,
        in_specs=(
            P(("expert", "dp"), None),
            P(("expert", "dp"), None),
            P(("expert", "dp"), None),
            P(("expert", "dp"), None),
            P(("expert", "dp"), None),
            P("dp", "expert"),
            P("dp", "expert"),
            P("dp", "expert"),
        ),
        out_specs=(
            P(("expert", "dp"), None),
            P("dp", "expert"),
            P("dp", "expert"),
            P("dp", "expert"),
        ),
        check_vma=False,
    )
```

```python
import functools

import jax
import jax.numpy as jnp
from jax import lax
from jax.experimental import pallas as pl
from jax.experimental.pallas import tpu as pltpu
from jax.sharding import PartitionSpec as P

SPLIT = 4
MOST = 5
TOP = 8
SIDES = 2
CORES = 2
TOKEN_GROUP = 1
GROUPS = 2
FOLDS = 2
FIRST_MIB = 60
CHUNKS = 7

F32 = jnp.float32
BF16 = jnp.bfloat16


def params(mib=16):
    return pltpu.CompilerParams(vmem_limit_bytes=int(mib * 1024 * 1024))


def cost(flops, moved):
    return pl.CostEstimate(flops=int(flops), bytes_accessed=int(moved), transcendentals=0)


def iota(shape, axis):
    return lax.broadcasted_iota(jnp.int32, shape, axis)


def dot(a, b, dims=((1,), (0,))):
    return lax.dot_general(a, b, (dims, ((), ())), preferred_element_type=F32)


def one_hot(wanted, columns):
    return (iota((wanted.shape[0], columns), 1) == wanted).astype(F32).astype(BF16)


def pick_rows(routes, keep, gates, expert, slot, valid):
    rows, tokens = expert.shape[0], routes.shape[1]
    chosen = jnp.zeros((rows, tokens), F32)
    gate = jnp.zeros((rows, tokens), F32)
    for k in range(routes.shape[0]):
        hit = (routes[k : k + 1, :] == expert) & (keep[k : k + 1, :] == 1)
        chosen = jnp.where(hit, 1.0, chosen)
        gate = jnp.where(hit, gates[k : k + 1, :], gate)
    upto = (iota((tokens, tokens), 0) <= iota((tokens, tokens), 1)).astype(F32).astype(BF16)
    rank = dot(chosen.astype(BF16), upto)
    hot = (chosen > 0.5) & (rank == (slot + 1).astype(F32)) & valid
    return hot, gate


def near(k, core):
    if isinstance(core, int):
        return 3 - k if core and k in (1, 2) else k
    return jnp.where((core == 1) & (k > 0) & (k < 3), 3 - k, k)


def gather_kernel(live, *refs):
    sources, outs, local, sems = refs[:5], refs[5:-6], refs[-6:-1], refs[-1]
    copies = [pltpu.make_async_copy(sources[i], local[i], sems.at[i]) for i in range(5)]
    for copy in copies:
        copy.start()
    routes_ref, keep_ref, gates_ref, x_ref, o_ref = local
    place, me = lax.axis_index("expert") // SPLIT, lax.axis_index("dp")
    half = x_ref.shape[1] // CORES
    for copy in copies[:3]:
        copy.wait()
    routes, keep, gates = routes_ref[...], keep_ref[...], gates_ref[...]

    row = iota((live * 8, 1), 0)
    expert, slot = place ^ (row // 8), lax.rem(row, 8)
    hot, _ = pick_rows(routes, keep, gates, expert, slot, slot < MOST)
    outs[-1][...] = hot.astype(F32)

    row = iota((live * SIDES * MOST, 1), 0)
    expert = place ^ (row // (SIDES * MOST))
    side, slot = lax.rem(row // MOST, SIDES), lax.rem(row, MOST)
    hot, gate = pick_rows(routes, keep, gates, expert, slot, row >= 0)
    hot_x = (hot & (side == 0)).astype(F32).astype(BF16)
    hot_s = hot & (side == 1)
    scale = jnp.sum(jnp.where(hot_s, gate, 0.0), axis=1, keepdims=True)
    hot_s = hot_s.astype(F32).astype(BF16)
    for copy in copies[3:]:
        copy.wait()
    fold = half // FOLDS
    each = SIDES * MOST
    folds = []
    for f in range(CORES * FOLDS):
        start = (me ^ (f // FOLDS)) * half + f % FOLDS * fold
        columns = pl.ds(pl.multiple_of(start, 128), fold)
        folds.append(dot(hot_x, x_ref[:, columns]) + scale * dot(hot_s, o_ref[:, columns]))
    count = live // GROUPS * each
    for q in range(CORES):
        for f in range(FOLDS):
            outs[q][:, f * fold : (f + 1) * fold] = folds[q * FOLDS + f][:count].astype(BF16)
    for d in range(live // GROUPS, live):
        chunk = [rows[d * each : (d + 1) * each] for rows in folds]
        outs[CORES + d - live // GROUPS][...] = jnp.concatenate(chunk, axis=0).astype(BF16)


def chunk_kernel(planes, mine_ref, other_ref, *outs):
    me = lax.axis_index("dp")
    rows, half = mine_ref.shape
    fold = half // FOLDS
    each = SIDES * MOST
    stacked = jnp.concatenate([mine_ref[...], other_ref[...]], axis=0)
    size = FOLDS * CORES * each
    row = iota((planes * size, 1), 0)
    d, part, at = row // size, lax.rem(row // (CORES * each), FOLDS), lax.rem(row, CORES * each)
    wanted = (at // each ^ me) * rows + d * each + lax.rem(at, each)
    total = jnp.zeros((planes * size, fold), F32)
    for f in range(FOLDS):
        pick = one_hot(jnp.where(part == f, wanted, -1), CORES * rows)
        total = total + dot(pick, stacked[:, f * fold : (f + 1) * fold])
    total = total.astype(BF16)
    for d in range(planes):
        outs[d][...] = total[d * size : (d + 1) * size]


def merge_near_kernel(*refs):
    chunks, out_ref = refs[:-1], refs[-1]
    size, fold = chunks[0].shape
    stacked = jnp.concatenate([chunk[...] for chunk in chunks], axis=0)
    rows = len(chunks) * CORES * MOST
    out = iota((SIDES * rows, 1), 0)
    side, at = out // rows, lax.rem(out, rows)
    d, replica, slot = at // (CORES * MOST), lax.rem(at // MOST, CORES), lax.rem(at, MOST)
    for f in range(FOLDS):
        wanted = d * size + ((f * CORES + replica) * SIDES + side) * MOST + slot
        picked = dot(one_hot(wanted, len(chunks) * size), stacked)
        out_ref[:, f * fold : (f + 1) * fold] = picked.astype(BF16)


def merge_far_kernel(*refs):
    chunks, out_ref = refs[:-1], refs[-1]
    me = lax.axis_index("dp")
    planes, (size, fold) = len(chunks) // CORES, chunks[0].shape
    stacked = jnp.concatenate([chunk[...] for chunk in chunks], axis=0)
    rows = planes * CORES * MOST
    out = iota((SIDES * rows, 1), 0)
    side, at = out // rows, lax.rem(out, rows)
    d, replica, slot = at // (CORES * MOST), lax.rem(at // MOST, CORES), lax.rem(at, MOST)
    q = replica ^ me
    first = (q * planes + d) * size + (q * FOLDS * SIDES + side) * MOST + slot
    for f in range(FOLDS):
        picked = dot(one_hot(first + f * SIDES * MOST, len(chunks) * size), stacked)
        out_ref[:, f * fold : (f + 1) * fold] = picked.astype(BF16)


def partial_kernel(*refs):
    blocks, (gate_ref, up_ref, down_ref, out_ref), sided = refs[:SPLIT], refs[SPLIT:-2], refs[-2:]
    each, width = blocks[0].shape[0], gate_ref.shape[1]
    rows = each // SIDES
    stacked = jnp.concatenate([block[...] for block in blocks], axis=0)
    at = iota((SPLIT * rows, 1), 0)
    block = near(at // rows, lax.axis_index("dp"))
    for side in range(SIDES):
        wanted = block * each + side * rows + lax.rem(at, rows)
        sided[side][...] = dot(one_hot(wanted, SPLIT * each), stacked).astype(BF16)
    out_ref[:, :width] = dot(sided[0][...], gate_ref[...])
    out_ref[:, width : 2 * width] = dot(sided[0][...], up_ref[...])
    out_ref[:, 2 * width :] = dot(sided[1][...], down_ref[...])


def sides_kernel(*refs):
    sums, (gate_ref, up_ref), outs = refs[: 2 * GROUPS], refs[2 * GROUPS : 2 * GROUPS + 2], refs[2 * GROUPS + 2 :]
    parts, sides_ref = outs[:-1], outs[-1]
    width = gate_ref.shape[1]
    rows = parts[0].shape[0] // FOLDS * GROUPS
    total = [sums[i][...] + sums[GROUPS + i][...] for i in range(GROUPS)]
    total = jnp.concatenate(total, axis=0)
    pre_gate, pre_up = total[:, :width], total[:, width : 2 * width]
    hidden_grad = total[:, 2 * width :]
    sigma = jax.nn.sigmoid(pre_gate)
    activated = pre_gate * sigma
    slope = sigma * (1.0 + pre_gate * (1.0 - sigma))
    gate_side = (hidden_grad * pre_up * slope).astype(BF16)
    up_side = (hidden_grad * activated).astype(BF16)
    sides_ref[:, :width] = gate_side
    sides_ref[:, width : 2 * width] = up_side
    sides_ref[:, 2 * width :] = (activated * pre_up).astype(BF16)
    across = ((1,), (1,))
    at = iota((SPLIT * rows, 1), 0)
    k = near(at // rows, lax.axis_index("dp"))
    group, row = lax.rem(at, rows) // (rows // GROUPS), lax.rem(at, rows // GROUPS)
    order = one_hot(((GROUPS - 1 - group) * SPLIT + k) * (rows // GROUPS) + row, SPLIT * rows)
    gate_side, up_side = dot(order, gate_side).astype(BF16), dot(order, up_side).astype(BF16)
    part = dot(gate_side, gate_ref[...], across) + dot(up_side, up_ref[...], across)
    each, fold = rows // GROUPS, parts[0].shape[1]
    for k in range(SPLIT):
        for group in range(GROUPS):
            start = (k * GROUPS + group) * each
            folds = [part[start : start + each, f * fold : (f + 1) * fold] for f in range(FOLDS)]
            parts[group * SPLIT + k][...] = jnp.concatenate(folds, axis=0).astype(BF16)


def grads_kernel(*refs):
    xs, ss = refs[:GROUPS], refs[GROUPS : 2 * GROUPS]
    sides_ref, outs, token_ref = refs[2 * GROUPS], refs[2 * GROUPS + 1 : -5], refs[-5]
    held, sems = refs[-4:-1], refs[-1]
    half, width = held[0].shape
    block = half // CHUNKS
    first = ((0,), (0,))
    copies = []
    for c in range(CHUNKS):
        part = slice(c * block, (c + 1) * block)
        x = jnp.concatenate([ref[:, part] for ref in xs], axis=0)
        s = jnp.concatenate([ref[:, part] for ref in ss], axis=0)
        for i, rows in enumerate((x, x, s)):
            held[i][part, :] = dot(rows, sides_ref[:, i * width : (i + 1) * width], first).astype(BF16)
            copy = pltpu.make_async_copy(
                held[i].at[pl.ds(c * block, block)], outs[i].at[pl.ds(c * block, block)], sems.at[i, c]
            )
            copy.start()
            copies.append(copy)
    for copy in copies:
        copy.wait()
    token_ref[...] = jnp.zeros(token_ref.shape, F32)


def sum_kernel(count, *refs):
    parts, outs = refs[:SPLIT], refs[SPLIT:]
    total = parts[0][...].astype(F32)
    for part in parts[1:]:
        total = total + part[...].astype(F32)
    total = total.astype(BF16)
    rows, fold = total.shape
    blocks = fold // 128
    each = CORES * MOST
    size = FOLDS * blocks * each
    row = iota((count * size, 1), 0)
    d, part, at = row // size, lax.rem(row // (blocks * each), FOLDS), lax.rem(row, each)
    block = lax.rem(row // each, blocks)
    wanted = (part * count + d) * each + at
    moved = jnp.zeros((count * size, 128), F32)
    for c in range(blocks):
        pick = one_hot(jnp.where(block == c, wanted, -1), rows)
        moved = moved + dot(pick, total[:, c * 128 : (c + 1) * 128])
    for d in range(count):
        outs[d][...] = moved[d * size : (d + 1) * size].astype(BF16)


def split_kernel(count, *refs):
    chunks, outs = refs[:count], refs[-CORES:]
    me = lax.axis_index("dp")
    size = chunks[0].shape[0]
    stacked = jnp.concatenate([chunk[...].astype(F32) for chunk in chunks], axis=0).astype(BF16)
    rows = count * 8
    out = iota((CORES * rows, 1), 0)
    q, d, slot = out // rows, lax.rem(out, rows) // 8, lax.rem(out, 8)
    first = jnp.where(slot < MOST, d * size + (q ^ me) * MOST + slot, -size)
    for c in range(outs[0].shape[1] // 128):
        picked = dot(one_hot(first + c * CORES * MOST, count * size), stacked).astype(BF16)
        for core in range(CORES):
            outs[core][:, c * 128 : (c + 1) * 128] = picked[core * rows : (core + 1) * rows]


def place_kernel(hot_ref, *refs):
    sources, out_ref, held, sems = refs[:-3], refs[-3], refs[-2], refs[-1]
    me = lax.axis_index("dp")
    half = held.shape[2]
    hot = hot_ref[...].astype(BF16)
    copies = []
    for q in range(CORES):
        rows = jnp.concatenate([ref[...] for ref in sources[q * GROUPS : (q + 1) * GROUPS]], axis=0)
        held[q] = dot(hot, rows, ((0,), (0,))).astype(BF16)
        columns = pl.ds(pl.multiple_of((me ^ q) * half, 128), half)
        copies.append(pltpu.make_async_copy(held.at[q], out_ref.at[:, columns], sems.at[q]))
        copies[q].start()
    for copy in copies:
        copy.wait()


def like(shape, dtype):
    return jax.ShapeDtypeStruct(shape, dtype)


def body(
    layer_input, out_grad, routes, gate_values, keep_mask, gate_weight, up_weight, down_transposed
):
    devices = lax.axis_size("expert")
    live = devices // SPLIT
    tokens, model = layer_input.shape
    half, width = gate_weight.shape
    fold = half // FOLDS
    rows = CORES * live * MOST
    total = SPLIT * rows
    planes = live // GROUPS
    vmem, hbm = pl.BlockSpec(memory_space=pltpu.VMEM), pl.BlockSpec(memory_space=pltpu.HBM)

    def call(kernel, name, out_shape, operands, flops=0, moved=0):
        return pl.pallas_call(
            kernel,
            out_shape=out_shape,
            in_specs=[vmem] * len(operands),
            out_specs=jax.tree.map(lambda _: vmem, out_shape),
            compiler_params=params(),
            cost_estimate=cost(flops, moved) if flops else None,
            name=name,
        )(*operands)

    def swap_cores(array):
        return lax.ppermute(array, "dp", [(r, r ^ 1) for r in range(CORES)])

    def along_z(array, d):
        hop = [(i, (i // SPLIT ^ d) * SPLIT + i % SPLIT) for i in range(devices)]
        return lax.ppermute(array, "expert", hop)

    def in_plane(array, k):
        hop = []
        for i in range(devices):
            for r in range(CORES):
                hop.append((i * CORES + r, (i ^ near(k, r)) * CORES + r))
        return lax.ppermute(array, ("expert", "dp"), hop)

    size = FOLDS * CORES * SIDES * MOST
    near_rows = like((planes * SIDES * MOST, half), BF16)
    mine, other, *far, hot = pl.pallas_call(
        functools.partial(gather_kernel, live),
        out_shape=[near_rows] * CORES
        + [like((size, fold), BF16)] * (live - planes)
        + [like((live * 8, tokens), F32)],
        in_specs=[hbm] * 5,
        out_specs=[vmem] * (CORES + live - planes + 1),
        scratch_shapes=[
            pltpu.VMEM((TOP, tokens), jnp.int32),
            pltpu.VMEM((TOP, tokens), jnp.int32),
            pltpu.VMEM((TOP, tokens), F32),
            pltpu.VMEM((tokens, model), BF16),
            pltpu.VMEM((tokens, model), BF16),
            pltpu.SemaphoreType.DMA((5,)),
        ],
        compiler_params=params(FIRST_MIB),
        name="gather_rows",
    )(routes.T, keep_mask.T, gate_values.T, layer_input, out_grad)
    far = [along_z(chunk, planes + d) for d, chunk in enumerate(far)]
    near_chunks = call(
        functools.partial(chunk_kernel, planes),
        "chunk_rows",
        [like((size, fold), BF16)] * planes,
        [mine, swap_cores(other)],
        1e10,
        2e7,
    )
    near_chunks = [near_chunks[0]] + [along_z(near_chunks[d], d) for d in range(1, planes)]
    mines, others, xs, ss = [], [], [], []
    rows_in_group = total // GROUPS
    for group in reversed(range(GROUPS)):
        here = far + [swap_cores(chunk) for chunk in far] if group else near_chunks
        rows_here = call(
            merge_far_kernel if group else merge_near_kernel,
            "merge_rows",
            like((SIDES * rows // GROUPS, half), BF16),
            here,
            1e8,
            1e6,
        )
        first, second = in_plane(rows_here, 1), in_plane(rows_here, 2)
        across = in_plane(first, 2)
        mine, x, s = call(
            partial_kernel,
            "partial_products",
            [like((rows_in_group, 3 * width), F32)] + [like((rows_in_group, half), BF16)] * SIDES,
            [rows_here, first, second, across, gate_weight, up_weight, down_transposed],
            6 * rows_in_group * half * width,
            6 * half * width,
        )
        mines.append(mine)
        others.append(swap_cores(mine))
        xs.append(x)
        ss.append(s)
    sided = call(
        sides_kernel,
        "sides_and_parts",
        [like((rows // GROUPS * FOLDS, fold), BF16)] * (GROUPS * SPLIT)
        + [like((total, 3 * width), BF16)],
        [*mines, *others, gate_weight, up_weight],
        4 * total * half * width,
        4 * half * width,
    )
    parts, sides = [], sided[-1]
    for group in range(GROUPS):
        mine = sided[group * SPLIT : (group + 1) * SPLIT]
        parts.append([mine[0]] + [in_plane(mine[k], k) for k in reversed(range(1, SPLIT))])
    gate_grad, up_grad, down_grad, token = pl.pallas_call(
        grads_kernel,
        out_shape=[like((half, width), BF16)] * 3 + [like((8, 128), F32)],
        in_specs=[vmem] * (2 * GROUPS + 1),
        out_specs=[hbm] * 3 + [vmem],
        scratch_shapes=[pltpu.VMEM((half, width), BF16)] * 3 + [pltpu.SemaphoreType.DMA((3, CHUNKS))],
        compiler_params=params(),
        cost_estimate=cost(6 * total * half * width, 6 * half * width + 4 * total * half),
        name="weight_grads",
    )(*xs, *ss, sides)
    back, over = [], []
    for group in range(GROUPS):
        ordered = group == TOKEN_GROUP
        chunks = call(
            functools.partial(sum_kernel, planes),
            "sum_parts",
            [like((half // 128 * CORES * MOST, 128), BF16)] * planes,
            parts[group],
        )
        first = group * planes
        chunks = [along_z(chunks[d], first + d) if first + d else chunks[0] for d in range(planes)]
        mine, other = call(
            functools.partial(split_kernel, planes),
            "split_rows",
            [like((planes * 8, half), BF16)] * CORES,
            chunks + [token] * ordered,
            1e10 if group else 1e8,
            1e6,
        )
        back.append(mine)
        over.append(swap_cores(other))
    input_grad = pl.pallas_call(
        place_kernel,
        out_shape=like((tokens, model), BF16),
        in_specs=[vmem] * (1 + CORES * GROUPS),
        out_specs=hbm,
        scratch_shapes=[pltpu.VMEM((CORES, tokens, half), BF16), pltpu.SemaphoreType.DMA((CORES,))],
        compiler_params=params(),
        name="place_rows",
    )(hot, *back, *over)
    return (input_grad, gate_grad, up_grad, down_grad)


def solution(mesh):
    return jax.shard_map(
        body,
        mesh=mesh,
        in_specs=(
            P(("expert", "dp"), None),
            P(("expert", "dp"), None),
            P(("expert", "dp"), None),
            P(("expert", "dp"), None),
            P(("expert", "dp"), None),
            P("dp", "expert"),
            P("dp", "expert"),
            P("dp", "expert"),
        ),
        out_specs=(
            P(("expert", "dp"), None),
            P("dp", "expert"),
            P("dp", "expert"),
            P("dp", "expert"),
        ),
        check_vma=False,
    )
```

```python
import functools

import jax
import jax.numpy as jnp
from jax import lax
from jax.experimental import pallas as pl
from jax.experimental.pallas import tpu as pltpu
from jax.sharding import PartitionSpec as P

SPLIT = 4
MOST = 5
TOP = 8
SIDES = 2
CORES = 2
TOKEN_GROUP = 1
GROUPS = 2
FOLDS = 2
FIRST_MIB = 60
CHUNKS = 7

F32 = jnp.float32
BF16 = jnp.bfloat16


def params(mib=16):
    return pltpu.CompilerParams(vmem_limit_bytes=int(mib * 1024 * 1024))


def cost(flops, moved):
    return pl.CostEstimate(flops=int(flops), bytes_accessed=int(moved), transcendentals=0)


def iota(shape, axis):
    return lax.broadcasted_iota(jnp.int32, shape, axis)


def dot(a, b, dims=((1,), (0,))):
    return lax.dot_general(a, b, (dims, ((), ())), preferred_element_type=F32)


def one_hot(wanted, columns):
    return (iota((wanted.shape[0], columns), 1) == wanted).astype(F32).astype(BF16)


def pick_rows(routes, keep, gates, expert, slot, valid):
    rows, tokens = expert.shape[0], routes.shape[1]
    chosen = jnp.zeros((rows, tokens), F32)
    gate = jnp.zeros((rows, tokens), F32)
    for k in range(routes.shape[0]):
        hit = (routes[k : k + 1, :] == expert) & (keep[k : k + 1, :] == 1)
        chosen = jnp.where(hit, 1.0, chosen)
        gate = jnp.where(hit, gates[k : k + 1, :], gate)
    upto = (iota((tokens, tokens), 0) <= iota((tokens, tokens), 1)).astype(F32).astype(BF16)
    rank = dot(chosen.astype(BF16), upto)
    hot = (chosen > 0.5) & (rank == (slot + 1).astype(F32)) & valid
    return hot, gate


def near(k, core):
    if isinstance(core, int):
        return 3 - k if core and k in (1, 2) else k
    return jnp.where((core == 1) & (k > 0) & (k < 3), 3 - k, k)


def gather_kernel(live, *refs):
    sources, outs, local, sems = refs[:5], refs[5:-6], refs[-6:-1], refs[-1]
    copies = [pltpu.make_async_copy(sources[i], local[i], sems.at[i]) for i in range(5)]
    for copy in copies:
        copy.start()
    routes_ref, keep_ref, gates_ref, x_ref, o_ref = local
    place, me = lax.axis_index("expert") // SPLIT, lax.axis_index("dp")
    half = x_ref.shape[1] // CORES
    for copy in copies[:3]:
        copy.wait()
    routes, keep, gates = routes_ref[...], keep_ref[...], gates_ref[...]

    row = iota((live * 8, 1), 0)
    expert, slot = place ^ (row // 8), lax.rem(row, 8)
    hot, _ = pick_rows(routes, keep, gates, expert, slot, slot < MOST)
    outs[-1][...] = hot.astype(F32)

    row = iota((live * SIDES * MOST, 1), 0)
    expert = place ^ (row // (SIDES * MOST))
    side, slot = lax.rem(row // MOST, SIDES), lax.rem(row, MOST)
    hot, gate = pick_rows(routes, keep, gates, expert, slot, row >= 0)
    hot_x = (hot & (side == 0)).astype(F32).astype(BF16)
    hot_s = hot & (side == 1)
    scale = jnp.sum(jnp.where(hot_s, gate, 0.0), axis=1, keepdims=True)
    hot_s = hot_s.astype(F32).astype(BF16)
    for copy in copies[3:]:
        copy.wait()
    fold = half // FOLDS
    each = SIDES * MOST
    folds = []
    for f in range(CORES * FOLDS):
        start = (me ^ (f // FOLDS)) * half + f % FOLDS * fold
        columns = pl.ds(pl.multiple_of(start, 128), fold)
        folds.append(dot(hot_x, x_ref[:, columns]) + scale * dot(hot_s, o_ref[:, columns]))
    count = live // GROUPS * each
    for q in range(CORES):
        for f in range(FOLDS):
            outs[q][:, f * fold : (f + 1) * fold] = folds[q * FOLDS + f][:count].astype(BF16)
    for d in range(live // GROUPS, live):
        chunk = [rows[d * each : (d + 1) * each] for rows in folds]
        outs[CORES + d - live // GROUPS][...] = jnp.concatenate(chunk, axis=0).astype(BF16)


def chunk_kernel(planes, mine_ref, other_ref, *outs):
    me = lax.axis_index("dp")
    rows, half = mine_ref.shape
    fold = half // FOLDS
    each = SIDES * MOST
    stacked = jnp.concatenate([mine_ref[...], other_ref[...]], axis=0)
    size = FOLDS * CORES * each
    row = iota((planes * size, 1), 0)
    d, part, at = row // size, lax.rem(row // (CORES * each), FOLDS), lax.rem(row, CORES * each)
    wanted = (at // each ^ me) * rows + d * each + lax.rem(at, each)
    total = jnp.zeros((planes * size, fold), F32)
    for f in range(FOLDS):
        pick = one_hot(jnp.where(part == f, wanted, -1), CORES * rows)
        total = total + dot(pick, stacked[:, f * fold : (f + 1) * fold])
    total = total.astype(BF16)
    for d in range(planes):
        outs[d][...] = total[d * size : (d + 1) * size]


def merge_near_kernel(*refs):
    chunks, out_ref = refs[:-1], refs[-1]
    size, fold = chunks[0].shape
    stacked = jnp.concatenate([chunk[...] for chunk in chunks], axis=0)
    rows = len(chunks) * CORES * MOST
    out = iota((SIDES * rows, 1), 0)
    side, at = out // rows, lax.rem(out, rows)
    d, replica, slot = at // (CORES * MOST), lax.rem(at // MOST, CORES), lax.rem(at, MOST)
    for f in range(FOLDS):
        wanted = d * size + ((f * CORES + replica) * SIDES + side) * MOST + slot
        picked = dot(one_hot(wanted, len(chunks) * size), stacked)
        out_ref[:, f * fold : (f + 1) * fold] = picked.astype(BF16)


def merge_far_kernel(*refs):
    chunks, out_ref = refs[:-1], refs[-1]
    me = lax.axis_index("dp")
    planes, (size, fold) = len(chunks) // CORES, chunks[0].shape
    stacked = jnp.concatenate([chunk[...] for chunk in chunks], axis=0)
    rows = planes * CORES * MOST
    out = iota((SIDES * rows, 1), 0)
    side, at = out // rows, lax.rem(out, rows)
    d, replica, slot = at // (CORES * MOST), lax.rem(at // MOST, CORES), lax.rem(at, MOST)
    q = replica ^ me
    first = (q * planes + d) * size + (q * FOLDS * SIDES + side) * MOST + slot
    for f in range(FOLDS):
        picked = dot(one_hot(first + f * SIDES * MOST, len(chunks) * size), stacked)
        out_ref[:, f * fold : (f + 1) * fold] = picked.astype(BF16)


def partial_kernel(*refs):
    blocks, (gate_ref, up_ref, down_ref, out_ref), sided = refs[:SPLIT], refs[SPLIT:-2], refs[-2:]
    each, width = blocks[0].shape[0], gate_ref.shape[1]
    rows = each // SIDES
    stacked = jnp.concatenate([block[...] for block in blocks], axis=0)
    at = iota((SPLIT * rows, 1), 0)
    block = near(at // rows, lax.axis_index("dp"))
    for side in range(SIDES):
        wanted = block * each + side * rows + lax.rem(at, rows)
        sided[side][...] = dot(one_hot(wanted, SPLIT * each), stacked).astype(BF16)
    out_ref[:, :width] = dot(sided[0][...], gate_ref[...])
    out_ref[:, width : 2 * width] = dot(sided[0][...], up_ref[...])
    out_ref[:, 2 * width :] = dot(sided[1][...], down_ref[...])


def sides_kernel(*refs):
    sums, (gate_ref, up_ref), outs = refs[: 2 * GROUPS], refs[2 * GROUPS : 2 * GROUPS + 2], refs[2 * GROUPS + 2 :]
    parts, sides_ref = outs[:-1], outs[-1]
    width = gate_ref.shape[1]
    rows = parts[0].shape[0] // FOLDS * GROUPS
    total = [sums[i][...] + sums[GROUPS + i][...] for i in range(GROUPS)]
    total = jnp.concatenate(total, axis=0)
    pre_gate, pre_up = total[:, :width], total[:, width : 2 * width]
    hidden_grad = total[:, 2 * width :]
    sigma = jax.nn.sigmoid(pre_gate)
    activated = pre_gate * sigma
    slope = sigma * (1.0 + pre_gate * (1.0 - sigma))
    gate_side = (hidden_grad * pre_up * slope).astype(BF16)
    up_side = (hidden_grad * activated).astype(BF16)
    sides_ref[:, :width] = gate_side
    sides_ref[:, width : 2 * width] = up_side
    sides_ref[:, 2 * width :] = (activated * pre_up).astype(BF16)
    across = ((1,), (1,))
    at = iota((SPLIT * rows, 1), 0)
    k = near(at // rows, lax.axis_index("dp"))
    group, row = lax.rem(at, rows) // (rows // GROUPS), lax.rem(at, rows // GROUPS)
    order = one_hot(((GROUPS - 1 - group) * SPLIT + k) * (rows // GROUPS) + row, SPLIT * rows)
    gate_side, up_side = dot(order, gate_side).astype(BF16), dot(order, up_side).astype(BF16)
    part = dot(gate_side, gate_ref[...], across) + dot(up_side, up_ref[...], across)
    each, fold = rows // GROUPS, parts[0].shape[1]
    for k in range(SPLIT):
        for group in range(GROUPS):
            start = (k * GROUPS + group) * each
            folds = [part[start : start + each, f * fold : (f + 1) * fold] for f in range(FOLDS)]
            parts[group * SPLIT + k][...] = jnp.concatenate(folds, axis=0).astype(BF16)


def grads_kernel(*refs):
    xs, ss = refs[:GROUPS], refs[GROUPS : 2 * GROUPS]
    sides_ref, outs, token_ref = refs[2 * GROUPS], refs[2 * GROUPS + 1 : -5], refs[-5]
    held, sems = refs[-4:-1], refs[-1]
    half, width = held[0].shape
    block = half // CHUNKS
    first = ((0,), (0,))
    copies = []
    for c in range(CHUNKS):
        part = slice(c * block, (c + 1) * block)
        x = jnp.concatenate([ref[:, part] for ref in xs], axis=0)
        s = jnp.concatenate([ref[:, part] for ref in ss], axis=0)
        for i, rows in enumerate((x, x, s)):
            held[i][part, :] = dot(rows, sides_ref[:, i * width : (i + 1) * width], first).astype(BF16)
            copy = pltpu.make_async_copy(
                held[i].at[pl.ds(c * block, block)], outs[i].at[pl.ds(c * block, block)], sems.at[i, c]
            )
            copy.start()
            copies.append(copy)
    for copy in copies:
        copy.wait()
    token_ref[...] = jnp.zeros(token_ref.shape, F32)


def sum_kernel(count, *refs):
    parts, outs = refs[:SPLIT], refs[SPLIT:]
    total = parts[0][...].astype(F32)
    for part in parts[1:]:
        total = total + part[...].astype(F32)
    total = total.astype(BF16)
    rows, fold = total.shape
    blocks = fold // 128
    each = CORES * MOST
    size = FOLDS * blocks * each
    row = iota((count * size, 1), 0)
    d, part, at = row // size, lax.rem(row // (blocks * each), FOLDS), lax.rem(row, each)
    block = lax.rem(row // each, blocks)
    wanted = (part * count + d) * each + at
    moved = jnp.zeros((count * size, 128), F32)
    for c in range(blocks):
        pick = one_hot(jnp.where(block == c, wanted, -1), rows)
        moved = moved + dot(pick, total[:, c * 128 : (c + 1) * 128])
    for d in range(count):
        outs[d][...] = moved[d * size : (d + 1) * size].astype(BF16)


def split_kernel(count, *refs):
    chunks, outs = refs[:count], refs[-CORES:]
    me = lax.axis_index("dp")
    size = chunks[0].shape[0]
    stacked = jnp.concatenate([chunk[...].astype(F32) for chunk in chunks], axis=0).astype(BF16)
    rows = count * 8
    out = iota((CORES * rows, 1), 0)
    q, d, slot = out // rows, lax.rem(out, rows) // 8, lax.rem(out, 8)
    first = jnp.where(slot < MOST, d * size + (q ^ me) * MOST + slot, -size)
    for c in range(outs[0].shape[1] // 128):
        picked = dot(one_hot(first + c * CORES * MOST, count * size), stacked).astype(BF16)
        for core in range(CORES):
            outs[core][:, c * 128 : (c + 1) * 128] = picked[core * rows : (core + 1) * rows]


def place_kernel(hot_ref, *refs):
    sources, out_ref, held, sems = refs[:-3], refs[-3], refs[-2], refs[-1]
    me = lax.axis_index("dp")
    half = held.shape[2]
    hot = hot_ref[...].astype(BF16)
    copies = []
    for q in range(CORES):
        rows = jnp.concatenate([ref[...] for ref in sources[q * GROUPS : (q + 1) * GROUPS]], axis=0)
        held[q] = dot(hot, rows, ((0,), (0,))).astype(BF16)
        columns = pl.ds(pl.multiple_of((me ^ q) * half, 128), half)
        copies.append(pltpu.make_async_copy(held.at[q], out_ref.at[:, columns], sems.at[q]))
        copies[q].start()
    for copy in copies:
        copy.wait()


def like(shape, dtype):
    return jax.ShapeDtypeStruct(shape, dtype)


def body(
    layer_input, out_grad, routes, gate_values, keep_mask, gate_weight, up_weight, down_transposed
):
    devices = lax.axis_size("expert")
    live = devices // SPLIT
    tokens, model = layer_input.shape
    half, width = gate_weight.shape
    fold = half // FOLDS
    rows = CORES * live * MOST
    total = SPLIT * rows
    planes = live // GROUPS
    vmem, hbm = pl.BlockSpec(memory_space=pltpu.VMEM), pl.BlockSpec(memory_space=pltpu.HBM)

    def call(kernel, name, out_shape, operands, flops=0, moved=0):
        return pl.pallas_call(
            kernel,
            out_shape=out_shape,
            in_specs=[vmem] * len(operands),
            out_specs=jax.tree.map(lambda _: vmem, out_shape),
            compiler_params=params(),
            cost_estimate=cost(flops, moved) if flops else None,
            name=name,
        )(*operands)

    def swap_cores(array):
        return lax.ppermute(array, "dp", [(r, r ^ 1) for r in range(CORES)])

    def along_z(array, d):
        hop = [(i, (i // SPLIT ^ d) * SPLIT + i % SPLIT) for i in range(devices)]
        return lax.ppermute(array, "expert", hop)

    def in_plane(array, k):
        hop = []
        for i in range(devices):
            for r in range(CORES):
                hop.append((i * CORES + r, (i ^ near(k, r)) * CORES + r))
        return lax.ppermute(array, ("expert", "dp"), hop)

    size = FOLDS * CORES * SIDES * MOST
    near_rows = like((planes * SIDES * MOST, half), BF16)
    mine, other, *far, hot = pl.pallas_call(
        functools.partial(gather_kernel, live),
        out_shape=[near_rows] * CORES
        + [like((size, fold), BF16)] * (live - planes)
        + [like((live * 8, tokens), F32)],
        in_specs=[hbm] * 5,
        out_specs=[vmem] * (CORES + live - planes + 1),
        scratch_shapes=[
            pltpu.VMEM((TOP, tokens), jnp.int32),
            pltpu.VMEM((TOP, tokens), jnp.int32),
            pltpu.VMEM((TOP, tokens), F32),
            pltpu.VMEM((tokens, model), BF16),
            pltpu.VMEM((tokens, model), BF16),
            pltpu.SemaphoreType.DMA((5,)),
        ],
        compiler_params=params(FIRST_MIB),
        name="gather_rows",
    )(routes.T, keep_mask.T, gate_values.T, layer_input, out_grad)
    far = [along_z(chunk, planes + d) for d, chunk in enumerate(far)]
    near_chunks = call(
        functools.partial(chunk_kernel, planes),
        "chunk_rows",
        [like((size, fold), BF16)] * planes,
        [mine, swap_cores(other)],
        1e10,
        2e7,
    )
    near_chunks = [near_chunks[0]] + [along_z(near_chunks[d], d) for d in range(1, planes)]
    mines, others, xs, ss = [], [], [], []
    rows_in_group = total // GROUPS
    for group in reversed(range(GROUPS)):
        here = far + [swap_cores(chunk) for chunk in far] if group else near_chunks
        rows_here = call(
            merge_far_kernel if group else merge_near_kernel,
            "merge_rows",
            like((SIDES * rows // GROUPS, half), BF16),
            here,
            1e8,
            1e6,
        )
        first, second = in_plane(rows_here, 1), in_plane(rows_here, 2)
        across = in_plane(first, 2)
        mine, x, s = call(
            partial_kernel,
            "partial_products",
            [like((rows_in_group, 3 * width), F32)] + [like((rows_in_group, half), BF16)] * SIDES,
            [rows_here, first, second, across, gate_weight, up_weight, down_transposed],
            6 * rows_in_group * half * width,
            6 * half * width,
        )
        mines.append(mine)
        others.append(swap_cores(mine))
        xs.append(x)
        ss.append(s)
    sided = call(
        sides_kernel,
        "sides_and_parts",
        [like((rows // GROUPS * FOLDS, fold), BF16)] * (GROUPS * SPLIT)
        + [like((total, 3 * width), BF16)],
        [*mines, *others, gate_weight, up_weight],
        4 * total * half * width,
        4 * half * width,
    )
    parts, sides = [], sided[-1]
    for group in range(GROUPS):
        mine = sided[group * SPLIT : (group + 1) * SPLIT]
        parts.append([mine[0]] + [in_plane(mine[k], k) for k in range(1, SPLIT)])
    gate_grad, up_grad, down_grad, token = pl.pallas_call(
        grads_kernel,
        out_shape=[like((half, width), BF16)] * 3 + [like((8, 128), F32)],
        in_specs=[vmem] * (2 * GROUPS + 1),
        out_specs=[hbm] * 3 + [vmem],
        scratch_shapes=[pltpu.VMEM((half, width), BF16)] * 3 + [pltpu.SemaphoreType.DMA((3, CHUNKS))],
        compiler_params=params(),
        cost_estimate=cost(6 * total * half * width, 6 * half * width + 4 * total * half),
        name="weight_grads",
    )(*xs, *ss, sides)
    back, over = [], []
    for group in range(GROUPS):
        ordered = group == TOKEN_GROUP
        chunks = call(
            functools.partial(sum_kernel, planes),
            "sum_parts",
            [like((half // 128 * CORES * MOST, 128), BF16)] * planes,
            parts[group],
        )
        first = group * planes
        chunks = [along_z(chunks[d], first + d) if first + d else chunks[0] for d in range(planes)]
        mine, other = call(
            functools.partial(split_kernel, planes),
            "split_rows",
            [like((planes * 8, half), BF16)] * CORES,
            chunks + [token] * ordered,
            1e10 if group else 1e8,
            1e6,
        )
        back.append(mine)
        over.append(swap_cores(other))
    input_grad = pl.pallas_call(
        place_kernel,
        out_shape=like((tokens, model), BF16),
        in_specs=[vmem] * (1 + CORES * GROUPS),
        out_specs=hbm,
        scratch_shapes=[pltpu.VMEM((CORES, tokens, half), BF16), pltpu.SemaphoreType.DMA((CORES,))],
        compiler_params=params(),
        name="place_rows",
    )(hot, *back, *over)
    return (input_grad, gate_grad, up_grad, down_grad)


def solution(mesh):
    return jax.shard_map(
        body,
        mesh=mesh,
        in_specs=(
            P(("expert", "dp"), None),
            P(("expert", "dp"), None),
            P(("expert", "dp"), None),
            P(("expert", "dp"), None),
            P(("expert", "dp"), None),
            P("dp", "expert"),
            P("dp", "expert"),
            P("dp", "expert"),
        ),
        out_specs=(
            P(("expert", "dp"), None),
            P("dp", "expert"),
            P("dp", "expert"),
            P("dp", "expert"),
        ),
        check_vma=False,
    )
```
